32 devices in a mesh: parts: 2 (over y), seq: 2 (over x), wide: 4 (over z), pair: 2 (over core).
Axes of the slice: x: 2, y: 2, z: 4, core: 2. Of those that a mesh axis runs over, the one named last changes fastest.
Arguments:
- tokens: bfloat16 [128, 8192], P(('parts', 'wide'), ('seq', 'pair')), parts along dimension 0, may hold values from -6 to 6
- gate_weight: bfloat16 [8192, 26624], P(('seq', 'pair'), 'wide'), may hold values from -0.0625 to 0.0625
- up_weight: bfloat16 [8192, 26624], P(('seq', 'pair'), 'wide'), may hold values from -0.0625 to 0.0625
- down_weight: bfloat16 [26624, 8192], P('wide', ('seq', 'pair')), may hold values from -0.0390625 to 0.0390625
Outputs:
- mixed: bfloat16 [128, 8192], P(('parts', 'wide'), ('seq', 'pair')), parts along dimension 0
The draws below stay inside these ranges and needn't reach their ends.
There are 2 independent parts, one for each index of `parts`. The reference program is written for one: setup_inputs(seed, part) draws one part's arguments, and reference() takes and returns one part's arrays. A program takes and returns all parts, laid end to end along the dimension named above; an argument that names none is the same for every part. Nothing has to cross between parts.
All inputs are finite; a program needn't handle non-finite values.
Results may differ from the reference program's by a relative error of at most 0.005.
Values may be sent and summed in bfloat16 or wider, within the bound.
No kernel may reach another device: no remote copies, remote signals or barrier semaphores. Data moves between devices by JAX's collectives and lax.ppermute only.
A program may use at most 192 MiB of HBM per device.

```python
import jax
import jax.numpy as jnp

D = 8192
FF = 26624
TOKENS = 64


def steps_of(stream_key, dims, shards, least, largest):
    def one(axis_at, parts):
        heights = jax.random.uniform(jax.random.fold_in(jax.random.fold_in(stream_key, 6), axis_at), (parts,), jnp.float32, least / len(shards), largest / len(shards))
        return jnp.repeat(jnp.exp(heights), dims[axis_at] // parts).reshape((-1,) + (1,) * (len(dims) - axis_at - 1))

    factor_of = one(*shards[0])
    for cut in shards[1:]:
        factor_of = factor_of * one(*cut)
    return factor_of


def bell_draw(stream_key, shape, scale, bound, cuts=(), kind=jnp.bfloat16):
    factor_of = steps_of(stream_key, shape, cuts, -0.22, 0.18) if cuts else 1.0
    drawn = jax.random.normal(stream_key, shape, jnp.float32) * scale * factor_of
    return jnp.minimum(jnp.maximum(drawn, -bound), bound).astype(kind)


def setup_inputs(seed: int = 0, part: int = 0) -> dict:
    splits = jax.random.split(jax.random.key(seed), 5)
    part_keys = jax.random.split(jax.random.fold_in(splits[4], part), 5)
    tokens = bell_draw(part_keys[0], (TOKENS, D), 1.0, 6.0, ((0, 4), (1, 4)))
    gate_weight = bell_draw(splits[1], (D, FF), D ** -0.5, 0.0625, ((0, 4), (1, 4)))
    up_weight = bell_draw(splits[2], (D, FF), D ** -0.5, 0.0625, ((0, 4), (1, 4)))
    down_weight = bell_draw(splits[3], (FF, D), FF ** -0.5, 0.0390625, ((0, 4), (1, 4)))
    return dict(tokens=tokens, gate_weight=gate_weight, up_weight=up_weight, down_weight=down_weight)


def reference(tokens, gate_weight, up_weight, down_weight):
    gate = jnp.dot(tokens, gate_weight, preferred_element_type=jnp.float32)
    up = jnp.dot(tokens, up_weight, preferred_element_type=jnp.float32)
    hidden = (jax.nn.silu(gate) * up).astype(jnp.bfloat16)
    mixed = jnp.dot(hidden, down_weight, preferred_element_type=jnp.float32)
    return mixed.astype(jnp.bfloat16)
```

```python
import functools

import jax
import jax.numpy as jnp
from jax import lax
from jax.experimental import pallas as pl
from jax.experimental.pallas import tpu as pltpu
from jax.sharding import PartitionSpec as P

BF16, F32 = jnp.bfloat16, jnp.float32
TILE = 512
SHARES = (4, 4, 3, 2)
PAIR_TYPE = F32


def on_chip():
    return pl.BlockSpec(memory_space=pltpu.VMEM)


def in_place():
    return pl.BlockSpec(memory_space=pl.ANY)


def cuts(columns):
    if columns % (TILE * sum(SHARES)):
        return [(0, columns)]
    unit = columns // sum(SHARES)
    chunks, start = [], 0
    for share in SHARES:
        chunks.append((start, share * unit))
        start += share * unit
    return chunks


def tile_of(width):
    return TILE if width % TILE == 0 else width


def copies(fetch, sources, targets, sems):
    made = []
    for at, ((axis, start, size), source, target) in enumerate(zip(fetch, sources, targets)):
        view = source.at[:, pl.ds(start, size)] if axis else source.at[pl.ds(start, size), :]
        made.append(pltpu.make_async_copy(view, target, sems.at[at]))
    return made


def call(body, operands, in_specs, outs, fetch, scratch, flops, traffic):
    fetched = []
    for array, axis, start, size in fetch:
        shape = (array.shape[0], size) if axis else (size, array.shape[1])
        fetched.append(pltpu.VMEM(shape, array.dtype))
    out = pl.pallas_call(
        body,
        out_shape=tuple(outs) + tuple(fetched),
        in_specs=list(in_specs) + [in_place()] * len(fetch),
        out_specs=tuple([on_chip()] * (len(outs) + len(fetch))),
        scratch_shapes=list(scratch) + [pltpu.SemaphoreType.DMA((max(len(fetch), 1),))],
        compiler_params=pltpu.CompilerParams(vmem_limit_bytes=12 * 2**20),
        cost_estimate=pl.CostEstimate(flops=flops, bytes_accessed=traffic, transcendentals=0),
    )(*operands, *[f[0] for f in fetch])
    return out[: len(outs)], out[len(outs) :]


def split_refs(refs, *counts):
    groups, at = [], 0
    for count in counts:
        groups.append(refs[at : at + count])
        at += count
    return groups


def load_kernel(fetch, *refs):
    sources, targets, (sems,) = split_refs(refs, len(fetch), len(fetch), 1)
    made = copies(fetch, sources, targets, sems)
    for copy in made:
        copy.start()
    for copy in made:
        copy.wait()


def gate_up_kernel(n_pair, fetch, *refs):
    (x, wg, wu), sources, (keep,), sends, targets, (res, sems) = split_refs(
        refs, 3, len(fetch), 1, n_pair - 1, len(fetch), 2
    )
    made = copies(fetch, sources, targets, sems)
    for copy in made:
        copy.start()
    me = lax.axis_index("pair")
    rows = keep.shape[1]
    width = wg.shape[1]
    tile = tile_of(width)

    @pl.loop(0, width // tile)
    def _(step):
        at = pl.ds(pl.multiple_of(step * tile, tile), tile)
        for which, weight in enumerate((wg, wu)):
            res[...] = jnp.dot(x[...], weight[:, at], preferred_element_type=F32)
            for k in range(n_pair):
                first = pl.multiple_of(lax.rem(me + k, n_pair) * rows, 16)
                target = sends[k - 1] if k else keep
                target[which, :, at] = res[pl.ds(first, rows), :].astype(target.dtype)

    for copy in made:
        copy.wait()


def pair_sum_kernel(n_pair, n_seq, *refs):
    (keep,), got, (own,), sends, _ = split_refs(refs, 1, n_pair - 1, 1, n_seq - 1, 1)
    me = lax.axis_index("seq")
    rows = own.shape[1]
    for k in range(n_seq):
        block = pl.ds(pl.multiple_of(lax.rem(me + k, n_seq) * rows, 16), rows)
        total = keep[:, block, :]
        for part in got:
            total += part[:, block, :].astype(F32)
        target = sends[k - 1] if k else own
        target[...] = total.astype(target.dtype)


def down_kernel(n_pair, n_seq, n_wide, first, last, fetch, *refs):
    pieces = n_pair * n_seq
    parts, (wd,), before, sources, outs, targets, (hidden, sems) = split_refs(
        refs, pieces, 1, 0 if first else 1, len(fetch), n_wide if last else 1, len(fetch), 2
    )
    made = copies(fetch, sources, targets, sems)
    for copy in made:
        copy.start()
    c, s = lax.axis_index("pair"), lax.axis_index("seq")
    rows = parts[0].shape[0]
    for dc in range(n_pair):
        for ds in range(n_seq):
            block = lax.rem(c + n_pair - dc, n_pair) * n_seq + lax.rem(s + n_seq - ds, n_seq)
            hidden[pl.ds(pl.multiple_of(block * rows, 16), rows), :] = parts[dc * n_seq + ds][...]
    width = wd.shape[1]
    tile = tile_of(width)

    @pl.loop(0, width // tile)
    def _(step):
        at = pl.ds(pl.multiple_of(step * tile, tile), tile)
        total = jnp.dot(hidden[...], wd[:, at], preferred_element_type=F32)
        if before:
            total += before[0][:, at]
        if last:
            share = total.shape[0] // n_wide
            for k in range(n_wide):
                place = (n_wide - k) % n_wide * share
                outs[k][:, at] = total[place : place + share].astype(outs[k].dtype)
        else:
            outs[0][:, at] = total

    for copy in made:
        copy.wait()


def shards(sizes, tokens, gate_weight, up_weight, down_weight):
    n_seq, n_wide, n_pair = sizes["seq"], sizes["wide"], sizes["pair"]

    def send(value, axis, k):
        n = sizes[axis]
        return lax.ppermute(value, axis, [(i, (i + k) % n) for i in range(n)])

    share, depth = tokens.shape
    rows = share * n_wide
    features = down_weight.shape[1]
    half, quarter = rows // n_pair, rows // n_pair // n_seq
    chunks = cuts(gate_weight.shape[1])
    size = tokens.dtype.itemsize

    def load_gate_up(j):
        if j == len(chunks):
            return [(down_weight, 0, *chunks[0])]
        return [(w, 1, *chunks[j]) for w in (gate_weight, up_weight)]

    def bytes_of(fetch):
        return sum(size * f[3] * f[0].shape[1 - f[1]] for f in fetch)

    x = jnp.concatenate([tokens] + [send(tokens, "wide", k) for k in range(1, n_wide)])

    fetch = load_gate_up(0)
    _, weights = call(
        functools.partial(load_kernel, [f[1:] for f in fetch]),
        [], [], [], fetch, [], 0, 2 * bytes_of(fetch),
    )

    hidden_parts = []
    for j, (start, width) in enumerate(chunks):
        fetch = load_gate_up(j + 1)
        outs, fetched = call(
            functools.partial(gate_up_kernel, n_pair, [f[1:] for f in fetch]),
            [x, *weights],
            [on_chip()] * 3,
            [pltpu.VMEM((2, half, width), F32)]
            + [pltpu.VMEM((2, half, width), PAIR_TYPE)] * (n_pair - 1),
            fetch,
            [pltpu.VMEM((rows, tile_of(width)), F32)],
            4 * rows * depth * width,
            2 * bytes_of(fetch),
        )
        weights = fetched
        got = [send(outs[k], "pair", k) for k in range(1, n_pair)]
        own, *sums = call(
            functools.partial(pair_sum_kernel, n_pair, n_seq),
            [outs[0], *got],
            [on_chip()] * n_pair,
            [pltpu.VMEM((2, quarter, width), F32)]
            + [pltpu.VMEM((2, quarter, width), BF16)] * (n_seq - 1),
            [], [], 0, 8 * half * width,
        )[0]
        total = own
        for k in range(1, n_seq):
            total = total + send(sums[k - 1], "seq", k).astype(F32)
        hidden = (jax.nn.silu(total[0]) * total[1]).astype(BF16)
        near = [hidden] + [send(hidden, "seq", k) for k in range(1, n_seq)]
        parts = list(near)
        for k in range(1, n_pair):
            parts += [send(part, "pair", k) for part in near]
        hidden_parts.append(parts)

    total = None
    for j, (start, width) in enumerate(chunks):
        first, last = j == 0, j == len(chunks) - 1
        fetch = [] if last else [(down_weight, 0, *chunks[j + 1])]
        if last:
            outs = [pltpu.VMEM((share, features), F32)]
            outs += [pltpu.VMEM((share, features), BF16)] * (n_wide - 1)
        else:
            outs = [pltpu.VMEM((rows, features), F32)]
        total, weights = call(
            functools.partial(down_kernel, n_pair, n_seq, n_wide, first, last, [f[1:] for f in fetch]),
            [*hidden_parts[j], *weights, *([] if first else total)],
            [on_chip()] * (n_pair * n_seq + 1 + (not first)),
            outs,
            fetch,
            [pltpu.VMEM((rows, width), BF16)],
            2 * rows * width * features,
            2 * bytes_of(fetch),
        )

    result = total[0]
    for k in range(1, n_wide):
        result = result + send(total[k], "wide", k).astype(F32)
    return result.astype(BF16)


def solution(mesh):
    return jax.shard_map(
        functools.partial(shards, dict(mesh.shape)),
        mesh=mesh,
        in_specs=(
            P(("parts", "wide"), ("seq", "pair")),
            P(("seq", "pair"), "wide"),
            P(("seq", "pair"), "wide"),
            P("wide", ("seq", "pair")),
        ),
        out_specs=P(("parts", "wide"), ("seq", "pair")),
        check_vma=False,
    )
```

```python
import functools

import jax
import jax.numpy as jnp
from jax import lax
from jax.experimental import pallas as pl
from jax.experimental.pallas import tpu as pltpu
from jax.sharding import PartitionSpec as P

BF16, F32 = jnp.bfloat16, jnp.float32
TILE = 512
SHARES = (6, 4, 3)
PAIR_TYPE = F32


def on_chip():
    return pl.BlockSpec(memory_space=pltpu.VMEM)


def in_place():
    return pl.BlockSpec(memory_space=pl.ANY)


def cuts(columns):
    if columns % (TILE * sum(SHARES)):
        return [(0, columns)]
    unit = columns // sum(SHARES)
    chunks, start = [], 0
    for share in SHARES:
        chunks.append((start, share * unit))
        start += share * unit
    return chunks


def tile_of(width):
    return TILE if width % TILE == 0 else width


def copies(fetch, sources, targets, sems):
    made = []
    for at, ((axis, start, size), source, target) in enumerate(zip(fetch, sources, targets)):
        view = source.at[:, pl.ds(start, size)] if axis else source.at[pl.ds(start, size), :]
        made.append(pltpu.make_async_copy(view, target, sems.at[at]))
    return made


def call(body, operands, outs, fetch, scratch, flops, traffic, after=(), aliases=None):
    fetched = []
    for array, axis, start, size in fetch:
        shape = (array.shape[0], size) if axis else (size, array.shape[1])
        fetched.append(pltpu.VMEM(shape, array.dtype))
    n_in = len(operands)

    def kernel(*refs):
        ins, rest = refs[:n_in], refs[n_in + len(after) :]
        sources, rest = rest[: len(fetch)], rest[len(fetch) :]
        results, rest = rest[: len(outs)], rest[len(outs) :]
        targets, (*room, sems) = rest[: len(fetch)], rest[len(fetch) :]
        made = copies([f[1:] for f in fetch], sources, targets, sems)
        for copy in made:
            copy.start()
        body(ins, results, room)
        for copy in made:
            copy.wait()

    out = pl.pallas_call(
        kernel,
        out_shape=tuple(outs) + tuple(fetched),
        in_specs=[on_chip()] * n_in + [in_place()] * (len(after) + len(fetch)),
        out_specs=tuple([on_chip()] * (len(outs) + len(fetch))),
        scratch_shapes=list(scratch) + [pltpu.SemaphoreType.DMA((max(len(fetch), 1),))],
        input_output_aliases=aliases or {},
        compiler_params=pltpu.CompilerParams(vmem_limit_bytes=4 * 2**20),
        cost_estimate=pl.CostEstimate(flops=flops, bytes_accessed=traffic, transcendentals=0),
    )(*operands, *after, *[pltpu.with_memory_space_constraint(f[0], pltpu.HBM) for f in fetch])
    return out[: len(outs)], out[len(outs) :]


def load_kernel(ins, outs, room):
    pass


def pair_part_kernel(n_pair, ins, outs, room):
    x, weight = ins
    keep, *sends = outs
    (res,) = room
    me = lax.axis_index("pair")
    rows = keep.shape[0]
    width = weight.shape[1]
    tile = tile_of(width)

    @pl.loop(0, width // tile)
    def _(step):
        at = pl.ds(pl.multiple_of(step * tile, tile), tile)
        res[...] = jnp.dot(x[...], weight[:, at], preferred_element_type=F32)
        for k in range(n_pair):
            first = pl.multiple_of(lax.rem(me + k, n_pair) * rows, 16)
            target = sends[k - 1] if k else keep
            target[:, at] = res[pl.ds(first, rows), :].astype(target.dtype)


def pair_sum_kernel(ins, outs, room):
    total = ins[0][...]
    for part in ins[1:]:
        total += part[...].astype(F32)
    for out in outs:
        out[...] = total.astype(out.dtype)


def down_kernel(n_wide, first, last, ins, outs, room):
    parts, (wd, *before) = (ins[:-1], ins[-1:]) if first else (ins[:-2], ins[-2:])
    (hidden,) = room
    n_pair = len(parts)
    c, w = lax.axis_index("pair"), lax.axis_index("wide")
    rows = parts[0].shape[0]
    for k in range(n_pair):
        block = lax.rem(c + n_pair - k, n_pair)
        hidden[pl.ds(pl.multiple_of(block * rows, 16), rows), :] = parts[k][...]
    width = wd.shape[1]
    tile = tile_of(width)

    @pl.loop(0, width // tile)
    def _(step):
        at = pl.ds(pl.multiple_of(step * tile, tile), tile)
        total = jnp.dot(hidden[...], wd[:, at], preferred_element_type=F32)
        if before:
            total += before[0][:, at]
        if last:
            own, others = outs
            share = total.shape[0] // n_wide
            for k in range(n_wide):
                piece = total[k * share : (k + 1) * share]
                if k == 0:
                    own[:, at] = piece
                    piece = jnp.zeros_like(piece)
                place = pl.multiple_of(lax.rem(w + n_wide - k, n_wide) * share, 16)
                others[pl.ds(place, share), at] = piece.astype(others.dtype)
        else:
            outs[0][:, at] = total


def shards(sizes, tokens, gate_weight, up_weight, down_weight):
    n_seq, n_wide, n_pair = sizes["seq"], sizes["wide"], sizes["pair"]

    def send(value, axis, k):
        n = sizes[axis]
        return lax.ppermute(value, axis, [(i, (i + k) % n) for i in range(n)])

    share, depth = tokens.shape
    rows = share * n_wide
    features = down_weight.shape[1]
    half = rows // n_pair
    chunks = cuts(gate_weight.shape[1])
    n = len(chunks)
    size = tokens.dtype.itemsize

    def gate_of(*picks):
        return [(gate_weight, 1, *chunks[j]) for j in picks if j < n]

    def down_of(*picks):
        return [(down_weight, 0, *chunks[j]) for j in picks if j < n]

    def bytes_of(fetch):
        return sum(size * f[3] * f[0].shape[1 - f[1]] for f in fetch)

    x = jnp.concatenate([tokens] + [send(tokens, "wide", k) for k in range(1, n_wide)])

    alive = []

    def project(weight, fetch, after=()):
        width = weight.shape[1]
        outs, fetched = call(
            functools.partial(pair_part_kernel, n_pair),
            [x, weight],
            [pltpu.VMEM((half, width), F32)] + [pltpu.VMEM((half, width), PAIR_TYPE)] * (n_pair - 1),
            fetch,
            [pltpu.VMEM((rows, tile_of(width)), F32)],
            2 * rows * depth * width,
            2 * bytes_of(fetch),
            after,
        )
        got = [send(outs[k], "pair", k) for k in range(1, n_pair)]
        alive.extend(got)
        return (outs[0], *got), fetched

    def pair_sum(parts):
        shape = parts[0].shape
        return call(
            pair_sum_kernel, parts, [pltpu.VMEM(shape, F32), pltpu.VMEM(shape, BF16)],
            [], [], 0, 8 * parts[0].size,
        )[0]

    def seq_parts(sums):
        parts = [send(sums[1], "seq", k) for k in range(1, n_seq)]
        alive.extend(parts)
        return [sums[0], *parts]

    def activate(ups, gates, start, width):
        up = sum(part[:, start : start + width].astype(F32) for part in ups)
        gate = sum(part.astype(F32) for part in gates)
        return (jax.nn.silu(gate) * up).astype(BF16)

    fetch = gate_of(n - 1)
    traffic = up_weight.size * size
    _, (gate_last,) = call(load_kernel, [], [], fetch, [], 0, traffic)
    up = pltpu.with_memory_space_constraint(up_weight, pltpu.VMEM)
    ups, gate = project(up, gate_of(0) if n > 1 else [], [gate_last])
    gate = {0: gate[0] if n > 1 else None, n - 1: gate_last}
    up_sums, gate_sums, down = None, [], {}
    parts = []
    for j in range(n):
        fetch = gate_of(1) if j == 0 else []
        if j == n - 1:
            fetch = fetch + down_of(0, 1)
        after = []
        if j == 1:
            up_sums = pair_sum(ups)
            after = [up_sums[1]]
        elif j > 1:
            gate_sums.append(pair_sum(parts[j - 2]))
            after = [gate_sums[-1][1]]
        outs, fetched = project(gate[j], fetch, after)
        parts.append(outs)
        if j == 0 and n > 1:
            gate[1], *fetched = fetched
        if j == n - 1:
            down.update(zip((0, 1), fetched))
    if up_sums is None:
        up_sums = pair_sum(ups)
    for j in range(len(gate_sums), n):
        gate_sums.append(pair_sum(parts[j]))
    up_parts = seq_parts(up_sums)
    hiddens = [activate(up_parts, seq_parts(gate_sums[j]), *chunks[j]) for j in range(n)]

    total = []
    for j, (start, width) in enumerate(chunks):
        first, last = j == 0, j == n - 1
        parts = [hiddens[j]] + [send(hiddens[j], "pair", k) for k in range(1, n_pair)]
        alive.extend(parts[1:])
        if last:
            outs = [pltpu.VMEM((share, features), F32), pltpu.VMEM((rows, features), BF16)]
        else:
            outs = [pltpu.VMEM((rows, features), F32)]
        fetch = down_of(2) if j == 0 else []
        total, fetched = call(
            functools.partial(down_kernel, n_wide, first, last),
            [*parts, down[j], *total],
            outs,
            fetch,
            [pltpu.VMEM((rows, width), BF16)],
            2 * rows * width * features,
            2 * bytes_of(fetch),
            alive if last else [],
        )
        if fetch:
            down[2] = fetched[0]

    own, others = total
    others = lax.all_to_all(others, "wide", 0, 0, tiled=True)
    result = own
    for k in range(n_wide):
        result = result + others[k * share : (k + 1) * share].astype(F32)
    return result.astype(BF16)


def solution(mesh):
    return jax.shard_map(
        functools.partial(shards, dict(mesh.shape)),
        mesh=mesh,
        in_specs=(
            P(("parts", "wide"), ("seq", "pair")),
            P(("seq", "pair"), "wide"),
            P(("seq", "pair"), "wide"),
            P("wide", ("seq", "pair")),
        ),
        out_specs=P(("parts", "wide"), ("seq", "pair")),
        check_vma=False,
    )
```

```python
import functools

import jax
import jax.numpy as jnp
from jax import lax
from jax.experimental import pallas as pl
from jax.experimental.pallas import tpu as pltpu
from jax.sharding import PartitionSpec as P

BF16, F32 = jnp.bfloat16, jnp.float32
TILE = 512
GATE = (8, 5)
DOWN = (4, 4, 3, 2)
PAIR_TYPE = F32
COST = 1


def on_chip():
    return pl.BlockSpec(memory_space=pltpu.VMEM)


def in_place():
    return pl.BlockSpec(memory_space=pl.ANY)


def cuts(columns, shares):
    if columns % (TILE * sum(shares)):
        return [(0, columns)]
    unit = columns // sum(shares)
    chunks, start = [], 0
    for share in shares:
        chunks.append((start, share * unit))
        start += share * unit
    return chunks


def tile_of(width):
    return TILE if width % TILE == 0 else width


def copies(fetch, sources, targets, sems):
    made = []
    for at, ((axis, start, size), source, target) in enumerate(zip(fetch, sources, targets)):
        view = source.at[:, pl.ds(start, size)] if axis else source.at[pl.ds(start, size), :]
        made.append(pltpu.make_async_copy(view, target, sems.at[at]))
    return made


def call(order, body, operands, outs, fetch, scratch, flops, traffic, after=()):
    fetched = []
    for array, axis, start, size in fetch:
        shape = (array.shape[0], size) if axis else (size, array.shape[1])
        fetched.append(pltpu.VMEM(shape, array.dtype))
    n_in = len(operands)
    after = [*after, *order[-1:]]

    def kernel(*refs):
        ins, rest = refs[:n_in], refs[n_in + len(after) :]
        sources, rest = rest[: len(fetch)], rest[len(fetch) :]
        results, rest = rest[: len(outs)], rest[len(outs) :]
        targets, (*room, sems) = rest[: len(fetch)], rest[len(fetch) :]
        made = copies([f[1:] for f in fetch], sources, targets, sems)
        for copy in made:
            copy.start()
        body(ins, results, room)
        for copy in made:
            copy.wait()

    out = pl.pallas_call(
        kernel,
        out_shape=tuple(outs) + tuple(fetched),
        in_specs=[on_chip()] * n_in + [in_place()] * (len(after) + len(fetch)),
        out_specs=tuple([on_chip()] * (len(outs) + len(fetch))),
        scratch_shapes=list(scratch) + [pltpu.SemaphoreType.DMA((max(len(fetch), 1),))],
        compiler_params=pltpu.CompilerParams(vmem_limit_bytes=4 * 2**20),
        cost_estimate=pl.CostEstimate(flops=int(flops), bytes_accessed=int(traffic), transcendentals=0),
    )(*operands, *after, *[pltpu.with_memory_space_constraint(f[0], pltpu.HBM) for f in fetch])
    order.append(min(out, key=lambda array: array.size))
    return out[: len(outs)], out[len(outs) :]


def load_kernel(ins, outs, room):
    outs[0][...] = ins[0][...]


def pair_part_kernel(n_pair, chunks, ins, outs, room):
    *blocks, weight = ins
    n = len(chunks)
    keep, sends = outs[0], outs[1 : 1 + n * (n_pair - 1)]
    x = blocks[0]
    if len(outs) > 1 + len(sends):
        x = outs[-1]
        share = blocks[0].shape[0]
        for k, block in enumerate(blocks):
            x[k * share : (k + 1) * share, :] = block[...]
    (res,) = room
    me = lax.axis_index("pair")
    rows = keep.shape[0]
    for j, (start, width) in enumerate(chunks):
        tile = tile_of(width)

        @pl.loop(0, width // tile)
        def _(step, j=j, start=start, tile=tile):
            def at(offset):
                return pl.ds(pl.multiple_of(offset + step * tile, tile), tile)

            res[...] = jnp.dot(x[...], weight[:, at(start)], preferred_element_type=F32)
            for k in range(n_pair):
                block = pl.ds(pl.multiple_of(lax.rem(me + k, n_pair) * rows, 16), rows)
                target, offset = (sends[(k - 1) * n + j], 0) if k else (keep, start)
                target[:, at(offset)] = res[block, :].astype(target.dtype)


def pair_sum_kernel(chunks, ins, outs, room):
    keep, got = ins[0], ins[1:]
    n, half = len(chunks), len(outs) // 2
    for j, (start, width) in enumerate(chunks):
        at = slice(start, start + width)
        total = keep[:, at]
        for part in got[j::n]:
            total += part[...].astype(F32)
        for own in (0, half):
            out = outs[own + j] if half == n else outs[own]
            out[:, slice(0, width) if half == n else at] = total.astype(out.dtype)


def activate_kernel(start, ins, outs, room):
    at = slice(start, start + outs[0].shape[1])
    half = len(ins) // 2
    up = sum(part[:, at].astype(F32) for part in ins[:half])
    gate = sum(part[...].astype(F32) for part in ins[half:])
    outs[0][...] = (gate / (1.0 + jnp.exp(-gate)) * up).astype(BF16)


def down_kernel(n_wide, first, last, ins, outs, room):
    parts, (wd, *before) = (ins[:-1], ins[-1:]) if first else (ins[:-2], ins[-2:])
    (hidden,) = room
    n_pair = len(parts)
    c = lax.axis_index("pair")
    rows = parts[0].shape[0]
    for k in range(n_pair):
        block = lax.rem(c + n_pair - k, n_pair)
        hidden[pl.ds(pl.multiple_of(block * rows, 16), rows), :] = parts[k][...]
    width = wd.shape[1]
    tile = tile_of(width)

    @pl.loop(0, width // tile)
    def _(step):
        at = pl.ds(pl.multiple_of(step * tile, tile), tile)
        total = jnp.dot(hidden[...], wd[:, at], preferred_element_type=F32)
        if before:
            total += before[0][:, at]
        if last:
            share = total.shape[0] // n_wide
            for k in range(n_wide):
                place = (n_wide - k) % n_wide * share
                outs[k][:, at] = total[place : place + share].astype(outs[k].dtype)
        else:
            outs[0][:, at] = total


def shards(sizes, tokens, gate_weight, up_weight, down_weight):
    n_seq, n_wide, n_pair = sizes["seq"], sizes["wide"], sizes["pair"]

    def send(value, axis, k):
        n = sizes[axis]
        return lax.ppermute(value, axis, [(i, (i + k) % n) for i in range(n)])

    share, depth = tokens.shape
    rows = share * n_wide
    features = down_weight.shape[1]
    half = rows // n_pair
    loads = cuts(gate_weight.shape[1], GATE)
    chunks = cuts(down_weight.shape[0], DOWN)
    n = len(chunks)
    size = tokens.dtype.itemsize

    def gate_of(*picks):
        return [(gate_weight, 1, *loads[j]) for j in picks if j < len(loads)]

    def bytes_of(fetch):
        return sum(size * f[3] * f[0].shape[1 - f[1]] for f in fetch)

    def down_of(*picks):
        return [(down_weight, 0, *chunks[j]) for j in picks if j < n]

    order = []

    def project(blocks, weight, chunks, fetch, after=()):
        width, n = weight.shape[1], len(chunks)
        outs, fetched = call(
            order,
            functools.partial(pair_part_kernel, n_pair, chunks),
            [*blocks, weight],
            [pltpu.VMEM((half, width), F32)]
            + [pltpu.VMEM((half, wide), PAIR_TYPE) for _, wide in chunks] * (n_pair - 1)
            + [pltpu.VMEM((rows, depth), BF16)] * (len(blocks) > 1),
            fetch,
            [pltpu.VMEM((rows, tile_of(width)), F32)],
            COST * 2 * rows * depth * width,
            COST * 2 * bytes_of(fetch),
            after,
        )
        got = [send(outs[1 + (k - 1) * n + j], "pair", k) for k in range(1, n_pair) for j in range(n)]
        return (outs[0], *got), outs[-1], fetched

    def pair_sum(parts, chunks, pieces, after=()):
        outs = call(
            order, functools.partial(pair_sum_kernel, chunks), parts,
            [pltpu.VMEM((half, width), kind) for kind in (F32, BF16) for _, width in pieces],
            [], [], 0, COST * 8 * parts[0].size, after,
        )[0]
        sums = []
        for own, away in zip(outs[: len(pieces)], outs[len(pieces) :]):
            sums.append([own] + [send(away, "seq", k) for k in range(1, n_seq)])
        return sums

    def activate(ups, gates, start, width):
        (hidden,), _ = call(
            order, functools.partial(activate_kernel, start), [*ups, *gates],
            [pltpu.VMEM((half, width), BF16)], [], [], 0, COST * 8 * half * width,
        )
        got = [send(hidden, "pair", k) for k in range(1, n_pair)]
        return [hidden, *got]

    def load(array, fetch, traffic, after=()):
        (array,), fetched = call(
            order, load_kernel, [array], [pltpu.VMEM(array.shape, BF16)], fetch, [], 0, traffic, after
        )
        return array, fetched

    def multiply_down(j, parts, total):
        first, last = j == 0, j == n - 1
        width = parts[0].shape[1]
        if last:
            outs = [pltpu.VMEM((share, features), F32)]
            outs += [pltpu.VMEM((share, features), BF16)] * (n_wide - 1)
        else:
            outs = [pltpu.VMEM((rows, features), F32)]
        fetch = down_of(2) if first and n > 3 else []
        total, fetched = call(
            order,
            functools.partial(down_kernel, n_wide, first, last),
            [*parts, down[j], *total],
            outs,
            fetch,
            [pltpu.VMEM((rows, width), BF16)],
            COST * 2 * rows * width * features,
            COST * 2 * bytes_of(fetch),
        )
        if fetch:
            down[2] = fetched[0]
        return total

    tokens, early = load(tokens, [(down_weight, 0, 0, 16)], 2 * up_weight.size * size)
    blocks = [tokens] + [send(tokens, "wide", k) for k in range(1, n_wide)]
    up = pltpu.with_memory_space_constraint(up_weight, pltpu.VMEM)
    ups, x, (gate,) = project(blocks, up, chunks, gate_of(0), early)
    down = {}
    if n > 1:
        x, (down[n - 1],) = load(x, down_of(n - 1), COST * 2 * bytes_of(down_of(n - 1)))
    columns = gate_weight.shape[1]
    (ups,) = pair_sum(ups, chunks, [(0, columns)])
    gates = []
    for j, (start, width) in enumerate(loads):
        inner = [(a - start, b) for a, b in chunks if start <= a < start + width]
        last = j == len(loads) - 1
        parts, _, (weight,) = project([x], gate, inner, down_of(0) if last else gate_of(j + 1))
        if last:
            down[0] = weight
        else:
            gate = weight
        gates.append((parts, inner))
    sums = pair_sum(*gates[0], gates[0][1])
    if n > 2:
        _, (down[1],) = load(x, down_of(1), COST * 2 * bytes_of(down_of(1)))
    load(x, [], 0, ups[1:])
    for parts, inner in gates[1:]:
        sums += pair_sum(parts, inner, inner)
    hiddens = [activate(ups, sums[j], *chunks[j]) for j in range(min(n, 2))]
    total = []
    for j in range(n):
        if j and j + 1 < n:
            hiddens.append(activate(ups, sums[j + 1], *chunks[j + 1]))
        total = multiply_down(j, hiddens[j], total)

    result = total[0]
    for k in range(1, n_wide):
        result = result + send(total[k], "wide", k).astype(F32)
    return result.astype(BF16)


def solution(mesh):
    return jax.shard_map(
        functools.partial(shards, dict(mesh.shape)),
        mesh=mesh,
        in_specs=(
            P(("parts", "wide"), ("seq", "pair")),
            P(("seq", "pair"), "wide"),
            P(("seq", "pair"), "wide"),
            P("wide", ("seq", "pair")),
        ),
        out_specs=P(("parts", "wide"), ("seq", "pair")),
        check_vma=False,
    )
```

```python
import functools

import jax
import jax.numpy as jnp
from jax import lax
from jax.experimental import pallas as pl
from jax.experimental.pallas import tpu as pltpu
from jax.sharding import PartitionSpec as P

BF16, F32 = jnp.bfloat16, jnp.float32
TILE = 512
GATE = (8, 5)
DOWN = (4, 4, 3, 2)
PAIR_TYPE = F32
COST = 1
SPLIT = 2


def on_chip():
    return pl.BlockSpec(memory_space=pltpu.VMEM)


def in_place():
    return pl.BlockSpec(memory_space=pl.ANY)


def cuts(columns, shares):
    if columns % (TILE * sum(shares)):
        return [(0, columns)]
    unit = columns // sum(shares)
    chunks, start = [], 0
    for share in shares:
        chunks.append((start, share * unit))
        start += share * unit
    return chunks


def tile_of(width):
    return TILE if width % TILE == 0 else width


def copies(fetch, sources, targets, sems):
    made = []
    for at, ((axis, start, size), source, target) in enumerate(zip(fetch, sources, targets)):
        view = source.at[:, pl.ds(start, size)] if axis else source.at[pl.ds(start, size), :]
        made.append(pltpu.make_async_copy(view, target, sems.at[at]))
    return made


def call(order, body, operands, outs, fetch, scratch, flops, traffic, after=()):
    fetched = []
    for array, axis, start, size in fetch:
        shape = (array.shape[0], size) if axis else (size, array.shape[1])
        fetched.append(pltpu.VMEM(shape, array.dtype))
    n_in = len(operands)
    after = [*after, *order[-1:]]

    def kernel(*refs):
        ins, rest = refs[:n_in], refs[n_in + len(after) :]
        sources, rest = rest[: len(fetch)], rest[len(fetch) :]
        results, rest = rest[: len(outs)], rest[len(outs) :]
        targets, (*room, sems) = rest[: len(fetch)], rest[len(fetch) :]
        made = copies([f[1:] for f in fetch], sources, targets, sems)
        for copy in made:
            copy.start()
        body(ins, results, room)
        for copy in made:
            copy.wait()

    out = pl.pallas_call(
        kernel,
        out_shape=tuple(outs) + tuple(fetched),
        in_specs=[on_chip()] * n_in + [in_place()] * (len(after) + len(fetch)),
        out_specs=tuple([on_chip()] * (len(outs) + len(fetch))),
        scratch_shapes=list(scratch) + [pltpu.SemaphoreType.DMA((max(len(fetch), 1),))],
        compiler_params=pltpu.CompilerParams(vmem_limit_bytes=4 * 2**20),
        cost_estimate=pl.CostEstimate(flops=int(flops), bytes_accessed=int(traffic), transcendentals=0),
    )(*operands, *after, *[pltpu.with_memory_space_constraint(f[0], pltpu.HBM) for f in fetch])
    order.append(min(out, key=lambda array: array.size))
    return out[: len(outs)], out[len(outs) :]


def load_kernel(ins, outs, room):
    for source, target in zip(ins, outs):
        target[...] = source[...]


def pair_part_kernel(n_pair, chunks, ins, outs, room):
    *blocks, weight = ins
    n = len(chunks)
    keep, sends = outs[0], outs[1 : 1 + n * (n_pair - 1)]
    x = blocks[0]
    if len(outs) > 1 + len(sends):
        x = outs[-1]
        share = blocks[0].shape[0]
        for k, block in enumerate(blocks):
            x[k * share : (k + 1) * share, :] = block[...]
    (res,) = room
    me = lax.axis_index("pair")
    rows = keep.shape[0]
    for j, (start, width) in enumerate(chunks):
        tile = tile_of(width)

        @pl.loop(0, width // tile)
        def _(step, j=j, start=start, tile=tile):
            def at(offset):
                return pl.ds(pl.multiple_of(offset + step * tile, tile), tile)

            res[...] = jnp.dot(x[...], weight[:, at(start)], preferred_element_type=F32)
            for k in range(n_pair):
                block = pl.ds(pl.multiple_of(lax.rem(me + k, n_pair) * rows, 16), rows)
                target, offset = (sends[(k - 1) * n + j], 0) if k else (keep, start)
                target[:, at(offset)] = res[block, :].astype(target.dtype)


def pair_sum_kernel(chunks, ins, outs, room):
    keep, got = ins[0], ins[1:]
    n, half = len(chunks), len(outs) // 2
    for j, (start, width) in enumerate(chunks):
        at = slice(start, start + width)
        total = keep[:, at]
        for part in got[j::n]:
            total += part[...].astype(F32)
        for own in (0, half):
            out = outs[own + j] if half == n else outs[own]
            out[:, slice(0, width) if half == n else at] = total.astype(out.dtype)


def activate_kernel(start, ins, outs, room):
    at = slice(start, start + outs[0].shape[1])
    half = len(ins) // 2
    up = sum(part[:, at].astype(F32) for part in ins[:half])
    gate = sum(part[...].astype(F32) for part in ins[half:])
    hidden = (gate / (1.0 + jnp.exp(-gate)) * up).astype(BF16)
    rows = outs[0].shape[0]
    for k, out in enumerate(outs):
        out[...] = hidden[k * rows : (k + 1) * rows]


def down_kernel(n_pair, n_wide, first, last, ins, outs, room):
    parts, (wd, *before) = (ins[:-1], ins[-1:]) if first else (ins[:-2], ins[-2:])
    (hidden,) = room
    c = lax.axis_index("pair")
    rows = parts[0].shape[0]
    pieces = len(parts) // n_pair
    for at, part in enumerate(parts):
        k, piece = divmod(at, pieces)
        block = lax.rem(c + n_pair - k, n_pair) * pieces + piece
        hidden[pl.ds(pl.multiple_of(block * rows, 16), rows), :] = part[...]
    width = wd.shape[1]
    tile = tile_of(width)

    @pl.loop(0, width // tile)
    def _(step):
        at = pl.ds(pl.multiple_of(step * tile, tile), tile)
        total = jnp.dot(hidden[...], wd[:, at], preferred_element_type=F32)
        if before:
            total += before[0][:, at]
        if last:
            share = total.shape[0] // n_wide
            for k in range(n_wide):
                place = (n_wide - k) % n_wide * share
                outs[k][:, at] = total[place : place + share].astype(outs[k].dtype)
        else:
            outs[0][:, at] = total


def shards(sizes, tokens, gate_weight, up_weight, down_weight):
    n_seq, n_wide, n_pair = sizes["seq"], sizes["wide"], sizes["pair"]

    def send(value, axis, k):
        n = sizes[axis]
        return lax.ppermute(value, axis, [(i, (i + k) % n) for i in range(n)])

    share, depth = tokens.shape
    rows = share * n_wide
    features = down_weight.shape[1]
    half = rows // n_pair
    loads = cuts(gate_weight.shape[1], GATE)
    chunks = cuts(down_weight.shape[0], DOWN)
    n = len(chunks)
    size = tokens.dtype.itemsize

    def gate_of(*picks):
        return [(gate_weight, 1, *loads[j]) for j in picks if j < len(loads)]

    def bytes_of(fetch):
        return sum(size * f[3] * f[0].shape[1 - f[1]] for f in fetch)

    def down_of(*picks):
        return [(down_weight, 0, *chunks[j]) for j in picks if j < n]

    order = []

    def project(blocks, weight, chunks, fetch, after=()):
        width, n = weight.shape[1], len(chunks)
        outs, fetched = call(
            order,
            functools.partial(pair_part_kernel, n_pair, chunks),
            [*blocks, weight],
            [pltpu.VMEM((half, width), F32)]
            + [pltpu.VMEM((half, wide), PAIR_TYPE) for _, wide in chunks] * (n_pair - 1)
            + [pltpu.VMEM((rows, depth), BF16)] * (len(blocks) > 1),
            fetch,
            [pltpu.VMEM((rows, tile_of(width)), F32)],
            COST * 2 * rows * depth * width,
            COST * 2 * bytes_of(fetch),
            after,
        )
        got = [send(outs[1 + (k - 1) * n + j], "pair", k) for k in range(1, n_pair) for j in range(n)]
        return (outs[0], *got), outs[-1], fetched

    def pair_sum(parts, chunks, pieces, after=()):
        outs = call(
            order, functools.partial(pair_sum_kernel, chunks), parts,
            [pltpu.VMEM((half, width), kind) for kind in (F32, BF16) for _, width in pieces],
            [], [], 0, COST * 8 * parts[0].size, after,
        )[0]
        sums = []
        for own, away in zip(outs[: len(pieces)], outs[len(pieces) :]):
            sums.append([own] + [send(away, "seq", k) for k in range(1, n_seq)])
        return sums

    def activate(ups, gates, start, width):
        hidden, _ = call(
            order, functools.partial(activate_kernel, start), [*ups, *gates],
            [pltpu.VMEM((half // SPLIT, width), BF16)] * SPLIT, [], [], 0, COST * 8 * half * width,
        )
        got = [send(piece, "pair", k) for k in range(1, n_pair) for piece in hidden]
        return [*hidden, *got]

    def load(array, fetch, traffic, after=()):
        (array,), fetched = call(
            order, load_kernel, [array], [pltpu.VMEM(array.shape, BF16)], fetch, [], 0, traffic, after
        )
        return array, fetched

    def multiply_down(j, parts, total):
        first, last = j == 0, j == n - 1
        width = parts[0].shape[1]
        if last:
            outs = [pltpu.VMEM((share, features), F32)]
            outs += [pltpu.VMEM((share, features), BF16)] * (n_wide - 1)
        else:
            outs = [pltpu.VMEM((rows, features), F32)]
        fetch = down_of(2) if first and n > 3 else []
        total, fetched = call(
            order,
            functools.partial(down_kernel, n_pair, n_wide, first, last),
            [*parts, down[j], *total],
            outs,
            fetch,
            [pltpu.VMEM((rows, width), BF16)],
            COST * 2 * rows * width * features,
            COST * 2 * bytes_of(fetch),
        )
        if fetch:
            down[2] = fetched[0]
        return total

    _, (tokens, *early) = call(
        order, load_kernel, [], [], [(tokens, 0, 0, share), (down_weight, 0, 0, share)], [],
        0, 2 * up_weight.size * size,
    )
    blocks = [tokens] + [send(tokens, "wide", k) for k in range(1, n_wide)]
    up = pltpu.with_memory_space_constraint(up_weight, pltpu.VMEM)
    columns = gate_weight.shape[1]
    ups, x, (gate,) = project(blocks, up, [(0, columns)], gate_of(0), early)
    down = {}
    if n > 1:
        x, (down[n - 1],) = load(x, down_of(n - 1), COST * 2 * bytes_of(down_of(n - 1)))
    (ups,) = pair_sum(ups, [(0, columns)], [(0, columns)])
    gates = []
    for j, (start, width) in enumerate(loads):
        inner = [(a - start, b) for a, b in chunks if start <= a < start + width]
        last = j == len(loads) - 1
        parts, _, (weight,) = project([x], gate, inner, down_of(0) if last else gate_of(j + 1))
        if last:
            down[0] = weight
        else:
            gate = weight
        gates.append((parts, inner))
    sums = pair_sum(*gates[0], gates[0][1])
    if n > 2:
        _, (down[1],) = load(x, down_of(1), COST * 2 * bytes_of(down_of(1)))
    load(x, [], 0, ups[1:])
    for parts, inner in gates[1:]:
        sums += pair_sum(parts, inner, inner)
    hiddens = [activate(ups, sums[j], *chunks[j]) for j in range(min(n, 2))]
    total = []
    for j in range(n):
        if j and j + 1 < n:
            hiddens.append(activate(ups, sums[j + 1], *chunks[j + 1]))
        total = multiply_down(j, hiddens[j], total)

    result = total[0]
    for k in range(1, n_wide):
        result = result + send(total[k], "wide", k).astype(F32)
    return result.astype(BF16)


def solution(mesh):
    return jax.shard_map(
        functools.partial(shards, dict(mesh.shape)),
        mesh=mesh,
        in_specs=(
            P(("parts", "wide"), ("seq", "pair")),
            P(("seq", "pair"), "wide"),
            P(("seq", "pair"), "wide"),
            P("wide", ("seq", "pair")),
        ),
        out_specs=P(("parts", "wide"), ("seq", "pair")),
        check_vma=False,
    )
```

```python
import functools

import jax
import jax.numpy as jnp
from jax import lax
from jax.experimental import pallas as pl
from jax.experimental.pallas import tpu as pltpu
from jax.sharding import PartitionSpec as P

BF16, F32 = jnp.bfloat16, jnp.float32
TILE = 512
GATE = (8, 5)
DOWN = (4, 4, 3, 2)
PAIR_TYPE = F32
COST = 1
SPLIT = 2


def on_chip():
    return pl.BlockSpec(memory_space=pltpu.VMEM)


def in_place():
    return pl.BlockSpec(memory_space=pl.ANY)


def cuts(columns, shares):
    if columns % (TILE * sum(shares)):
        return [(0, columns)]
    unit = columns // sum(shares)
    chunks, start = [], 0
    for share in shares:
        chunks.append((start, share * unit))
        start += share * unit
    return chunks


def tile_of(width):
    return TILE if width % TILE == 0 else width


def copies(fetch, sources, targets, sems):
    made = []
    for at, ((axis, start, size), source, target) in enumerate(zip(fetch, sources, targets)):
        view = source.at[:, pl.ds(start, size)] if axis else source.at[pl.ds(start, size), :]
        made.append(pltpu.make_async_copy(view, target, sems.at[at]))
    return made


def call(order, body, operands, outs, fetch, scratch, flops, traffic, after=()):
    fetched = []
    for array, axis, start, size in fetch:
        shape = (array.shape[0], size) if axis else (size, array.shape[1])
        fetched.append(pltpu.VMEM(shape, array.dtype))
    n_in = len(operands)
    after = [*after, *order[-1:]]

    def kernel(*refs):
        ins, rest = refs[:n_in], refs[n_in + len(after) :]
        sources, rest = rest[: len(fetch)], rest[len(fetch) :]
        results, rest = rest[: len(outs)], rest[len(outs) :]
        targets, (*room, sems) = rest[: len(fetch)], rest[len(fetch) :]
        made = copies([f[1:] for f in fetch], sources, targets, sems)
        for copy in made:
            copy.start()
        body(ins, results, room)
        for copy in made:
            copy.wait()

    out = pl.pallas_call(
        kernel,
        out_shape=tuple(outs) + tuple(fetched),
        in_specs=[on_chip()] * n_in + [in_place()] * (len(after) + len(fetch)),
        out_specs=tuple([on_chip()] * (len(outs) + len(fetch))),
        scratch_shapes=list(scratch) + [pltpu.SemaphoreType.DMA((max(len(fetch), 1),))],
        compiler_params=pltpu.CompilerParams(vmem_limit_bytes=4 * 2**20),
        cost_estimate=pl.CostEstimate(flops=int(flops), bytes_accessed=int(traffic), transcendentals=0),
    )(*operands, *after, *[pltpu.with_memory_space_constraint(f[0], pltpu.HBM) for f in fetch])
    order.append(min(out, key=lambda array: array.size))
    return out[: len(outs)], out[len(outs) :]


def load_kernel(ins, outs, room):
    for source, target in zip(ins, outs):
        target[...] = source[...]


def pair_part_kernel(n_pair, chunks, ins, outs, room):
    *blocks, weight = ins
    n = len(chunks)
    keep, sends = outs[0], outs[1 : 1 + n * (n_pair - 1)]
    x = blocks[0]
    if len(outs) > 1 + len(sends):
        x = outs[-1]
        share = blocks[0].shape[0]
        for k, block in enumerate(blocks):
            x[k * share : (k + 1) * share, :] = block[...]
    (res,) = room
    me = lax.axis_index("pair")
    rows = keep.shape[0]
    for j, (start, width) in enumerate(chunks):
        tile = tile_of(width)

        @pl.loop(0, width // tile)
        def _(step, j=j, start=start, tile=tile):
            def at(offset):
                return pl.ds(pl.multiple_of(offset + step * tile, tile), tile)

            res[...] = jnp.dot(x[...], weight[:, at(start)], preferred_element_type=F32)
            for k in range(n_pair):
                block = pl.ds(pl.multiple_of(lax.rem(me + k, n_pair) * rows, 16), rows)
                target, offset = (sends[(k - 1) * n + j], 0) if k else (keep, start)
                target[:, at(offset)] = res[block, :].astype(target.dtype)


def pair_sum_kernel(chunks, ins, outs, room):
    keep, got = ins[0], ins[1:]
    n, half = len(chunks), len(outs) // 2
    for j, (start, width) in enumerate(chunks):
        at = slice(start, start + width)
        total = keep[:, at]
        for part in got[j::n]:
            total += part[...].astype(F32)
        for own in (0, half):
            out = outs[own + j] if half == n else outs[own]
            out[:, slice(0, width) if half == n else at] = total.astype(out.dtype)


def activate_kernel(start, ins, outs, room):
    at = slice(start, start + outs[0].shape[1])
    half = len(ins) // 2
    up = sum(part[:, at].astype(F32) for part in ins[:half])
    gate = sum(part[...].astype(F32) for part in ins[half:])
    hidden = (gate / (1.0 + jnp.exp(-gate)) * up).astype(BF16)
    rows = outs[0].shape[0]
    for k, out in enumerate(outs):
        out[...] = hidden[k * rows : (k + 1) * rows]


def down_kernel(n_pair, n_wide, first, last, ins, outs, room):
    parts, (wd, *before) = (ins[:-1], ins[-1:]) if first else (ins[:-2], ins[-2:])
    (hidden,) = room
    c = lax.axis_index("pair")
    rows = parts[0].shape[0]
    pieces = len(parts) // n_pair
    for at, part in enumerate(parts):
        k, piece = divmod(at, pieces)
        block = lax.rem(c + n_pair - k, n_pair) * pieces + piece
        hidden[pl.ds(pl.multiple_of(block * rows, 16), rows), :] = part[...]
    width = wd.shape[1]
    tile = tile_of(width)

    @pl.loop(0, width // tile)
    def _(step):
        at = pl.ds(pl.multiple_of(step * tile, tile), tile)
        total = jnp.dot(hidden[...], wd[:, at], preferred_element_type=F32)
        if before:
            total += before[0][:, at]
        if last:
            share = total.shape[0] // n_wide
            for k in range(n_wide):
                place = (k if n_wide & (n_wide - 1) == 0 else (n_wide - k) % n_wide) * share
                outs[k][:, at] = total[place : place + share].astype(outs[k].dtype)
        else:
            outs[0][:, at] = total


def shards(sizes, tokens, gate_weight, up_weight, down_weight):
    n_seq, n_wide, n_pair = sizes["seq"], sizes["wide"], sizes["pair"]

    def send(value, axis, k):
        n = sizes[axis]
        paired = axis == "wide" and n & (n - 1) == 0
        return lax.ppermute(value, axis, [(i, i ^ k if paired else (i + k) % n) for i in range(n)])

    share, depth = tokens.shape
    rows = share * n_wide
    features = down_weight.shape[1]
    half = rows // n_pair
    loads = cuts(gate_weight.shape[1], GATE)
    chunks = cuts(down_weight.shape[0], DOWN)
    n = len(chunks)
    size = tokens.dtype.itemsize

    def gate_of(*picks):
        return [(gate_weight, 1, *loads[j]) for j in picks if j < len(loads)]

    def bytes_of(fetch):
        return sum(size * f[3] * f[0].shape[1 - f[1]] for f in fetch)

    def down_of(*picks):
        return [(down_weight, 0, *chunks[j]) for j in picks if j < n]

    order = []

    def project(blocks, weight, chunks, fetch, after=()):
        width, n = weight.shape[1], len(chunks)
        outs, fetched = call(
            order,
            functools.partial(pair_part_kernel, n_pair, chunks),
            [*blocks, weight],
            [pltpu.VMEM((half, width), F32)]
            + [pltpu.VMEM((half, wide), PAIR_TYPE) for _, wide in chunks] * (n_pair - 1)
            + [pltpu.VMEM((rows, depth), BF16)] * (len(blocks) > 1),
            fetch,
            [pltpu.VMEM((rows, tile_of(width)), F32)],
            COST * 2 * rows * depth * width,
            COST * 2 * bytes_of(fetch),
            after,
        )
        got = [send(outs[1 + (k - 1) * n + j], "pair", k) for k in range(1, n_pair) for j in range(n)]
        return (outs[0], *got), outs[-1], fetched

    def pair_sum(parts, chunks, pieces, after=()):
        outs = call(
            order, functools.partial(pair_sum_kernel, chunks), parts,
            [pltpu.VMEM((half, width), kind) for kind in (F32, BF16) for _, width in pieces],
            [], [], 0, COST * 8 * parts[0].size, after,
        )[0]
        sums = []
        for own, away in zip(outs[: len(pieces)], outs[len(pieces) :]):
            sums.append([own] + [send(away, "seq", k) for k in range(1, n_seq)])
        return sums

    def activate(ups, gates, start, width):
        hidden, _ = call(
            order, functools.partial(activate_kernel, start), [*ups, *gates],
            [pltpu.VMEM((half // SPLIT, width), BF16)] * SPLIT, [], [], 0, COST * 8 * half * width,
        )
        got = [send(piece, "pair", k) for k in range(1, n_pair) for piece in hidden]
        return [*hidden, *got]

    def load(array, fetch, traffic, after=()):
        (array,), fetched = call(
            order, load_kernel, [array], [pltpu.VMEM(array.shape, BF16)], fetch, [], 0, traffic, after
        )
        return array, fetched

    def multiply_down(j, parts, total):
        first, last = j == 0, j == n - 1
        width = parts[0].shape[1]
        if last:
            outs = [pltpu.VMEM((share, features), F32)]
            outs += [pltpu.VMEM((share, features), BF16)] * (n_wide - 1)
        else:
            outs = [pltpu.VMEM((rows, features), F32)]
        return call(
            order,
            functools.partial(down_kernel, n_pair, n_wide, first, last),
            [*parts, down[j], *total],
            outs,
            [],
            [pltpu.VMEM((rows, width), BF16)],
            COST * 2 * rows * width * features,
            0,
        )[0]

    _, (tokens, *early) = call(
        order, load_kernel, [], [], [(tokens, 0, 0, share), (down_weight, 0, 0, share)], [],
        0, 2 * up_weight.size * size,
    )
    blocks = [tokens] + [send(tokens, "wide", k) for k in range(1, n_wide)]
    up = pltpu.with_memory_space_constraint(up_weight, pltpu.VMEM)
    columns = gate_weight.shape[1]
    ups, x, (gate,) = project(blocks, up, [(0, columns)], gate_of(0), early)
    down, gates = {}, []
    for j, (start, width) in enumerate(loads):
        inner = [(a - start, b) for a, b in chunks if start <= a < start + width]
        last = j == len(loads) - 1
        parts, _, (weight,) = project([x], gate, inner, down_of(0) if last else gate_of(j + 1))
        if last:
            down[0] = weight
        else:
            gate = weight
        gates.append((parts, inner))
        if j == 0:
            (ups,) = pair_sum(ups, [(0, columns)], [(0, columns)])
    sums = pair_sum(*gates[0], gates[0][1])
    if n > 1:
        late = list(range(1, n))
        _, more = load(x, down_of(*late), COST * 2 * bytes_of(down_of(*late)))
        down.update(zip(late, more))
    load(x, [], 0, ups[1:])
    for parts, inner in gates[1:]:
        sums += pair_sum(parts, inner, inner)
    hiddens = [activate(ups, sums[j], *chunks[j]) for j in range(min(n, 2))]
    total = []
    for j in range(n):
        if j and j + 1 < n:
            hiddens.append(activate(ups, sums[j + 1], *chunks[j + 1]))
        total = multiply_down(j, hiddens[j], total)

    result = total[0]
    for k in range(1, n_wide):
        result = result + send(total[k], "wide", k).astype(F32)
    return result.astype(BF16)


def solution(mesh):
    return jax.shard_map(
        functools.partial(shards, dict(mesh.shape)),
        mesh=mesh,
        in_specs=(
            P(("parts", "wide"), ("seq", "pair")),
            P(("seq", "pair"), "wide"),
            P(("seq", "pair"), "wide"),
            P("wide", ("seq", "pair")),
        ),
        out_specs=P(("parts", "wide"), ("seq", "pair")),
        check_vma=False,
    )
```

```python
import functools

import jax
import jax.numpy as jnp
from jax import lax
from jax.experimental import pallas as pl
from jax.experimental.pallas import tpu as pltpu
from jax.sharding import PartitionSpec as P

BF16, F32 = jnp.bfloat16, jnp.float32
TILE = 512
GATE = (9, 4)
DOWN = (4, 5, 4)
PAIR_TYPE = F32
COST = 1
SPLIT = 2


def on_chip():
    return pl.BlockSpec(memory_space=pltpu.VMEM)


def in_place():
    return pl.BlockSpec(memory_space=pl.ANY)


def cuts(columns, shares):
    if columns % (TILE * sum(shares)):
        return [(0, columns)]
    unit = columns // sum(shares)
    chunks, start = [], 0
    for share in shares:
        chunks.append((start, share * unit))
        start += share * unit
    return chunks


def tile_of(width):
    return TILE if width % TILE == 0 else width


def copies(fetch, sources, targets, sems):
    made = []
    for at, ((axis, start, size), source, target) in enumerate(zip(fetch, sources, targets)):
        view = source.at[:, pl.ds(start, size)] if axis else source.at[pl.ds(start, size), :]
        made.append(pltpu.make_async_copy(view, target, sems.at[at]))
    return made


def call(order, body, operands, outs, fetch, scratch, flops, traffic, after=()):
    fetched = []
    for array, axis, start, size in fetch:
        shape = (array.shape[0], size) if axis else (size, array.shape[1])
        fetched.append(pltpu.VMEM(shape, array.dtype))
    n_in = len(operands)
    after = [*after, *order[-1:]]

    def kernel(*refs):
        ins, rest = refs[:n_in], refs[n_in + len(after) :]
        sources, rest = rest[: len(fetch)], rest[len(fetch) :]
        results, rest = rest[: len(outs)], rest[len(outs) :]
        targets, (*room, sems) = rest[: len(fetch)], rest[len(fetch) :]
        made = copies([f[1:] for f in fetch], sources, targets, sems)
        for copy in made:
            copy.start()
        body(ins, results, room)
        for copy in made:
            copy.wait()

    out = pl.pallas_call(
        kernel,
        out_shape=tuple(outs) + tuple(fetched),
        in_specs=[on_chip()] * n_in + [in_place()] * (len(after) + len(fetch)),
        out_specs=tuple([on_chip()] * (len(outs) + len(fetch))),
        scratch_shapes=list(scratch) + [pltpu.SemaphoreType.DMA((max(len(fetch), 1),))],
        compiler_params=pltpu.CompilerParams(vmem_limit_bytes=4 * 2**20),
        cost_estimate=pl.CostEstimate(flops=int(flops), bytes_accessed=int(traffic), transcendentals=0),
    )(*operands, *after, *[pltpu.with_memory_space_constraint(f[0], pltpu.HBM) for f in fetch])
    order.append(min(out, key=lambda array: array.size))
    return out[: len(outs)], out[len(outs) :]


def load_kernel(ins, outs, room):
    for source, target in zip(ins, outs):
        target[...] = source[...]


def pair_part_kernel(n_pair, chunks, ins, outs, room):
    *blocks, weight = ins
    n = len(chunks)
    keep, sends = outs[0], outs[1 : 1 + n * (n_pair - 1)]
    x = blocks[0]
    if len(outs) > 1 + len(sends):
        x = outs[-1]
        share = blocks[0].shape[0]
        for k, block in enumerate(blocks):
            x[k * share : (k + 1) * share, :] = block[...]
    (res,) = room
    me = lax.axis_index("pair")
    rows = keep.shape[0]
    for j, (start, width) in enumerate(chunks):
        tile = tile_of(width)

        @pl.loop(0, width // tile)
        def _(step, j=j, start=start, tile=tile):
            def at(offset):
                return pl.ds(pl.multiple_of(offset + step * tile, tile), tile)

            res[...] = jnp.dot(x[...], weight[:, at(start)], preferred_element_type=F32)
            for k in range(n_pair):
                block = pl.ds(pl.multiple_of(lax.rem(me + k, n_pair) * rows, 16), rows)
                target, offset = (sends[(k - 1) * n + j], 0) if k else (keep, start)
                target[:, at(offset)] = res[block, :].astype(target.dtype)


def pair_sum_kernel(chunks, ins, outs, room):
    keep, got = ins[0], ins[1:]
    n, half = len(chunks), len(outs) // 2
    for j, (start, width) in enumerate(chunks):
        at = slice(start, start + width)
        total = keep[:, at]
        for part in got[j::n]:
            total += part[...].astype(F32)
        for own in (0, half):
            out = outs[own + j] if half == n else outs[own]
            out[:, slice(0, width) if half == n else at] = total.astype(out.dtype)


def activate_kernel(start, ins, outs, room):
    at = slice(start, start + outs[0].shape[1])
    half = len(ins) // 2
    up = sum(part[:, at].astype(F32) for part in ins[:half])
    gate = sum(part[...].astype(F32) for part in ins[half:])
    hidden = (gate / (1.0 + jnp.exp(-gate)) * up).astype(BF16)
    rows = outs[0].shape[0]
    for k, out in enumerate(outs):
        out[...] = hidden[k * rows : (k + 1) * rows]


def down_kernel(n_pair, n_wide, first, last, ins, outs, room):
    parts, (wd, *before) = (ins[:-1], ins[-1:]) if first else (ins[:-2], ins[-2:])
    (hidden,) = room
    c = lax.axis_index("pair")
    rows = parts[0].shape[0]
    pieces = len(parts) // n_pair
    for at, part in enumerate(parts):
        k, piece = divmod(at, pieces)
        block = lax.rem(c + n_pair - k, n_pair) * pieces + piece
        hidden[pl.ds(pl.multiple_of(block * rows, 16), rows), :] = part[...]
    width = wd.shape[1]
    tile = tile_of(width)

    @pl.loop(0, width // tile)
    def _(step):
        at = pl.ds(pl.multiple_of(step * tile, tile), tile)
        total = jnp.dot(hidden[...], wd[:, at], preferred_element_type=F32)
        if before:
            total += before[0][:, at]
        if last:
            share = total.shape[0] // n_wide
            for k in range(n_wide):
                place = (k if n_wide & (n_wide - 1) == 0 else (n_wide - k) % n_wide) * share
                outs[k][:, at] = total[place : place + share].astype(outs[k].dtype)
        else:
            outs[0][:, at] = total


def shards(sizes, tokens, gate_weight, up_weight, down_weight):
    n_seq, n_wide, n_pair = sizes["seq"], sizes["wide"], sizes["pair"]

    def send(value, axis, k):
        n = sizes[axis]
        paired = axis == "wide" and n & (n - 1) == 0
        return lax.ppermute(value, axis, [(i, i ^ k if paired else (i + k) % n) for i in range(n)])

    share, depth = tokens.shape
    rows = share * n_wide
    features = down_weight.shape[1]
    half = rows // n_pair
    loads = cuts(gate_weight.shape[1], GATE)
    chunks = cuts(down_weight.shape[0], DOWN)
    n = len(chunks)
    size = tokens.dtype.itemsize

    def gate_of(*picks):
        return [(gate_weight, 1, *loads[j]) for j in picks if j < len(loads)]

    def bytes_of(fetch):
        return sum(size * f[3] * f[0].shape[1 - f[1]] for f in fetch)

    def down_of(*picks):
        return [(down_weight, 0, *chunks[j]) for j in picks if j < n]

    order = []

    def project(blocks, weight, chunks, fetch, after=()):
        width, n = weight.shape[1], len(chunks)
        outs, fetched = call(
            order,
            functools.partial(pair_part_kernel, n_pair, chunks),
            [*blocks, weight],
            [pltpu.VMEM((half, width), F32)]
            + [pltpu.VMEM((half, wide), PAIR_TYPE) for _, wide in chunks] * (n_pair - 1)
            + [pltpu.VMEM((rows, depth), BF16)] * (len(blocks) > 1),
            fetch,
            [pltpu.VMEM((rows, tile_of(width)), F32)],
            COST * 2 * rows * depth * width,
            COST * 2 * bytes_of(fetch),
            after,
        )
        got = [send(outs[1 + (k - 1) * n + j], "pair", k) for k in range(1, n_pair) for j in range(n)]
        return (outs[0], *got), outs[-1], fetched

    def pair_sum(parts, chunks, pieces, after=()):
        outs = call(
            order, functools.partial(pair_sum_kernel, chunks), parts,
            [pltpu.VMEM((half, width), kind) for kind in (F32, BF16) for _, width in pieces],
            [], [], 0, COST * 8 * parts[0].size, after,
        )[0]
        sums = []
        for own, away in zip(outs[: len(pieces)], outs[len(pieces) :]):
            sums.append([own] + [send(away, "seq", k) for k in range(1, n_seq)])
        return sums

    def activate(ups, gates, start, width):
        hidden, _ = call(
            order, functools.partial(activate_kernel, start), [*ups, *gates],
            [pltpu.VMEM((half // SPLIT, width), BF16)] * SPLIT, [], [], 0, COST * 8 * half * width,
        )
        got = [send(piece, "pair", k) for k in range(1, n_pair) for piece in hidden]
        return [*hidden, *got]

    def load(array, fetch, traffic, after=()):
        (array,), fetched = call(
            order, load_kernel, [array], [pltpu.VMEM(array.shape, BF16)], fetch, [], 0, traffic, after
        )
        return array, fetched

    def multiply_down(j, parts, total):
        first, last = j == 0, j == n - 1
        width = parts[0].shape[1]
        if last:
            outs = [pltpu.VMEM((share, features), F32)]
            outs += [pltpu.VMEM((share, features), BF16)] * (n_wide - 1)
        else:
            outs = [pltpu.VMEM((rows, features), F32)]
        return call(
            order,
            functools.partial(down_kernel, n_pair, n_wide, first, last),
            [*parts, down[j], *total],
            outs,
            [],
            [pltpu.VMEM((rows, width), BF16)],
            COST * 2 * rows * width * features,
            0,
        )[0]

    _, (tokens, *early) = call(
        order, load_kernel, [], [], [(tokens, 0, 0, share), (down_weight, 0, 0, share)], [],
        0, 2 * up_weight.size * size,
    )
    blocks = [tokens] + [send(tokens, "wide", k) for k in range(1, n_wide)]
    up = pltpu.with_memory_space_constraint(up_weight, pltpu.VMEM)
    columns = gate_weight.shape[1]
    ups, x, (gate,) = project(blocks, up, [(0, columns)], gate_of(0), early)
    down, gates = {}, []
    for j, (start, width) in enumerate(loads):
        inner = [(a - start, b) for a, b in chunks if start <= a < start + width]
        last = j == len(loads) - 1
        parts, _, (weight,) = project([x], gate, inner, down_of(0) if last else gate_of(j + 1))
        if last:
            down[0] = weight
        else:
            gate = weight
        gates.append((parts, inner))
        if j == 0:
            (ups,) = pair_sum(ups, [(0, columns)], [(0, columns)])
    sums = []
    for parts, inner in gates:
        sums += pair_sum(parts, inner, inner)
    if n > 1:
        late = list(range(1, n))
        _, more = load(x, down_of(*late), 0)
        down.update(zip(late, more))
    load(x, [], 0, ups[1:])
    hiddens = [activate(ups, sums[j], *chunks[j]) for j in range(min(n, 2))]
    total = []
    for j in range(n):
        if j and j + 1 < n:
            hiddens.append(activate(ups, sums[j + 1], *chunks[j + 1]))
        total = multiply_down(j, hiddens[j], total)

    result = total[0]
    for k in range(1, n_wide):
        result = result + send(total[k], "wide", k).astype(F32)
    return result.astype(BF16)


def solution(mesh):
    return jax.shard_map(
        functools.partial(shards, dict(mesh.shape)),
        mesh=mesh,
        in_specs=(
            P(("parts", "wide"), ("seq", "pair")),
            P(("seq", "pair"), "wide"),
            P(("seq", "pair"), "wide"),
            P("wide", ("seq", "pair")),
        ),
        out_specs=P(("parts", "wide"), ("seq", "pair")),
        check_vma=False,
    )
```

```python
import functools

import jax
import jax.numpy as jnp
from jax import lax
from jax.experimental import pallas as pl
from jax.experimental.pallas import tpu as pltpu
from jax.sharding import PartitionSpec as P

BF16, F32 = jnp.bfloat16, jnp.float32
TILE = 512
GATE = (4, 4, 5)
UP = (7, 6)
DOWN = (4, 4, 5)
PAIR_TYPE = BF16
COST = 1
SPLIT = 2


def on_chip():
    return pl.BlockSpec(memory_space=pltpu.VMEM)


def in_place():
    return pl.BlockSpec(memory_space=pl.ANY)


def cuts(columns, shares):
    if columns % (TILE * sum(shares)):
        return [(0, columns)]
    unit = columns // sum(shares)
    chunks, start = [], 0
    for share in shares:
        chunks.append((start, share * unit))
        start += share * unit
    return chunks


def tile_of(width):
    return TILE if width % TILE == 0 else width


def copies(fetch, sources, targets, sems):
    made = []
    for at, ((axis, start, size), source, target) in enumerate(zip(fetch, sources, targets)):
        view = source.at[:, pl.ds(start, size)] if axis else source.at[pl.ds(start, size), :]
        made.append(pltpu.make_async_copy(view, target, sems.at[at]))
    return made


def call(order, body, operands, outs, fetch, scratch, flops, traffic, after=(), carry=()):
    fetched = []
    moves = [*fetch, *((operands[-1], *move) for move in carry)]
    for array, axis, start, size in moves:
        shape = (array.shape[0], size) if axis else (size, array.shape[1])
        fetched.append(pltpu.VMEM(shape, array.dtype))
    n_in = len(operands)
    after = [*after, *order[-1:]]

    def kernel(*refs):
        ins, rest = refs[:n_in], refs[n_in + len(after) :]
        sources, rest = [*rest[: len(fetch)], *[ins[-1] for _ in carry]], rest[len(fetch) :]
        results, rest = rest[: len(outs)], rest[len(outs) :]
        targets, (*room, sems) = rest[: len(moves)], rest[len(moves) :]
        made = copies([move[1:] for move in moves], sources, targets, sems)
        for copy in made:
            copy.start()
        body(ins, results, room)
        for copy in made:
            copy.wait()

    out = pl.pallas_call(
        kernel,
        out_shape=tuple(outs) + tuple(fetched),
        in_specs=[on_chip()] * n_in + [in_place()] * (len(after) + len(fetch)),
        out_specs=tuple([on_chip()] * (len(outs) + len(moves))),
        scratch_shapes=list(scratch) + [pltpu.SemaphoreType.DMA((max(len(moves), 1),))],
        compiler_params=pltpu.CompilerParams(vmem_limit_bytes=4 * 2**20),
        cost_estimate=pl.CostEstimate(flops=int(flops), bytes_accessed=int(traffic), transcendentals=0),
    )(*operands, *after, *[pltpu.with_memory_space_constraint(f[0], pltpu.HBM) for f in fetch])
    order.append(min(out, key=lambda array: array.size))
    return out[: len(outs)], out[len(outs) :]


def load_kernel(ins, outs, room):
    for source, target in zip(ins, outs):
        target[...] = source[...]


def pair_part_kernel(n_pair, chunks, n_weights, ins, outs, room):
    blocks, weights = ins[:-n_weights], ins[-n_weights:]
    n = len(chunks)
    keep, sends = outs[0], outs[1 : 1 + n * (n_pair - 1)]
    x = blocks[0]
    if len(outs) > 1 + len(sends):
        x = outs[-1]
        share = blocks[0].shape[0]
        for k, block in enumerate(blocks):
            x[k * share : (k + 1) * share, :] = block[...]
    (res,) = room
    me = lax.axis_index("pair")
    rows = keep.shape[0]
    start = 0
    for weight in weights:
        for j, (first, width) in enumerate(chunks):
            low, high = max(start, first), min(start + weight.shape[1], first + width)
            if low >= high:
                continue
            tile = tile_of(high - low)

            @pl.loop(0, (high - low) // tile)
            def _(step, weight=weight, tile=tile, j=j, low=low, first=first, start=start):
                def at(offset):
                    return pl.ds(pl.multiple_of(offset + step * tile, tile), tile)

                res[...] = jnp.dot(x[...], weight[:, at(low - start)], preferred_element_type=F32)
                for k in range(n_pair):
                    block = pl.ds(pl.multiple_of(lax.rem(me + k, n_pair) * rows, 16), rows)
                    target, offset = (sends[(k - 1) * n + j], low - first) if k else (keep, low)
                    target[:, at(offset)] = res[block, :].astype(target.dtype)

        start += weight.shape[1]


def pair_sum_kernel(chunks, ins, outs, room):
    keep, got = ins[0], ins[1:]
    n, half = len(chunks), len(outs) // 2
    for j, (start, width) in enumerate(chunks):
        at = slice(start, start + width)
        total = keep[:, at]
        for part in got[j::n]:
            total += part[...].astype(F32)
        for own in (0, half):
            out = outs[own + j] if half == n else outs[own]
            out[:, slice(0, width) if half == n else at] = total.astype(out.dtype)


def pair_join_kernel(widths, ins, outs, room):
    count, start = len(ins) // len(widths), 0
    for j, width in enumerate(widths):
        total = sum(part[...].astype(F32) for part in ins[j * count : (j + 1) * count])
        for out in outs:
            out[:, start : start + width] = total.astype(out.dtype)
        start += width


def activate_kernel(slices, ins, outs, room):
    n_parts = len(ins) // (len(slices) + 1)
    pieces = []
    for j, at in enumerate(slices):
        pieces.append(sum(part[:, at].astype(F32) for part in ins[j * n_parts : (j + 1) * n_parts]))
    up = pieces[0] if len(pieces) == 1 else jnp.concatenate(pieces, axis=1)
    gate = sum(part[...].astype(F32) for part in ins[len(slices) * n_parts :])
    hidden = (gate / (1.0 + jnp.exp(-gate)) * up).astype(BF16)
    rows = outs[0].shape[0]
    for k, out in enumerate(outs):
        out[...] = hidden[k * rows : (k + 1) * rows]


def down_kernel(n_pair, n_wide, first, last, ins, outs, room):
    parts, (wd, *before) = (ins[:-1], ins[-1:]) if first else (ins[:-2], ins[-2:])
    (hidden,) = room
    c = lax.axis_index("pair")
    rows = parts[0].shape[0]
    pieces = len(parts) // n_pair
    for at, part in enumerate(parts):
        k, piece = divmod(at, pieces)
        block = lax.rem(c + n_pair - k, n_pair) * pieces + piece
        hidden[pl.ds(pl.multiple_of(block * rows, 16), rows), :] = part[...]
    width = wd.shape[1]
    tile = tile_of(width)

    @pl.loop(0, width // tile)
    def _(step):
        at = pl.ds(pl.multiple_of(step * tile, tile), tile)
        total = jnp.dot(hidden[...], wd[:, at], preferred_element_type=F32)
        if before:
            total += before[0][:, at]
        if last:
            share = total.shape[0] // n_wide
            for k in range(n_wide):
                place = (k if n_wide & (n_wide - 1) == 0 else (n_wide - k) % n_wide) * share
                outs[k][:, at] = total[place : place + share].astype(outs[k].dtype)
        else:
            outs[0][:, at] = total


def shards(sizes, tokens, gate_weight, up_weight, down_weight):
    n_seq, n_wide, n_pair = sizes["seq"], sizes["wide"], sizes["pair"]

    def send(value, axis, k):
        n = sizes[axis]
        paired = axis == "wide" and n & (n - 1) == 0
        return lax.ppermute(value, axis, [(i, i ^ k if paired else (i + k) % n) for i in range(n)])

    share, depth = tokens.shape
    rows = share * n_wide
    features = down_weight.shape[1]
    half = rows // n_pair
    loads = cuts(gate_weight.shape[1], GATE)
    chunks = cuts(down_weight.shape[0], DOWN)
    n = len(chunks)
    size = tokens.dtype.itemsize

    def gate_of(*picks):
        return [(gate_weight, 1, *loads[j]) for j in picks if j < len(loads)]

    def bytes_of(fetch):
        return sum(size * f[3] * f[0].shape[1 - f[1]] for f in fetch)

    def down_of(*picks):
        return [(down_weight, 0, *chunks[j]) for j in picks if j < n]

    order = []

    def project(blocks, weights, chunks, fetch, after=(), carry=()):
        width, n = sum(width for _, width in chunks), len(chunks)
        outs, fetched = call(
            order,
            functools.partial(pair_part_kernel, n_pair, chunks, len(weights)),
            [*blocks, *weights],
            [pltpu.VMEM((half, width), F32)]
            + [pltpu.VMEM((half, wide), PAIR_TYPE) for _, wide in chunks] * (n_pair - 1)
            + [pltpu.VMEM((rows, depth), BF16)] * (len(blocks) > 1),
            fetch,
            [pltpu.VMEM((rows, tile_of(width)), F32)],
            COST * 2 * rows * depth * width,
            COST * 2 * bytes_of(fetch),
            after,
            carry,
        )
        got = [send(outs[1 + (k - 1) * n + j], "pair", k) for k in range(1, n_pair) for j in range(n)]
        return (outs[0], *got), outs[-1], fetched

    def pair_sum(parts, chunks, pieces, after=()):
        outs = call(
            order, functools.partial(pair_sum_kernel, chunks), parts,
            [pltpu.VMEM((half, width), kind) for kind in (F32, BF16) for _, width in pieces],
            [], [], 0, COST * 8 * parts[0].size, after,
        )[0]
        sums = []
        for own, away in zip(outs[: len(pieces)], outs[len(pieces) :]):
            sums.append([own] + [send(away, "seq", k) for k in range(1, n_seq)])
        return sums

    def activate(j):
        start, width = chunks[j]
        slices, parts = [], []
        for (first, wide), up in zip(spans, ups):
            low, high = max(start, first), min(start + width, first + wide)
            if low < high:
                slices.append(slice(low - first, high - first))
                parts += up
        hidden, _ = call(
            order, functools.partial(activate_kernel, slices), [*parts, *sums[j]],
            [pltpu.VMEM((half // SPLIT, width), BF16)] * SPLIT, [], [], 0, COST * 8 * half * width,
        )
        got = [send(piece, "pair", k) for k in range(1, n_pair) for piece in hidden]
        return [*hidden, *got]

    def load(array, fetch, traffic, after=()):
        (array,), fetched = call(
            order, load_kernel, [array], [pltpu.VMEM(array.shape, BF16)], fetch, [], 0, traffic, after
        )
        return array, fetched

    def multiply_down(j, parts, total):
        first, last = j == 0, j == n - 1
        width = parts[0].shape[1]
        if last:
            outs = [pltpu.VMEM((share, features), F32)]
            outs += [pltpu.VMEM((share, features), BF16)] * (n_wide - 1)
        else:
            outs = [pltpu.VMEM((rows, features), F32)]
        return call(
            order,
            functools.partial(down_kernel, n_pair, n_wide, first, last),
            [*parts, down[j], *total],
            outs,
            [],
            [pltpu.VMEM((rows, width), BF16)],
            COST * 2 * rows * width * features,
            0,
        )[0]

    _, (tokens, *early) = call(
        order, load_kernel, [], [], [(tokens, 0, 0, share), (down_weight, 0, 0, share)], [],
        0, 2 * up_weight.size * size,
    )
    blocks = [tokens] + [send(tokens, "wide", k) for k in range(1, n_wide)]
    up = pltpu.with_memory_space_constraint(up_weight, pltpu.VMEM)
    spans = cuts(up_weight.shape[1], UP)
    ups, gate, down, sums = [], [], {}, []
    if n == 1:
        parts, x, gate = project(blocks, [up], spans, gate_of(0), early)
        ups = pair_sum(parts, spans, spans)
        parts, _, (down[0],) = project([x], gate, chunks, down_of(0))
        sums = pair_sum(parts, chunks, chunks)
    else:
        parts, x, (gate_0, rest) = project(blocks, [up], spans[:1], gate_of(0), early, [(1, *spans[1])])
        more, _, (gate_1,) = project([x], [rest], [(0, spans[1][1])], gate_of(1))
        columns = up_weight.shape[1]
        (own, away), _ = call(
            order, functools.partial(pair_join_kernel, [width for _, width in spans]), [*parts, *more],
            [pltpu.VMEM((half, columns), F32), pltpu.VMEM((half, columns), BF16)],
            [], [], 0, COST * 8 * half * columns,
        )
        ups.append([own] + [send(away, "seq", k) for k in range(1, n_seq)])
        spans = [(0, columns)]
        edge = loads[2][0]
        inner = [chunk for chunk in chunks if chunk[0] < edge]
        parts, _, (gate_2,) = project([x], [gate_0, gate_1], inner, gate_of(2))
        rest = [(start - edge, width) for start, width in chunks if start >= edge]
        more, _, (down[0],) = project([x], [gate_2], rest, down_of(0))
        sums = pair_sum(parts, inner, inner) + pair_sum(more, rest, rest)
    if n > 1:
        late = list(range(1, n))
        _, more = load(x, down_of(*late), 0)
        down.update(zip(late, more))
    load(x, [], 0, [part for up in ups for part in up[1:]])
    hiddens = [activate(j) for j in range(min(n, 2))]
    total = []
    for j in range(n):
        if j and j + 1 < n:
            hiddens.append(activate(j + 1))
        total = multiply_down(j, hiddens[j], total)

    result = total[0]
    for k in reversed(range(1, n_wide)):
        result = result + send(total[k], "wide", k).astype(F32)
    return result.astype(BF16)


def solution(mesh):
    return jax.shard_map(
        functools.partial(shards, dict(mesh.shape)),
        mesh=mesh,
        in_specs=(
            P(("parts", "wide"), ("seq", "pair")),
            P(("seq", "pair"), "wide"),
            P(("seq", "pair"), "wide"),
            P("wide", ("seq", "pair")),
        ),
        out_specs=P(("parts", "wide"), ("seq", "pair")),
        check_vma=False,
    )
```

```python
import functools

import jax
import jax.numpy as jnp
from jax import lax
from jax.experimental import pallas as pl
from jax.experimental.pallas import tpu as pltpu
from jax.sharding import PartitionSpec as P

BF16, F32 = jnp.bfloat16, jnp.float32
TILE = 512
GATE = (8, 5)
DOWN = (4, 4, 5)
PAIR_TYPE = BF16
COST = 1
SPLIT = 2


def on_chip():
    return pl.BlockSpec(memory_space=pltpu.VMEM)


def in_place():
    return pl.BlockSpec(memory_space=pl.ANY)


def cuts(columns, shares):
    if columns % (TILE * sum(shares)):
        return [(0, columns)]
    unit = columns // sum(shares)
    chunks, start = [], 0
    for share in shares:
        chunks.append((start, share * unit))
        start += share * unit
    return chunks


def tile_of(width):
    return TILE if width % TILE == 0 else width


def copies(fetch, sources, targets, sems):
    made = []
    for at, ((axis, start, size), source, target) in enumerate(zip(fetch, sources, targets)):
        view = source.at[:, pl.ds(start, size)] if axis else source.at[pl.ds(start, size), :]
        made.append(pltpu.make_async_copy(view, target, sems.at[at]))
    return made


def call(order, body, operands, outs, fetch, scratch, flops, traffic, after=()):
    fetched = []
    for array, axis, start, size in fetch:
        shape = (array.shape[0], size) if axis else (size, array.shape[1])
        fetched.append(pltpu.VMEM(shape, array.dtype))
    n_in = len(operands)
    after = [*after, *order[-1:]]

    def kernel(*refs):
        ins, rest = refs[:n_in], refs[n_in + len(after) :]
        sources, rest = rest[: len(fetch)], rest[len(fetch) :]
        results, rest = rest[: len(outs)], rest[len(outs) :]
        targets, (*room, sems) = rest[: len(fetch)], rest[len(fetch) :]
        made = copies([f[1:] for f in fetch], sources, targets, sems)
        for copy in made:
            copy.start()
        body(ins, results, room)
        for copy in made:
            copy.wait()

    out = pl.pallas_call(
        kernel,
        out_shape=tuple(outs) + tuple(fetched),
        in_specs=[on_chip()] * n_in + [in_place()] * (len(after) + len(fetch)),
        out_specs=tuple([on_chip()] * (len(outs) + len(fetch))),
        scratch_shapes=list(scratch) + [pltpu.SemaphoreType.DMA((max(len(fetch), 1),))],
        compiler_params=pltpu.CompilerParams(vmem_limit_bytes=4 * 2**20),
        cost_estimate=pl.CostEstimate(flops=int(flops), bytes_accessed=int(traffic), transcendentals=0),
    )(*operands, *after, *[pltpu.with_memory_space_constraint(f[0], pltpu.HBM) for f in fetch])
    order.append(min(out, key=lambda array: array.size))
    return out[: len(outs)], out[len(outs) :]


def load_kernel(ins, outs, room):
    for source, target in zip(ins, outs):
        target[...] = source[...]


def pair_part_kernel(n_pair, chunks, ins, outs, room):
    *blocks, weight = ins
    n = len(chunks)
    keep, sends = outs[0], outs[1 : 1 + n * (n_pair - 1)]
    x = blocks[0]
    if len(outs) > 1 + len(sends):
        x = outs[-1]
        share = blocks[0].shape[0]
        for k, block in enumerate(blocks):
            x[k * share : (k + 1) * share, :] = block[...]
    (res,) = room
    me = lax.axis_index("pair")
    rows = keep.shape[0]
    for j, (start, width) in enumerate(chunks):
        tile = tile_of(width)

        @pl.loop(0, width // tile)
        def _(step, j=j, start=start, tile=tile):
            def at(offset):
                return pl.ds(pl.multiple_of(offset + step * tile, tile), tile)

            res[...] = jnp.dot(x[...], weight[:, at(start)], preferred_element_type=F32)
            for k in range(n_pair):
                block = pl.ds(pl.multiple_of(lax.rem(me + k, n_pair) * rows, 16), rows)
                target, offset = (sends[(k - 1) * n + j], 0) if k else (keep, start)
                target[:, at(offset)] = res[block, :].astype(target.dtype)


def pair_sum_kernel(chunks, ins, outs, room):
    keep, got = ins[0], ins[1:]
    n, half = len(chunks), len(outs) // 2
    for j, (start, width) in enumerate(chunks):
        at = slice(start, start + width)
        total = keep[:, at]
        for part in got[j::n]:
            total += part[...].astype(F32)
        for own in (0, half):
            out = outs[own + j] if half == n else outs[own]
            out[:, slice(0, width) if half == n else at] = total.astype(out.dtype)


def activate_kernel(start, ins, outs, room):
    at = slice(start, start + outs[0].shape[1])
    half = len(ins) // 2
    up = sum(part[:, at].astype(F32) for part in ins[:half])
    gate = sum(part[...].astype(F32) for part in ins[half:])
    hidden = (gate / (1.0 + jnp.exp(-gate)) * up).astype(BF16)
    rows = outs[0].shape[0]
    for k, out in enumerate(outs):
        out[...] = hidden[k * rows : (k + 1) * rows]


def down_kernel(n_pair, n_wide, first, last, ins, outs, room):
    parts, (wd, *before) = (ins[:-1], ins[-1:]) if first else (ins[:-2], ins[-2:])
    (hidden,) = room
    c = lax.axis_index("pair")
    rows = parts[0].shape[0]
    pieces = len(parts) // n_pair
    for at, part in enumerate(parts):
        k, piece = divmod(at, pieces)
        block = lax.rem(c + n_pair - k, n_pair) * pieces + piece
        hidden[pl.ds(pl.multiple_of(block * rows, 16), rows), :] = part[...]
    width = wd.shape[1]
    tile = tile_of(width)

    @pl.loop(0, width // tile)
    def _(step):
        at = pl.ds(pl.multiple_of(step * tile, tile), tile)
        total = jnp.dot(hidden[...], wd[:, at], preferred_element_type=F32)
        if before:
            total += before[0][:, at]
        if last:
            share = total.shape[0] // n_wide
            for k in range(n_wide):
                place = (k if n_wide & (n_wide - 1) == 0 else (n_wide - k) % n_wide) * share
                outs[k][:, at] = total[place : place + share].astype(outs[k].dtype)
        else:
            outs[0][:, at] = total


def shards(sizes, tokens, gate_weight, up_weight, down_weight):
    n_seq, n_wide, n_pair = sizes["seq"], sizes["wide"], sizes["pair"]

    def send(value, axis, k):
        n = sizes[axis]
        paired = axis == "wide" and n & (n - 1) == 0
        return lax.ppermute(value, axis, [(i, i ^ k if paired else (i + k) % n) for i in range(n)])

    share, depth = tokens.shape
    rows = share * n_wide
    features = down_weight.shape[1]
    half = rows // n_pair
    loads = cuts(gate_weight.shape[1], GATE)
    chunks = cuts(down_weight.shape[0], DOWN)
    n = len(chunks)
    size = tokens.dtype.itemsize

    def gate_of(*picks):
        return [(gate_weight, 1, *loads[j]) for j in picks if j < len(loads)]

    def bytes_of(fetch):
        return sum(size * f[3] * f[0].shape[1 - f[1]] for f in fetch)

    def down_of(*picks):
        return [(down_weight, 0, *chunks[j]) for j in picks if j < n]

    order = []

    def project(blocks, weight, chunks, fetch, after=()):
        width, n = weight.shape[1], len(chunks)
        outs, fetched = call(
            order,
            functools.partial(pair_part_kernel, n_pair, chunks),
            [*blocks, weight],
            [pltpu.VMEM((half, width), F32)]
            + [pltpu.VMEM((half, wide), PAIR_TYPE) for _, wide in chunks] * (n_pair - 1)
            + [pltpu.VMEM((rows, depth), BF16)] * (len(blocks) > 1),
            fetch,
            [pltpu.VMEM((rows, tile_of(width)), F32)],
            COST * 2 * rows * depth * width,
            COST * 2 * bytes_of(fetch),
            after,
        )
        got = [send(outs[1 + (k - 1) * n + j], "pair", k) for k in range(1, n_pair) for j in range(n)]
        return (outs[0], *got), outs[-1], fetched

    def pair_sum(parts, chunks, pieces, after=()):
        outs = call(
            order, functools.partial(pair_sum_kernel, chunks), parts,
            [pltpu.VMEM((half, width), kind) for kind in (F32, BF16) for _, width in pieces],
            [], [], 0, COST * 8 * parts[0].size, after,
        )[0]
        sums = []
        for own, away in zip(outs[: len(pieces)], outs[len(pieces) :]):
            sums.append([own] + [send(away, "seq", k) for k in range(1, n_seq)])
        return sums

    def activate(ups, gates, start, width):
        hidden, _ = call(
            order, functools.partial(activate_kernel, start), [*ups, *gates],
            [pltpu.VMEM((half // SPLIT, width), BF16)] * SPLIT, [], [], 0, COST * 8 * half * width,
        )
        got = [send(piece, "pair", k) for k in range(1, n_pair) for piece in hidden]
        return [*hidden, *got]

    def load(array, fetch, traffic, after=()):
        (array,), fetched = call(
            order, load_kernel, [array], [pltpu.VMEM(array.shape, BF16)], fetch, [], 0, traffic, after
        )
        return array, fetched

    def multiply_down(j, parts, total):
        first, last = j == 0, j == n - 1
        width = parts[0].shape[1]
        if last:
            outs = [pltpu.VMEM((share, features), F32)]
            outs += [pltpu.VMEM((share, features), BF16)] * (n_wide - 1)
        else:
            outs = [pltpu.VMEM((rows, features), F32)]
        return call(
            order,
            functools.partial(down_kernel, n_pair, n_wide, first, last),
            [*parts, down[j], *total],
            outs,
            [],
            [pltpu.VMEM((rows, width), BF16)],
            COST * 2 * rows * width * features,
            0,
        )[0]

    _, (tokens, *early) = call(
        order, load_kernel, [], [], [(tokens, 0, 0, share), (down_weight, 0, 0, share)], [],
        0, 2 * up_weight.size * size,
    )
    blocks = [tokens] + [send(tokens, "wide", k) for k in range(1, n_wide)]
    up = pltpu.with_memory_space_constraint(up_weight, pltpu.VMEM)
    columns = gate_weight.shape[1]
    ups, x, (gate,) = project(blocks, up, [(0, columns)], gate_of(0), early)
    (ups,) = pair_sum(ups, [(0, columns)], [(0, columns)])
    down, gates = {}, []
    for j, (start, width) in enumerate(loads):
        inner = [(a - start, b) for a, b in chunks if start <= a < start + width]
        last = j == len(loads) - 1
        parts, _, (weight,) = project([x], gate, inner, down_of(0) if last else gate_of(j + 1))
        if last:
            down[0] = weight
        else:
            gate = weight
        gates.append((parts, inner))
    sums = []
    for parts, inner in gates:
        sums += pair_sum(parts, inner, inner)
    if n > 1:
        late = list(range(1, n))
        _, more = load(x, down_of(*late), 0)
        down.update(zip(late, more))
    load(x, [], 0, ups[1:])
    hiddens = [activate(ups, sums[j], *chunks[j]) for j in range(min(n, 2))]
    total = []
    for j in range(n):
        if j and j + 1 < n:
            hiddens.append(activate(ups, sums[j + 1], *chunks[j + 1]))
        total = multiply_down(j, hiddens[j], total)

    result = total[0]
    for k in reversed(range(1, n_wide)):
        result = result + send(total[k], "wide", k).astype(F32)
    return result.astype(BF16)


def solution(mesh):
    return jax.shard_map(
        functools.partial(shards, dict(mesh.shape)),
        mesh=mesh,
        in_specs=(
            P(("parts", "wide"), ("seq", "pair")),
            P(("seq", "pair"), "wide"),
            P(("seq", "pair"), "wide"),
            P("wide", ("seq", "pair")),
        ),
        out_specs=P(("parts", "wide"), ("seq", "pair")),
        check_vma=False,
    )
```

```python
import functools

import jax
import jax.numpy as jnp
from jax import lax
from jax.experimental import pallas as pl
from jax.experimental.pallas import tpu as pltpu
from jax.sharding import PartitionSpec as P

BF16, F32 = jnp.bfloat16, jnp.float32
TILE = 512
GATE = (8, 2, 3)
DOWN = (5, 5, 3)
DOWN_LOADS = dict(gate=((0, 3),), rest=((3, 1),), late=((4, 1), (5, 5), (10, 3)))
PAIR_TYPE = BF16
COST = 0.05
SPLIT = 2


def on_chip():
    return pl.BlockSpec(memory_space=pltpu.VMEM)


def in_place():
    return pl.BlockSpec(memory_space=pl.ANY)


def cuts(columns, shares):
    if columns % (TILE * sum(shares)):
        return [(0, columns)]
    unit = columns // sum(shares)
    chunks, start = [], 0
    for share in shares:
        chunks.append((start, share * unit))
        start += share * unit
    return chunks


def tile_of(width):
    return TILE if width % TILE == 0 else width


def copies(fetch, sources, targets, sems):
    made = []
    for at, ((axis, start, size), source, target) in enumerate(zip(fetch, sources, targets)):
        view = source.at[:, pl.ds(start, size)] if axis else source.at[pl.ds(start, size), :]
        made.append(pltpu.make_async_copy(view, target, sems.at[at]))
    return made


def call(order, body, operands, outs, fetch, scratch, flops, traffic, after=()):
    fetched = []
    for array, axis, start, size in fetch:
        shape = (array.shape[0], size) if axis else (size, array.shape[1])
        fetched.append(pltpu.VMEM(shape, array.dtype))
    n_in = len(operands)
    after = [*after, *order[-1:]]

    def kernel(*refs):
        ins, rest = refs[:n_in], refs[n_in + len(after) :]
        sources, rest = rest[: len(fetch)], rest[len(fetch) :]
        results, rest = rest[: len(outs)], rest[len(outs) :]
        targets, (*room, sems) = rest[: len(fetch)], rest[len(fetch) :]
        made = copies([f[1:] for f in fetch], sources, targets, sems)
        for copy in made:
            copy.start()
        body(ins, results, room)
        for copy in made:
            copy.wait()

    out = pl.pallas_call(
        kernel,
        out_shape=tuple(outs) + tuple(fetched),
        in_specs=[on_chip()] * n_in + [in_place()] * (len(after) + len(fetch)),
        out_specs=tuple([on_chip()] * (len(outs) + len(fetch))),
        scratch_shapes=list(scratch) + [pltpu.SemaphoreType.DMA((max(len(fetch), 1),))],
        compiler_params=pltpu.CompilerParams(vmem_limit_bytes=4 * 2**20),
        cost_estimate=pl.CostEstimate(flops=int(flops), bytes_accessed=int(traffic), transcendentals=0),
    )(*operands, *after, *[pltpu.with_memory_space_constraint(f[0], pltpu.HBM) for f in fetch])
    order.append(min(out, key=lambda array: array.size))
    return out[: len(outs)], out[len(outs) :]


def load_kernel(ins, outs, room):
    for source, target in zip(ins, outs):
        target[...] = source[...]


def pair_part_kernel(n_pair, chunks, n_weights, ins, outs, room):
    blocks, weights = ins[:-n_weights], ins[-n_weights:]
    n = len(chunks)
    keep, sends = outs[0], outs[1 : 1 + n * (n_pair - 1)]
    x = blocks[0]
    if len(outs) > 1 + len(sends):
        x = outs[-1]
        share = blocks[0].shape[0]
        for k, block in enumerate(blocks):
            x[k * share : (k + 1) * share, :] = block[...]
    (res,) = room
    me = lax.axis_index("pair")
    rows = keep.shape[0]
    start = 0
    for weight in weights:
        for j, (first, width) in enumerate(chunks):
            low, high = max(start, first), min(start + weight.shape[1], first + width)
            if low >= high:
                continue
            tile = tile_of(high - low)

            @pl.loop(0, (high - low) // tile)
            def _(step, weight=weight, tile=tile, j=j, low=low, first=first, start=start):
                def at(offset):
                    return pl.ds(pl.multiple_of(offset + step * tile, tile), tile)

                res[...] = jnp.dot(x[...], weight[:, at(low - start)], preferred_element_type=F32)
                for k in range(n_pair):
                    block = pl.ds(pl.multiple_of(lax.rem(me + k, n_pair) * rows, 16), rows)
                    target, offset = (sends[(k - 1) * n + j], low - first) if k else (keep, low)
                    target[:, at(offset)] = res[block, :].astype(target.dtype)

        start += weight.shape[1]


def pair_sum_kernel(chunks, ins, outs, room):
    keep, got = ins[0], ins[1:]
    n, half = len(chunks), len(outs) // 2
    for j, (start, width) in enumerate(chunks):
        at = slice(start, start + width)
        total = keep[:, at]
        for part in got[j::n]:
            total += part[...].astype(F32)
        for own in (0, half):
            out = outs[own + j] if half == n else outs[own]
            out[:, slice(0, width) if half == n else at] = total.astype(out.dtype)


def pair_join_kernel(counts, ins, outs, room):
    n_outs, at, chunk = len(outs) // 2, 0, 0
    received = (len(ins) - len(counts)) // sum(counts)
    for count in counts:
        own, got = ins[at], ins[at + 1 : at + 1 + received * count]
        start = 0
        for j in range(count):
            width = outs[chunk].shape[1]
            total = own[:, start : start + width]
            for part in got[j::count]:
                total += part[...].astype(F32)
            outs[chunk][...] = total
            outs[n_outs + chunk][...] = total.astype(BF16)
            start, chunk = start + width, chunk + 1
        at += 1 + len(got)


def activate_kernel(start, ins, outs, room):
    at = slice(start, start + outs[0].shape[1])
    half = len(ins) // 2
    up = sum(part[:, at].astype(F32) for part in ins[:half])
    gate = sum(part[...].astype(F32) for part in ins[half:])
    hidden = (gate / (1.0 + jnp.exp(-gate)) * up).astype(BF16)
    rows = outs[0].shape[0]
    for k, out in enumerate(outs):
        out[...] = hidden[k * rows : (k + 1) * rows]


def down_kernel(n_pair, n_wide, n_weights, first, last, ins, outs, room):
    before = ins[-1:] if not first else []
    ins = ins[: len(ins) - len(before)]
    parts, weights = ins[:-n_weights], ins[-n_weights:]
    (hidden,) = room
    c = lax.axis_index("pair")
    rows = parts[0].shape[0]
    pieces = len(parts) // n_pair
    for at, part in enumerate(parts):
        k, piece = divmod(at, pieces)
        block = lax.rem(c + n_pair - k, n_pair) * pieces + piece
        hidden[pl.ds(pl.multiple_of(block * rows, 16), rows), :] = part[...]
    width = weights[0].shape[1]
    tile = tile_of(width)

    @pl.loop(0, width // tile)
    def _(step):
        at = pl.ds(pl.multiple_of(step * tile, tile), tile)
        total, start = 0, 0
        for weight in weights:
            deep = slice(start, start + weight.shape[0])
            total += jnp.dot(hidden[:, deep], weight[:, at], preferred_element_type=F32)
            start += weight.shape[0]
        if before:
            total += before[0][:, at]
        if last:
            share = total.shape[0] // n_wide
            for k in range(n_wide):
                place = (k if n_wide & (n_wide - 1) == 0 else (n_wide - k) % n_wide) * share
                outs[k][:, at] = total[place : place + share].astype(outs[k].dtype)
        else:
            outs[0][:, at] = total


def shards(sizes, tokens, gate_weight, up_weight, down_weight):
    n_seq, n_wide, n_pair = sizes["seq"], sizes["wide"], sizes["pair"]

    def send(value, axis, k):
        n = sizes[axis]
        paired = axis == "wide" and n & (n - 1) == 0
        return lax.ppermute(value, axis, [(i, i ^ k if paired else (i + k) % n) for i in range(n)])

    share, depth = tokens.shape
    rows = share * n_wide
    features = down_weight.shape[1]
    half = rows // n_pair
    loads = cuts(gate_weight.shape[1], GATE)
    chunks = cuts(down_weight.shape[0], DOWN)
    n = len(chunks)
    size = tokens.dtype.itemsize

    def bytes_of(fetch):
        return sum(size * f[3] * f[0].shape[1 - f[1]] for f in fetch)

    unit = gate_weight.shape[1] // sum(GATE)

    def gate_of(j):
        return [(gate_weight, 1, *loads[j])]

    def down_of(name):
        return [(down_weight, 0, start * unit, count * unit) for start, count in DOWN_LOADS[name]]

    def keep(name, fetched):
        for (start, _), array in zip(DOWN_LOADS[name], fetched):
            down[start * unit] = array

    order = []

    def project(blocks, weights, chunks, fetch, after=()):
        width, n = sum(width for _, width in chunks), len(chunks)
        outs, fetched = call(
            order,
            functools.partial(pair_part_kernel, n_pair, chunks, len(weights)),
            [*blocks, *weights],
            [pltpu.VMEM((half, width), F32)]
            + [pltpu.VMEM((half, wide), PAIR_TYPE) for _, wide in chunks] * (n_pair - 1)
            + [pltpu.VMEM((rows, depth), BF16)] * (len(blocks) > 1),
            fetch,
            [pltpu.VMEM((rows, tile_of(width)), F32)],
            COST * 2 * rows * depth * width,
            COST * 2 * bytes_of(fetch),
            after,
        )
        got = [send(outs[1 + (k - 1) * n + j], "pair", k) for k in range(1, n_pair) for j in range(n)]
        return (outs[0], *got), outs[-1], fetched

    def pair_sum(parts, chunks, pieces, after=()):
        outs = call(
            order, functools.partial(pair_sum_kernel, chunks), parts,
            [pltpu.VMEM((half, width), kind) for kind in (F32, BF16) for _, width in pieces],
            [], [], 0, COST * 8 * parts[0].size, after,
        )[0]
        sums = []
        for own, away in zip(outs[: len(pieces)], outs[len(pieces) :]):
            sums.append([own] + [send(away, "seq", k) for k in range(1, n_seq)])
        return sums

    def pair_join(groups):
        widths = [width for _, inner in groups for _, width in inner]
        outs = call(
            order, functools.partial(pair_join_kernel, [len(inner) for _, inner in groups]),
            [part for parts, _ in groups for part in parts],
            [pltpu.VMEM((half, width), kind) for kind in (F32, BF16) for width in widths],
            [], [], 0, COST * 8 * half * sum(widths),
        )[0]
        sums = []
        for own, away in zip(outs[: len(widths)], outs[len(widths) :]):
            sums.append([own] + [send(away, "seq", k) for k in range(1, n_seq)])
        return sums

    def activate(ups, gates, start, width):
        hidden, _ = call(
            order, functools.partial(activate_kernel, start), [*ups, *gates],
            [pltpu.VMEM((half // SPLIT, width), BF16)] * SPLIT, [], [], 0, COST * 8 * half * width,
        )
        got = [send(piece, "pair", k) for k in range(1, n_pair) for piece in hidden]
        return [*hidden, *got]

    def load(array, fetch, traffic, after=()):
        (array,), fetched = call(
            order, load_kernel, [array], [pltpu.VMEM(array.shape, BF16)], fetch, [], 0, traffic, after
        )
        return array, fetched

    def multiply_down(j, parts, total):
        first, last = j == 0, j == n - 1
        start, width = chunks[j]
        weights = [down[at] for at in sorted(down) if start <= at < start + width]
        if last:
            outs = [pltpu.VMEM((share, features), F32)]
            outs += [pltpu.VMEM((share, features), BF16)] * (n_wide - 1)
        else:
            outs = [pltpu.VMEM((rows, features), F32)]
        return call(
            order,
            functools.partial(down_kernel, n_pair, n_wide, len(weights), first, last),
            [*parts, *weights, *total],
            outs,
            [],
            [pltpu.VMEM((rows, width), BF16)],
            COST * 2 * rows * width * features,
            0,
        )[0]

    _, (tokens, *early) = call(
        order, load_kernel, [], [], [(tokens, 0, 0, share), (down_weight, 0, 0, share)], [],
        0, 2 * up_weight.size * size,
    )
    blocks = [tokens] + [send(tokens, "wide", k) for k in range(1, n_wide)]
    up = pltpu.with_memory_space_constraint(up_weight, pltpu.VMEM)
    columns = gate_weight.shape[1]
    down, whole = {}, [(0, columns)]
    if n == 1:
        ups, x, gate = project(blocks, [up], whole, gate_of(0), early)
        (ups,) = pair_sum(ups, whole, whole)
        parts, _, (down[0],) = project([x], gate, chunks, [(down_weight, 0, 0, columns)])
        sums = pair_sum(parts, chunks, chunks)
    else:
        ups, x, first = project(blocks, [up], whole, gate_of(0), early)
        x, second = load(x, gate_of(1), COST * 2 * bytes_of(gate_of(1)))
        (ups,) = pair_sum(ups, whole, whole)
        edge = loads[2][0]
        inner = [chunk for chunk in chunks if chunk[0] < edge]
        parts, _, (third, *more) = project([x], [*first, *second], inner, gate_of(2) + down_of("gate"))
        keep("gate", more)
        outer = [(start - edge, width) for start, width in chunks if start >= edge]
        others, _, more = project([x], [third], outer, down_of("rest"))
        keep("rest", more)
        sums = pair_join([(parts, inner), (others, outer)])
        _, more = load(x, down_of("late"), 0)
        keep("late", more)
    load(x, [], 0, ups[1:])
    hiddens = [activate(ups, sums[j], *chunks[j]) for j in range(min(n, 2))]
    total = []
    for j in range(n):
        if j and j + 1 < n:
            hiddens.append(activate(ups, sums[j + 1], *chunks[j + 1]))
        total = multiply_down(j, hiddens[j], total)

    result = total[0]
    for k in reversed(range(1, n_wide)):
        result = result + send(total[k], "wide", k).astype(F32)
    return result.astype(BF16)


def solution(mesh):
    return jax.shard_map(
        functools.partial(shards, dict(mesh.shape)),
        mesh=mesh,
        in_specs=(
            P(("parts", "wide"), ("seq", "pair")),
            P(("seq", "pair"), "wide"),
            P(("seq", "pair"), "wide"),
            P("wide", ("seq", "pair")),
        ),
        out_specs=P(("parts", "wide"), ("seq", "pair")),
        check_vma=False,
    )
```

```python
import functools

import jax
import jax.numpy as jnp
from jax import lax
from jax.experimental import pallas as pl
from jax.experimental.pallas import tpu as pltpu
from jax.sharding import PartitionSpec as P

BF16, F32 = jnp.bfloat16, jnp.float32
TILE = 512
GATE = (8, 5)
DOWN = (4, 4, 5)
DOWN_LOADS = dict(wait=((0, 1),), gate=(), late=((1, 3), (4, 4), (8, 1)), first=((9, 2),), second=((11, 2),))
PAIR_TYPE = BF16
COST = 1
SPLIT = 2


def on_chip():
    return pl.BlockSpec(memory_space=pltpu.VMEM)


def in_place():
    return pl.BlockSpec(memory_space=pl.ANY)


def cuts(columns, shares):
    if columns % (TILE * sum(shares)):
        return [(0, columns)]
    unit = columns // sum(shares)
    chunks, start = [], 0
    for share in shares:
        chunks.append((start, share * unit))
        start += share * unit
    return chunks


def tile_of(width):
    return TILE if width % TILE == 0 else width


def copies(fetch, sources, targets, sems):
    made = []
    for at, ((axis, start, size), source, target) in enumerate(zip(fetch, sources, targets)):
        view = source.at[:, pl.ds(start, size)] if axis else source.at[pl.ds(start, size), :]
        made.append(pltpu.make_async_copy(view, target, sems.at[at]))
    return made


def call(order, body, operands, outs, fetch, scratch, flops, traffic, after=()):
    fetched = []
    for array, axis, start, size in fetch:
        shape = (array.shape[0], size) if axis else (size, array.shape[1])
        fetched.append(pltpu.VMEM(shape, array.dtype))
    n_in = len(operands)
    after = [*after, *order[-1:]]

    def kernel(*refs):
        ins, rest = refs[:n_in], refs[n_in + len(after) :]
        sources, rest = rest[: len(fetch)], rest[len(fetch) :]
        results, rest = rest[: len(outs)], rest[len(outs) :]
        targets, (*room, sems) = rest[: len(fetch)], rest[len(fetch) :]
        made = copies([f[1:] for f in fetch], sources, targets, sems)
        for copy in made:
            copy.start()
        body(ins, results, room)
        for copy in made:
            copy.wait()

    out = pl.pallas_call(
        kernel,
        out_shape=tuple(outs) + tuple(fetched),
        in_specs=[on_chip()] * n_in + [in_place()] * (len(after) + len(fetch)),
        out_specs=tuple([on_chip()] * (len(outs) + len(fetch))),
        scratch_shapes=list(scratch) + [pltpu.SemaphoreType.DMA((max(len(fetch), 1),))],
        compiler_params=pltpu.CompilerParams(vmem_limit_bytes=4 * 2**20),
        cost_estimate=pl.CostEstimate(flops=int(flops), bytes_accessed=int(traffic), transcendentals=0),
    )(*operands, *after, *[pltpu.with_memory_space_constraint(f[0], pltpu.HBM) for f in fetch])
    order.append(min(out, key=lambda array: array.size))
    return out[: len(outs)], out[len(outs) :]


def load_kernel(ins, outs, room):
    for source, target in zip(ins, outs):
        target[...] = source[...]


def pair_part_kernel(n_pair, chunks, n_weights, ins, outs, room):
    blocks, weights = ins[:-n_weights], ins[-n_weights:]
    n = len(chunks)
    keep, sends = outs[0], outs[1 : 1 + n * (n_pair - 1)]
    x = blocks[0]
    if len(outs) > 1 + len(sends):
        x = outs[-1]
        share = blocks[0].shape[0]
        for k, block in enumerate(blocks):
            x[k * share : (k + 1) * share, :] = block[...]
    (res,) = room
    me = lax.axis_index("pair")
    rows = keep.shape[0]
    start = 0
    for weight in weights:
        for j, (first, width) in enumerate(chunks):
            low, high = max(start, first), min(start + weight.shape[1], first + width)
            if low >= high:
                continue
            tile = tile_of(high - low)

            @pl.loop(0, (high - low) // tile)
            def _(step, weight=weight, tile=tile, j=j, low=low, first=first, start=start):
                def at(offset):
                    return pl.ds(pl.multiple_of(offset + step * tile, tile), tile)

                res[...] = jnp.dot(x[...], weight[:, at(low - start)], preferred_element_type=F32)
                for k in range(n_pair):
                    block = pl.ds(pl.multiple_of(lax.rem(me + k, n_pair) * rows, 16), rows)
                    target, offset = (sends[(k - 1) * n + j], low - first) if k else (keep, low)
                    target[:, at(offset)] = res[block, :].astype(target.dtype)

        start += weight.shape[1]


def pair_sum_kernel(chunks, ins, outs, room):
    keep, got = ins[0], ins[1:]
    n, half = len(chunks), len(outs) // 2
    for j, (start, width) in enumerate(chunks):
        at = slice(start, start + width)
        total = keep[:, at]
        for part in got[j::n]:
            total += part[...].astype(F32)
        for own in (0, half):
            out = outs[own + j] if half == n else outs[own]
            out[:, slice(0, width) if half == n else at] = total.astype(out.dtype)


def pair_join_kernel(counts, ins, outs, room):
    n_outs, at, chunk = len(outs) // 2, 0, 0
    received = (len(ins) - len(counts)) // sum(counts)
    for count in counts:
        own, got = ins[at], ins[at + 1 : at + 1 + received * count]
        start = 0
        for j in range(count):
            width = outs[chunk].shape[1]
            total = own[:, start : start + width]
            for part in got[j::count]:
                total += part[...].astype(F32)
            outs[chunk][...] = total
            outs[n_outs + chunk][...] = total.astype(BF16)
            start, chunk = start + width, chunk + 1
        at += 1 + len(got)


def activate_kernel(start, ins, outs, room):
    at = slice(start, start + outs[0].shape[1])
    half = len(ins) // 2
    up = sum(part[:, at].astype(F32) for part in ins[:half])
    gate = sum(part[...].astype(F32) for part in ins[half:])
    hidden = (gate / (1.0 + jnp.exp(-gate)) * up).astype(BF16)
    rows = outs[0].shape[0]
    for k, out in enumerate(outs):
        out[...] = hidden[k * rows : (k + 1) * rows]


def down_kernel(n_pair, n_wide, n_weights, first, last, ins, outs, room):
    before = ins[-1:] if not first else []
    ins = ins[: len(ins) - len(before)]
    parts, weights = ins[:-n_weights], ins[-n_weights:]
    (hidden,) = room
    c = lax.axis_index("pair")
    rows = parts[0].shape[0]
    pieces = len(parts) // n_pair
    for at, part in enumerate(parts):
        k, piece = divmod(at, pieces)
        block = lax.rem(c + n_pair - k, n_pair) * pieces + piece
        hidden[pl.ds(pl.multiple_of(block * rows, 16), rows), :] = part[...]
    width = weights[0].shape[1]
    tile = tile_of(width)

    @pl.loop(0, width // tile)
    def _(step):
        at = pl.ds(pl.multiple_of(step * tile, tile), tile)
        total, start = 0, 0
        for weight in weights:
            deep = slice(start, start + weight.shape[0])
            total += jnp.dot(hidden[:, deep], weight[:, at], preferred_element_type=F32)
            start += weight.shape[0]
        if before:
            total += before[0][:, at]
        if last:
            share = total.shape[0] // n_wide
            for k in range(n_wide):
                place = (k if n_wide & (n_wide - 1) == 0 else (n_wide - k) % n_wide) * share
                outs[k][:, at] = total[place : place + share].astype(outs[k].dtype)
        else:
            outs[0][:, at] = total


def shards(sizes, tokens, gate_weight, up_weight, down_weight):
    n_seq, n_wide, n_pair = sizes["seq"], sizes["wide"], sizes["pair"]

    def send(value, axis, k):
        n = sizes[axis]
        paired = axis == "wide" and n & (n - 1) == 0
        return lax.ppermute(value, axis, [(i, i ^ k if paired else (i + k) % n) for i in range(n)])

    share, depth = tokens.shape
    rows = share * n_wide
    features = down_weight.shape[1]
    half = rows // n_pair
    loads = cuts(gate_weight.shape[1], GATE)
    chunks = cuts(down_weight.shape[0], DOWN)
    n = len(chunks)
    size = tokens.dtype.itemsize

    def bytes_of(fetch):
        return sum(size * f[3] * f[0].shape[1 - f[1]] for f in fetch)

    unit = gate_weight.shape[1] // sum(GATE)

    def gate_of(j):
        return [(gate_weight, 1, *loads[j])]

    def down_of(name):
        return [(down_weight, 0, start * unit, count * unit) for start, count in DOWN_LOADS[name]]

    def keep(name, fetched):
        for (start, _), array in zip(DOWN_LOADS[name], fetched):
            down[start * unit] = array

    order = []

    def project(blocks, weights, chunks, fetch, after=()):
        width, n = sum(width for _, width in chunks), len(chunks)
        outs, fetched = call(
            order,
            functools.partial(pair_part_kernel, n_pair, chunks, len(weights)),
            [*blocks, *weights],
            [pltpu.VMEM((half, width), F32)]
            + [pltpu.VMEM((half, wide), PAIR_TYPE) for _, wide in chunks] * (n_pair - 1)
            + [pltpu.VMEM((rows, depth), BF16)] * (len(blocks) > 1),
            fetch,
            [pltpu.VMEM((rows, tile_of(width)), F32)],
            COST * 2 * rows * depth * width,
            COST * 2 * bytes_of(fetch),
            after,
        )
        got = [send(outs[1 + (k - 1) * n + j], "pair", k) for k in range(1, n_pair) for j in range(n)]
        return (outs[0], *got), outs[-1], fetched

    def pair_sum(parts, chunks, pieces, after=()):
        outs = call(
            order, functools.partial(pair_sum_kernel, chunks), parts,
            [pltpu.VMEM((half, width), kind) for kind in (F32, BF16) for _, width in pieces],
            [], [], 0, COST * 8 * parts[0].size, after,
        )[0]
        sums = []
        for own, away in zip(outs[: len(pieces)], outs[len(pieces) :]):
            sums.append([own] + [send(away, "seq", k) for k in range(1, n_seq)])
        return sums

    def pair_join(groups):
        widths = [width for _, inner in groups for _, width in inner]
        outs = call(
            order, functools.partial(pair_join_kernel, [len(inner) for _, inner in groups]),
            [part for parts, _ in groups for part in parts],
            [pltpu.VMEM((half, width), kind) for kind in (F32, BF16) for width in widths],
            [], [], 0, COST * 8 * half * sum(widths),
        )[0]
        sums = []
        for own, away in zip(outs[: len(widths)], outs[len(widths) :]):
            sums.append([own] + [send(away, "seq", k) for k in range(1, n_seq)])
        return sums

    def activate(ups, gates, start, width):
        hidden, _ = call(
            order, functools.partial(activate_kernel, start), [*ups, *gates],
            [pltpu.VMEM((half // SPLIT, width), BF16)] * SPLIT, [], [], 0, COST * 8 * half * width,
        )
        got = [send(piece, "pair", k) for k in range(1, n_pair) for piece in hidden]
        return [*hidden, *got]

    def load(array, fetch, traffic, after=()):
        (array,), fetched = call(
            order, load_kernel, [array], [pltpu.VMEM(array.shape, BF16)], fetch, [], 0, traffic, after
        )
        return array, fetched

    def multiply_down(j, parts, total):
        first, last = j == 0, j == n - 1
        start, width = chunks[j]
        weights = [down[at] for at in sorted(down) if start <= at < start + width]
        if last:
            outs = [pltpu.VMEM((share, features), F32)]
            outs += [pltpu.VMEM((share, features), BF16)] * (n_wide - 1)
        else:
            outs = [pltpu.VMEM((rows, features), F32)]
        name = ("first", "second", "")[min(j, 2)]
        fetch = down_of(name) if n > 1 and name else []
        total, more = call(
            order,
            functools.partial(down_kernel, n_pair, n_wide, len(weights), first, last),
            [*parts, *weights, *total],
            outs,
            fetch,
            [pltpu.VMEM((rows, width), BF16)],
            COST * 2 * rows * width * features,
            COST * 2 * bytes_of(fetch),
        )
        if fetch:
            keep(name, more)
        return total

    _, (tokens, *early) = call(
        order, load_kernel, [], [], [(tokens, 0, 0, share), (down_weight, 0, 0, share)], [],
        0, 2 * up_weight.size * size,
    )
    blocks = [tokens] + [send(tokens, "wide", k) for k in range(1, n_wide)]
    up = pltpu.with_memory_space_constraint(up_weight, pltpu.VMEM)
    columns = gate_weight.shape[1]
    down, whole = {}, [(0, columns)]
    if n == 1:
        ups, x, gate = project(blocks, [up], whole, gate_of(0), early)
        (ups,) = pair_sum(ups, whole, whole)
        parts, _, (down[0],) = project([x], gate, chunks, [(down_weight, 0, 0, columns)])
        sums = pair_sum(parts, chunks, chunks)
    else:
        ups, x, first = project(blocks, [up], whole, gate_of(0), early)
        x, more = load(x, down_of("wait"), COST * 2 * bytes_of(down_of("wait")))
        keep("wait", more)
        (ups,) = pair_sum(ups, whole, whole)
        edge = loads[1][0]
        inner = [chunk for chunk in chunks if chunk[0] < edge]
        parts, _, (second, *more) = project([x], first, inner, gate_of(1) + down_of("gate"))
        keep("gate", more)
        outer = [(start - edge, width) for start, width in chunks if start >= edge]
        others, _, _ = project([x], [second], outer, [])
        sums = pair_sum(parts, inner, inner) + pair_sum(others, outer, outer)
        _, more = load(x, down_of("late"), 0)
        keep("late", more)
    load(x, [], 0, ups[1:])
    hiddens = [activate(ups, sums[j], *chunks[j]) for j in range(min(n, 2))]
    total = []
    for j in range(n):
        if j and j + 1 < n:
            hiddens.append(activate(ups, sums[j + 1], *chunks[j + 1]))
        total = multiply_down(j, hiddens[j], total)

    result = total[0]
    for k in reversed(range(1, n_wide)):
        result = result + send(total[k], "wide", k).astype(F32)
    return result.astype(BF16)


def solution(mesh):
    return jax.shard_map(
        functools.partial(shards, dict(mesh.shape)),
        mesh=mesh,
        in_specs=(
            P(("parts", "wide"), ("seq", "pair")),
            P(("seq", "pair"), "wide"),
            P(("seq", "pair"), "wide"),
            P("wide", ("seq", "pair")),
        ),
        out_specs=P(("parts", "wide"), ("seq", "pair")),
        check_vma=False,
    )
```

```python
import functools

import jax
import jax.numpy as jnp
from jax import lax
from jax.experimental import pallas as pl
from jax.experimental.pallas import tpu as pltpu
from jax.sharding import PartitionSpec as P

BF16, F32 = jnp.bfloat16, jnp.float32
TILE = 512
GATE = (9, 4)
DOWN = (5, 4, 4)
DOWN_LOADS = dict(wait=((0, 1),), gate=((1, 1),), late=((2, 3), (5, 4)), first=((9, 2),), second=((11, 2),))
PAIR_TYPE = BF16
COST = 1
SPLIT = 2


def on_chip():
    return pl.BlockSpec(memory_space=pltpu.VMEM)


def in_place():
    return pl.BlockSpec(memory_space=pl.ANY)


def cuts(columns, shares):
    if columns % (TILE * sum(shares)):
        return [(0, columns)]
    unit = columns // sum(shares)
    chunks, start = [], 0
    for share in shares:
        chunks.append((start, share * unit))
        start += share * unit
    return chunks


def tile_of(width):
    return TILE if width % TILE == 0 else width


def copies(fetch, sources, targets, sems):
    made = []
    for at, ((axis, start, size), source, target) in enumerate(zip(fetch, sources, targets)):
        view = source.at[:, pl.ds(start, size)] if axis else source.at[pl.ds(start, size), :]
        made.append(pltpu.make_async_copy(view, target, sems.at[at]))
    return made


def call(order, body, operands, outs, fetch, scratch, flops, traffic, after=()):
    fetched = []
    for array, axis, start, size in fetch:
        shape = (array.shape[0], size) if axis else (size, array.shape[1])
        fetched.append(pltpu.VMEM(shape, array.dtype))
    n_in = len(operands)
    after = [*after, *order[-1:]]

    def kernel(*refs):
        ins, rest = refs[:n_in], refs[n_in + len(after) :]
        sources, rest = rest[: len(fetch)], rest[len(fetch) :]
        results, rest = rest[: len(outs)], rest[len(outs) :]
        targets, (*room, sems) = rest[: len(fetch)], rest[len(fetch) :]
        made = copies([f[1:] for f in fetch], sources, targets, sems)
        for copy in made:
            copy.start()
        body(ins, results, room)
        for copy in made:
            copy.wait()

    out = pl.pallas_call(
        kernel,
        out_shape=tuple(outs) + tuple(fetched),
        in_specs=[on_chip()] * n_in + [in_place()] * (len(after) + len(fetch)),
        out_specs=tuple([on_chip()] * (len(outs) + len(fetch))),
        scratch_shapes=list(scratch) + [pltpu.SemaphoreType.DMA((max(len(fetch), 1),))],
        compiler_params=pltpu.CompilerParams(vmem_limit_bytes=4 * 2**20),
        cost_estimate=pl.CostEstimate(flops=int(flops), bytes_accessed=int(traffic), transcendentals=0),
    )(*operands, *after, *[pltpu.with_memory_space_constraint(f[0], pltpu.HBM) for f in fetch])
    order.append(min(out, key=lambda array: array.size))
    return out[: len(outs)], out[len(outs) :]


def load_kernel(ins, outs, room):
    for source, target in zip(ins, outs):
        target[...] = source[...]


def pair_part_kernel(n_pair, chunks, n_weights, ins, outs, room):
    blocks, weights = ins[:-n_weights], ins[-n_weights:]
    n = len(chunks)
    keep, sends = outs[0], outs[1 : 1 + n * (n_pair - 1)]
    x = blocks[0]
    if len(outs) > 1 + len(sends):
        x = outs[-1]
        share = blocks[0].shape[0]
        for k, block in enumerate(blocks):
            x[k * share : (k + 1) * share, :] = block[...]
    (res,) = room
    me = lax.axis_index("pair")
    rows = keep.shape[0]
    start = 0
    for weight in weights:
        for j, (first, width) in enumerate(chunks):
            low, high = max(start, first), min(start + weight.shape[1], first + width)
            if low >= high:
                continue
            tile = tile_of(high - low)

            @pl.loop(0, (high - low) // tile)
            def _(step, weight=weight, tile=tile, j=j, low=low, first=first, start=start):
                def at(offset):
                    return pl.ds(pl.multiple_of(offset + step * tile, tile), tile)

                res[...] = jnp.dot(x[...], weight[:, at(low - start)], preferred_element_type=F32)
                for k in range(n_pair):
                    block = pl.ds(pl.multiple_of(lax.rem(me + k, n_pair) * rows, 16), rows)
                    target, offset = (sends[(k - 1) * n + j], low - first) if k else (keep, low)
                    target[:, at(offset)] = res[block, :].astype(target.dtype)

        start += weight.shape[1]


def pair_sum_kernel(chunks, pieces, ins, outs, room):
    keep, got = ins[0], ins[1:]
    n, half = len(chunks), len(pieces)
    for j, (first, wide) in enumerate(chunks):
        for k, (start, width) in enumerate(pieces):
            low, high = max(first, start), min(first + wide, start + width)
            if low >= high:
                continue
            total = keep[:, low:high]
            for part in got[j::n]:
                total += part[:, low - first : high - first].astype(F32)
            for out in (outs[k], outs[half + k]):
                out[:, low - start : high - start] = total.astype(out.dtype)


def activate_kernel(start, ins, outs, room):
    at = slice(start, start + outs[0].shape[1])
    half = len(ins) // 2
    up = sum(part[:, at].astype(F32) for part in ins[:half])
    gate = sum(part[...].astype(F32) for part in ins[half:])
    hidden = (gate / (1.0 + jnp.exp(-gate)) * up).astype(BF16)
    rows = outs[0].shape[0]
    for k, out in enumerate(outs):
        out[...] = hidden[k * rows : (k + 1) * rows]


def down_kernel(n_pair, n_wide, n_weights, first, last, ins, outs, room):
    before = ins[-1:] if not first else []
    ins = ins[: len(ins) - len(before)]
    parts, weights = ins[:-n_weights], ins[-n_weights:]
    (hidden,) = room
    c = lax.axis_index("pair")
    rows = parts[0].shape[0]
    pieces = len(parts) // n_pair
    for at, part in enumerate(parts):
        k, piece = divmod(at, pieces)
        block = lax.rem(c + n_pair - k, n_pair) * pieces + piece
        hidden[pl.ds(pl.multiple_of(block * rows, 16), rows), :] = part[...]
    width = weights[0].shape[1]
    tile = tile_of(width)

    @pl.loop(0, width // tile)
    def _(step):
        at = pl.ds(pl.multiple_of(step * tile, tile), tile)
        total, start = 0, 0
        for weight in weights:
            deep = slice(start, start + weight.shape[0])
            total += jnp.dot(hidden[:, deep], weight[:, at], preferred_element_type=F32)
            start += weight.shape[0]
        if before:
            total += before[0][:, at]
        if last:
            share = total.shape[0] // n_wide
            for k in range(n_wide):
                place = (k if n_wide & (n_wide - 1) == 0 else (n_wide - k) % n_wide) * share
                outs[k][:, at] = total[place : place + share].astype(outs[k].dtype)
        else:
            outs[0][:, at] = total


def shards(sizes, tokens, gate_weight, up_weight, down_weight):
    n_seq, n_wide, n_pair = sizes["seq"], sizes["wide"], sizes["pair"]

    def send(value, axis, k):
        n = sizes[axis]
        paired = axis == "wide" and n & (n - 1) == 0
        return lax.ppermute(value, axis, [(i, i ^ k if paired else (i + k) % n) for i in range(n)])

    share, depth = tokens.shape
    rows = share * n_wide
    features = down_weight.shape[1]
    half = rows // n_pair
    loads = cuts(gate_weight.shape[1], GATE)
    chunks = cuts(down_weight.shape[0], DOWN)
    n = len(chunks)
    size = tokens.dtype.itemsize

    def bytes_of(fetch):
        return sum(size * f[3] * f[0].shape[1 - f[1]] for f in fetch)

    unit = gate_weight.shape[1] // sum(GATE)

    def gate_of(j):
        return [(gate_weight, 1, *loads[j])]

    def down_of(name):
        return [(down_weight, 0, start * unit, count * unit) for start, count in DOWN_LOADS[name]]

    def keep(name, fetched):
        for (start, _), array in zip(DOWN_LOADS[name], fetched):
            down[start * unit] = array

    order = []

    def project(blocks, weights, chunks, fetch, after=()):
        width, n = sum(width for _, width in chunks), len(chunks)
        outs, fetched = call(
            order,
            functools.partial(pair_part_kernel, n_pair, chunks, len(weights)),
            [*blocks, *weights],
            [pltpu.VMEM((half, width), F32)]
            + [pltpu.VMEM((half, wide), PAIR_TYPE) for _, wide in chunks] * (n_pair - 1)
            + [pltpu.VMEM((rows, depth), BF16)] * (len(blocks) > 1),
            fetch,
            [pltpu.VMEM((rows, tile_of(width)), F32)],
            COST * 2 * rows * depth * width,
            COST * 2 * bytes_of(fetch),
            after,
        )
        got = [send(outs[1 + (k - 1) * n + j], "pair", k) for k in range(1, n_pair) for j in range(n)]
        return (outs[0], *got), outs[-1], fetched

    def pair_sum(parts, chunks, pieces, after=()):
        outs = call(
            order, functools.partial(pair_sum_kernel, chunks, pieces), parts,
            [pltpu.VMEM((half, width), kind) for kind in (F32, BF16) for _, width in pieces],
            [], [], 0, COST * 8 * parts[0].size, after,
        )[0]
        sums = []
        for own, away in zip(outs[: len(pieces)], outs[len(pieces) :]):
            sums.append([own] + [send(away, "seq", k) for k in range(1, n_seq)])
        return sums

    def activate(ups, gates, start, width):
        split = SPLIT if start == 0 else 1
        hidden, _ = call(
            order, functools.partial(activate_kernel, start), [*ups, *gates],
            [pltpu.VMEM((half // split, width), BF16)] * split, [], [], 0, COST * 8 * half * width,
        )
        got = [send(piece, "pair", k) for k in range(1, n_pair) for piece in hidden]
        return [*hidden, *got]

    def load(array, fetch, traffic, after=()):
        (array,), fetched = call(
            order, load_kernel, [array], [pltpu.VMEM(array.shape, BF16)], fetch, [], 0, traffic, after
        )
        return array, fetched

    def multiply_down(j, parts, total):
        first, last = j == 0, j == n - 1
        start, width = chunks[j]
        weights = [down[at] for at in sorted(down) if start <= at < start + width]
        if last:
            outs = [pltpu.VMEM((share, features), F32)]
            outs += [pltpu.VMEM((share, features), BF16)] * (n_wide - 1)
        else:
            outs = [pltpu.VMEM((rows, features), F32)]
        name = ("first", "second", "")[min(j, 2)]
        fetch = down_of(name) if n > 1 and name else []
        total, more = call(
            order,
            functools.partial(down_kernel, n_pair, n_wide, len(weights), first, last),
            [*parts, *weights, *total],
            outs,
            fetch,
            [pltpu.VMEM((rows, width), BF16)],
            COST * 2 * rows * width * features,
            COST * 2 * bytes_of(fetch),
        )
        if fetch:
            keep(name, more)
        return total

    _, (tokens, *early) = call(
        order, load_kernel, [], [], [(tokens, 0, 0, share), (down_weight, 0, 0, share)], [],
        0, 2 * up_weight.size * size,
    )
    blocks = [tokens] + [send(tokens, "wide", k) for k in range(1, n_wide)]
    up = pltpu.with_memory_space_constraint(up_weight, pltpu.VMEM)
    columns = gate_weight.shape[1]
    down, whole = {}, [(0, columns)]
    if n == 1:
        ups, x, gate = project(blocks, [up], whole, gate_of(0), early)
        (ups,) = pair_sum(ups, whole, whole)
        parts, _, (down[0],) = project([x], gate, chunks, [(down_weight, 0, 0, columns)])
        sums = pair_sum(parts, chunks, chunks)
    else:
        ups, x, first = project(blocks, [up], whole, gate_of(0), early)
        x, more = load(x, down_of("wait"), COST * 2 * bytes_of(down_of("wait")))
        keep("wait", more)
        (ups,) = pair_sum(ups, whole, whole)
        edge = loads[1][0]
        inner = [chunk for chunk in chunks if chunk[0] < edge]
        parts, _, (second, *more) = project([x], first, inner, gate_of(1) + down_of("gate"))
        keep("gate", more)
        outer = [(start - edge, width) for start, width in chunks if start >= edge]
        others, _, _ = project([x], [second], outer, [])
        sums = pair_sum(parts, inner, inner) + pair_sum(others, outer, outer)
        _, more = load(x, down_of("late"), 0)
        keep("late", more)
    load(x, [], 0, ups[1:])
    hiddens = [activate(ups, sums[j], *chunks[j]) for j in range(min(n, 2))]
    total = []
    for j in range(n):
        if j and j + 1 < n:
            hiddens.append(activate(ups, sums[j + 1], *chunks[j + 1]))
        total = multiply_down(j, hiddens[j], total)

    result = total[0]
    for k in reversed(range(1, n_wide)):
        result = result + send(total[k], "wide", k).astype(F32)
    return result.astype(BF16)


def solution(mesh):
    return jax.shard_map(
        functools.partial(shards, dict(mesh.shape)),
        mesh=mesh,
        in_specs=(
            P(("parts", "wide"), ("seq", "pair")),
            P(("seq", "pair"), "wide"),
            P(("seq", "pair"), "wide"),
            P("wide", ("seq", "pair")),
        ),
        out_specs=P(("parts", "wide"), ("seq", "pair")),
        check_vma=False,
    )
```

```python
import functools

import jax
import jax.numpy as jnp
from jax import lax
from jax.experimental import pallas as pl
from jax.experimental.pallas import tpu as pltpu
from jax.sharding import PartitionSpec as P

BF16, F32 = jnp.bfloat16, jnp.float32
TILE = 512
GATE = (8, 5)
DOWN = (4, 4, 5)
DOWN_LOADS = dict(wait=((0, 1),), rest=((1, 2),), late=((3, 1), (4, 4), (8, 1)), first=((9, 2),), second=((11, 2),))
PAIR_TYPE = BF16
COST = 1
SPLIT = 2


def on_chip():
    return pl.BlockSpec(memory_space=pltpu.VMEM)


def in_place():
    return pl.BlockSpec(memory_space=pl.ANY)


def cuts(columns, shares):
    if columns % (TILE * sum(shares)):
        return [(0, columns)]
    unit = columns // sum(shares)
    chunks, start = [], 0
    for share in shares:
        chunks.append((start, share * unit))
        start += share * unit
    return chunks


def tile_of(width):
    return TILE if width % TILE == 0 else width


def copies(fetch, sources, targets, sems):
    made = []
    for at, ((axis, start, size), source, target) in enumerate(zip(fetch, sources, targets)):
        view = source.at[:, pl.ds(start, size)] if axis else source.at[pl.ds(start, size), :]
        made.append(pltpu.make_async_copy(view, target, sems.at[at]))
    return made


def call(order, body, operands, outs, fetch, scratch, flops, traffic, after=()):
    fetched = []
    for array, axis, start, size in fetch:
        shape = (array.shape[0], size) if axis else (size, array.shape[1])
        fetched.append(pltpu.VMEM(shape, array.dtype))
    n_in = len(operands)
    after = [*after, *order[-1:]]

    def kernel(*refs):
        ins, rest = refs[:n_in], refs[n_in + len(after) :]
        sources, rest = rest[: len(fetch)], rest[len(fetch) :]
        results, rest = rest[: len(outs)], rest[len(outs) :]
        targets, (*room, sems) = rest[: len(fetch)], rest[len(fetch) :]
        made = copies([f[1:] for f in fetch], sources, targets, sems)
        for copy in made:
            copy.start()
        body(ins, results, room)
        for copy in made:
            copy.wait()

    out = pl.pallas_call(
        kernel,
        out_shape=tuple(outs) + tuple(fetched),
        in_specs=[on_chip()] * n_in + [in_place()] * (len(after) + len(fetch)),
        out_specs=tuple([on_chip()] * (len(outs) + len(fetch))),
        scratch_shapes=list(scratch) + [pltpu.SemaphoreType.DMA((max(len(fetch), 1),))],
        compiler_params=pltpu.CompilerParams(vmem_limit_bytes=4 * 2**20),
        cost_estimate=pl.CostEstimate(flops=int(flops), bytes_accessed=int(traffic), transcendentals=0),
    )(*operands, *after, *[pltpu.with_memory_space_constraint(f[0], pltpu.HBM) for f in fetch])
    order.append(min(out, key=lambda array: array.size))
    return out[: len(outs)], out[len(outs) :]


def load_kernel(ins, outs, room):
    for source, target in zip(ins, outs):
        target[...] = source[...]


def pair_part_kernel(n_pair, chunks, n_weights, ins, outs, room):
    blocks, weights = ins[:-n_weights], ins[-n_weights:]
    n = len(chunks)
    keep, sends = outs[0], outs[1 : 1 + n * (n_pair - 1)]
    x = blocks[0]
    if len(outs) > 1 + len(sends):
        x = outs[-1]
        share = blocks[0].shape[0]
        for k, block in enumerate(blocks):
            x[k * share : (k + 1) * share, :] = block[...]
    (res,) = room
    me = lax.axis_index("pair")
    rows = keep.shape[0]
    start = 0
    for weight in weights:
        for j, (first, width) in enumerate(chunks):
            low, high = max(start, first), min(start + weight.shape[1], first + width)
            if low >= high:
                continue
            tile = tile_of(high - low)

            @pl.loop(0, (high - low) // tile)
            def _(step, weight=weight, tile=tile, j=j, low=low, first=first, start=start):
                def at(offset):
                    return pl.ds(pl.multiple_of(offset + step * tile, tile), tile)

                res[...] = jnp.dot(x[...], weight[:, at(low - start)], preferred_element_type=F32)
                for k in range(n_pair):
                    block = pl.ds(pl.multiple_of(lax.rem(me + k, n_pair) * rows, 16), rows)
                    target, offset = (sends[(k - 1) * n + j], low - first) if k else (keep, low)
                    target[:, at(offset)] = res[block, :].astype(target.dtype)

        start += weight.shape[1]


def pair_sum_kernel(chunks, pieces, ins, outs, room):
    keep, got = ins[0], ins[1:]
    n, half = len(chunks), len(pieces)
    for j, (first, wide) in enumerate(chunks):
        for k, (start, width) in enumerate(pieces):
            low, high = max(first, start), min(first + wide, start + width)
            if low >= high:
                continue
            total = keep[:, low:high]
            for part in got[j::n]:
                total += part[:, low - first : high - first].astype(F32)
            for out in (outs[k], outs[half + k]):
                out[:, low - start : high - start] = total.astype(out.dtype)


def activate_kernel(start, ins, outs, room):
    at = slice(start, start + outs[0].shape[1])
    half = len(ins) // 2
    up = sum(part[:, at].astype(F32) for part in ins[:half])
    gate = sum(part[...].astype(F32) for part in ins[half:])
    hidden = (gate / (1.0 + jnp.exp(-gate)) * up).astype(BF16)
    rows = outs[0].shape[0]
    for k, out in enumerate(outs):
        out[...] = hidden[k * rows : (k + 1) * rows]


def down_kernel(n_pair, n_wide, n_weights, first, last, ins, outs, room):
    before = ins[-1:] if not first else []
    ins = ins[: len(ins) - len(before)]
    parts, weights = ins[:-n_weights], ins[-n_weights:]
    (hidden,) = room
    c = lax.axis_index("pair")
    rows = parts[0].shape[0]
    pieces = len(parts) // n_pair
    for at, part in enumerate(parts):
        k, piece = divmod(at, pieces)
        block = lax.rem(c + n_pair - k, n_pair) * pieces + piece
        hidden[pl.ds(pl.multiple_of(block * rows, 16), rows), :] = part[...]
    width = weights[0].shape[1]
    tile = tile_of(width)

    @pl.loop(0, width // tile)
    def _(step):
        at = pl.ds(pl.multiple_of(step * tile, tile), tile)
        total, start = 0, 0
        for weight in weights:
            deep = slice(start, start + weight.shape[0])
            total += jnp.dot(hidden[:, deep], weight[:, at], preferred_element_type=F32)
            start += weight.shape[0]
        if before:
            total += before[0][:, at]
        if last:
            share = total.shape[0] // n_wide
            for k in range(n_wide):
                place = (k if n_wide & (n_wide - 1) == 0 else (n_wide - k) % n_wide) * share
                outs[k][:, at] = total[place : place + share].astype(outs[k].dtype)
        else:
            outs[0][:, at] = total


def shards(sizes, tokens, gate_weight, up_weight, down_weight):
    n_seq, n_wide, n_pair = sizes["seq"], sizes["wide"], sizes["pair"]

    def send(value, axis, k):
        n = sizes[axis]
        paired = axis == "wide" and n & (n - 1) == 0
        return lax.ppermute(value, axis, [(i, i ^ k if paired else (i + k) % n) for i in range(n)])

    share, depth = tokens.shape
    rows = share * n_wide
    features = down_weight.shape[1]
    half = rows // n_pair
    loads = cuts(gate_weight.shape[1], GATE)
    chunks = cuts(down_weight.shape[0], DOWN)
    n = len(chunks)
    size = tokens.dtype.itemsize

    def bytes_of(fetch):
        return sum(size * f[3] * f[0].shape[1 - f[1]] for f in fetch)

    unit = gate_weight.shape[1] // sum(GATE)

    def gate_of(j):
        return [(gate_weight, 1, *loads[j])]

    def down_of(name):
        return [(down_weight, 0, start * unit, count * unit) for start, count in DOWN_LOADS[name]]

    def keep(name, fetched):
        for (start, _), array in zip(DOWN_LOADS[name], fetched):
            down[start * unit] = array

    order = []

    def project(blocks, weights, chunks, fetch, after=()):
        width, n = sum(width for _, width in chunks), len(chunks)
        outs, fetched = call(
            order,
            functools.partial(pair_part_kernel, n_pair, chunks, len(weights)),
            [*blocks, *weights],
            [pltpu.VMEM((half, width), F32)]
            + [pltpu.VMEM((half, wide), PAIR_TYPE) for _, wide in chunks] * (n_pair - 1)
            + [pltpu.VMEM((rows, depth), BF16)] * (len(blocks) > 1),
            fetch,
            [pltpu.VMEM((rows, tile_of(width)), F32)],
            COST * 2 * rows * depth * width,
            COST * 2 * bytes_of(fetch),
            after,
        )
        got = [send(outs[1 + (k - 1) * n + j], "pair", k) for k in range(1, n_pair) for j in range(n)]
        return (outs[0], *got), outs[-1], fetched

    def pair_sum(parts, chunks, pieces, after=()):
        outs = call(
            order, functools.partial(pair_sum_kernel, chunks, pieces), parts,
            [pltpu.VMEM((half, width), kind) for kind in (F32, BF16) for _, width in pieces],
            [], [], 0, COST * 8 * parts[0].size, after,
        )[0]
        sums = []
        for own, away in zip(outs[: len(pieces)], outs[len(pieces) :]):
            sums.append([own] + [send(away, "seq", k) for k in range(1, n_seq)])
        return sums

    def activate(ups, gates, start, width):
        split = SPLIT if start == 0 else 1
        hidden, _ = call(
            order, functools.partial(activate_kernel, start), [*ups, *gates],
            [pltpu.VMEM((half // split, width), BF16)] * split, [], [], 0, COST * 8 * half * width,
        )
        got = [send(piece, "pair", k) for k in range(1, n_pair) for piece in hidden]
        return [*hidden, *got]

    def load(array, fetch, traffic, after=()):
        (array,), fetched = call(
            order, load_kernel, [array], [pltpu.VMEM(array.shape, BF16)], fetch, [], 0, traffic, after
        )
        return array, fetched

    def multiply_down(j, parts, total):
        first, last = j == 0, j == n - 1
        start, width = chunks[j]
        weights = [down[at] for at in sorted(down) if start <= at < start + width]
        if last:
            outs = [pltpu.VMEM((share, features), F32)]
            outs += [pltpu.VMEM((share, features), BF16)] * (n_wide - 1)
        else:
            outs = [pltpu.VMEM((rows, features), F32)]
        name = ("first", "second", "")[min(j, 2)]
        fetch = down_of(name) if n > 1 and name else []
        total, more = call(
            order,
            functools.partial(down_kernel, n_pair, n_wide, len(weights), first, last),
            [*parts, *weights, *total],
            outs,
            fetch,
            [pltpu.VMEM((rows, width), BF16)],
            COST * 2 * rows * width * features,
            COST * 2 * bytes_of(fetch),
        )
        if fetch:
            keep(name, more)
        return total

    _, (tokens, *early) = call(
        order, load_kernel, [], [], [(tokens, 0, 0, share), (down_weight, 0, 0, share)], [],
        0, 2 * up_weight.size * size,
    )
    blocks = [tokens] + [send(tokens, "wide", k) for k in range(1, n_wide)]
    up = pltpu.with_memory_space_constraint(up_weight, pltpu.VMEM)
    columns = gate_weight.shape[1]
    down, whole = {}, [(0, columns)]
    if n == 1:
        ups, x, gate = project(blocks, [up], whole, gate_of(0), early)
        (ups,) = pair_sum(ups, whole, whole)
        parts, _, (down[0],) = project([x], gate, chunks, [(down_weight, 0, 0, columns)])
        sums = pair_sum(parts, chunks, chunks)
    else:
        ups, x, first = project(blocks, [up], whole, gate_of(0), early)
        x, more = load(x, down_of("wait"), COST * 2 * bytes_of(down_of("wait")))
        keep("wait", more)
        (ups,) = pair_sum(ups, whole, whole)
        edge = loads[1][0]
        inner = [chunk for chunk in chunks if chunk[0] < edge]
        parts, _, (second,) = project([x], first, inner, gate_of(1))
        outer = [(start - edge, width) for start, width in chunks if start >= edge]
        others, _, more = project([x], [second], outer, down_of("rest"))
        keep("rest", more)
        sums = pair_sum(parts, inner, inner) + pair_sum(others, outer, outer)
        _, more = load(x, down_of("late"), 0)
        keep("late", more)
    load(x, [], 0, ups[1:])
    hiddens = [activate(ups, sums[j], *chunks[j]) for j in range(min(n, 2))]
    total = []
    for j in range(n):
        if j and j + 1 < n:
            hiddens.append(activate(ups, sums[j + 1], *chunks[j + 1]))
        total = multiply_down(j, hiddens[j], total)

    result = total[0]
    for k in reversed(range(1, n_wide)):
        result = result + send(total[k], "wide", k).astype(F32)
    return result.astype(BF16)


def solution(mesh):
    return jax.shard_map(
        functools.partial(shards, dict(mesh.shape)),
        mesh=mesh,
        in_specs=(
            P(("parts", "wide"), ("seq", "pair")),
            P(("seq", "pair"), "wide"),
            P(("seq", "pair"), "wide"),
            P("wide", ("seq", "pair")),
        ),
        out_specs=P(("parts", "wide"), ("seq", "pair")),
        check_vma=False,
    )
```

```python
import functools

import jax
import jax.numpy as jnp
from jax import lax
from jax.experimental import pallas as pl
from jax.experimental.pallas import tpu as pltpu
from jax.sharding import PartitionSpec as P

BF16, F32 = jnp.bfloat16, jnp.float32
TILE = 512
GATE = (8, 5)
DOWN = (4, 4, 5)
DOWN_LOADS = dict(wait=((0, 1),), rest=((1, 2),), late=((3, 1), (4, 4), (8, 1)), first=((9, 2),), second=((11, 2),))
PAIR_TYPE = BF16
COST = 1
SPLIT = 2


def on_chip():
    return pl.BlockSpec(memory_space=pltpu.VMEM)


def in_place():
    return pl.BlockSpec(memory_space=pl.ANY)


def cuts(columns, shares):
    if columns % (TILE * sum(shares)):
        return [(0, columns)]
    unit = columns // sum(shares)
    chunks, start = [], 0
    for share in shares:
        chunks.append((start, share * unit))
        start += share * unit
    return chunks


def tile_of(width):
    return TILE if width % TILE == 0 else width


def copies(fetch, sources, targets, sems):
    made = []
    for at, ((axis, start, size), source, target) in enumerate(zip(fetch, sources, targets)):
        view = source.at[:, pl.ds(start, size)] if axis else source.at[pl.ds(start, size), :]
        made.append(pltpu.make_async_copy(view, target, sems.at[at]))
    return made


def call(order, body, operands, outs, fetch, scratch, flops, traffic, after=()):
    fetched = []
    for array, axis, start, size in fetch:
        shape = (array.shape[0], size) if axis else (size, array.shape[1])
        fetched.append(pltpu.VMEM(shape, array.dtype))
    n_in = len(operands)
    after = [*after, *order[-1:]]

    def kernel(*refs):
        ins, rest = refs[:n_in], refs[n_in + len(after) :]
        sources, rest = rest[: len(fetch)], rest[len(fetch) :]
        results, rest = rest[: len(outs)], rest[len(outs) :]
        targets, (*room, sems) = rest[: len(fetch)], rest[len(fetch) :]
        made = copies([f[1:] for f in fetch], sources, targets, sems)
        for copy in made:
            copy.start()
        body(ins, results, room)
        for copy in made:
            copy.wait()

    out = pl.pallas_call(
        kernel,
        out_shape=tuple(outs) + tuple(fetched),
        in_specs=[on_chip()] * n_in + [in_place()] * (len(after) + len(fetch)),
        out_specs=tuple([on_chip()] * (len(outs) + len(fetch))),
        scratch_shapes=list(scratch) + [pltpu.SemaphoreType.DMA((max(len(fetch), 1),))],
        compiler_params=pltpu.CompilerParams(vmem_limit_bytes=4 * 2**20),
        cost_estimate=pl.CostEstimate(flops=int(flops), bytes_accessed=int(traffic), transcendentals=0),
    )(*operands, *after, *[pltpu.with_memory_space_constraint(f[0], pltpu.HBM) for f in fetch])
    order.append(min(out, key=lambda array: array.size))
    return out[: len(outs)], out[len(outs) :]


def load_kernel(ins, outs, room):
    for source, target in zip(ins, outs):
        target[...] = source[...]


def pair_part_kernel(n_pair, chunks, n_weights, ins, outs, room):
    blocks, weights = ins[:-n_weights], ins[-n_weights:]
    n = len(chunks)
    keep, sends = outs[0], outs[1 : 1 + n * (n_pair - 1)]
    x = blocks[0]
    if len(outs) > 1 + len(sends):
        x = outs[-1]
        share = blocks[0].shape[0]
        for k, block in enumerate(blocks):
            x[k * share : (k + 1) * share, :] = block[...]
    (res,) = room
    me = lax.axis_index("pair")
    rows = keep.shape[0]
    start = 0
    for weight in weights:
        for j, (first, width) in enumerate(chunks):
            low, high = max(start, first), min(start + weight.shape[1], first + width)
            if low >= high:
                continue
            tile = tile_of(high - low)

            @pl.loop(0, (high - low) // tile)
            def _(step, weight=weight, tile=tile, j=j, low=low, first=first, start=start):
                def at(offset):
                    return pl.ds(pl.multiple_of(offset + step * tile, tile), tile)

                res[...] = jnp.dot(x[...], weight[:, at(low - start)], preferred_element_type=F32)
                for k in range(n_pair):
                    block = pl.ds(pl.multiple_of(lax.rem(me + k, n_pair) * rows, 16), rows)
                    target, offset = (sends[(k - 1) * n + j], low - first) if k else (keep, low)
                    target[:, at(offset)] = res[block, :].astype(target.dtype)

        start += weight.shape[1]


def pair_sum_kernel(chunks, pieces, ins, outs, room):
    keep, got = ins[0], ins[1:]
    n, half = len(chunks), len(pieces)
    for j, (first, wide) in enumerate(chunks):
        for k, (start, width) in enumerate(pieces):
            low, high = max(first, start), min(first + wide, start + width)
            if low >= high:
                continue
            total = keep[:, low:high]
            for part in got[j::n]:
                total += part[:, low - first : high - first].astype(F32)
            for out in (outs[k], outs[half + k]):
                out[:, low - start : high - start] = total.astype(out.dtype)


def activate_kernel(start, ins, outs, room):
    at = slice(start, start + outs[0].shape[1])
    half = len(ins) // 2
    up = sum(part[:, at].astype(F32) for part in ins[:half])
    gate = sum(part[...].astype(F32) for part in ins[half:])
    hidden = (gate / (1.0 + jnp.exp(-gate)) * up).astype(BF16)
    rows = outs[0].shape[0]
    for k, out in enumerate(outs):
        out[...] = hidden[k * rows : (k + 1) * rows]


def down_kernel(n_pair, n_wide, n_weights, first, last, ins, outs, room):
    before = ins[-1:] if not first else []
    ins = ins[: len(ins) - len(before)]
    parts, weights = ins[:-n_weights], ins[-n_weights:]
    (hidden,) = room
    c = lax.axis_index("pair")
    rows = parts[0].shape[0]
    pieces = len(parts) // n_pair
    for at, part in enumerate(parts):
        k, piece = divmod(at, pieces)
        block = lax.rem(c + n_pair - k, n_pair) * pieces + piece
        hidden[pl.ds(pl.multiple_of(block * rows, 16), rows), :] = part[...]
    width = weights[0].shape[1]
    tile = tile_of(width)

    @pl.loop(0, width // tile)
    def _(step):
        at = pl.ds(pl.multiple_of(step * tile, tile), tile)
        total, start = 0, 0
        for weight in weights:
            deep = slice(start, start + weight.shape[0])
            total += jnp.dot(hidden[:, deep], weight[:, at], preferred_element_type=F32)
            start += weight.shape[0]
        if before:
            total += before[0][:, at]
        if last:
            share = total.shape[0] // n_wide
            for k in range(n_wide):
                place = (k if n_wide & (n_wide - 1) == 0 else (n_wide - k) % n_wide) * share
                outs[k][:, at] = total[place : place + share].astype(outs[k].dtype)
        else:
            outs[0][:, at] = total


def shards(sizes, tokens, gate_weight, up_weight, down_weight):
    n_seq, n_wide, n_pair = sizes["seq"], sizes["wide"], sizes["pair"]

    def send(value, axis, k):
        n = sizes[axis]
        paired = axis == "wide" and n & (n - 1) == 0
        return lax.ppermute(value, axis, [(i, i ^ k if paired else (i + k) % n) for i in range(n)])

    share, depth = tokens.shape
    rows = share * n_wide
    features = down_weight.shape[1]
    half = rows // n_pair
    loads = cuts(gate_weight.shape[1], GATE)
    chunks = cuts(down_weight.shape[0], DOWN)
    n = len(chunks)
    size = tokens.dtype.itemsize

    def bytes_of(fetch):
        return sum(size * f[3] * f[0].shape[1 - f[1]] for f in fetch)

    unit = gate_weight.shape[1] // sum(GATE)

    def gate_of(j):
        return [(gate_weight, 1, *loads[j])]

    def down_of(name):
        return [(down_weight, 0, start * unit, count * unit) for start, count in DOWN_LOADS[name]]

    def keep(name, fetched):
        for (start, _), array in zip(DOWN_LOADS[name], fetched):
            down[start * unit] = array

    order = []

    def project(blocks, weights, chunks, fetch, after=()):
        width, n = sum(width for _, width in chunks), len(chunks)
        outs, fetched = call(
            order,
            functools.partial(pair_part_kernel, n_pair, chunks, len(weights)),
            [*blocks, *weights],
            [pltpu.VMEM((half, width), F32)]
            + [pltpu.VMEM((half, wide), PAIR_TYPE) for _, wide in chunks] * (n_pair - 1)
            + [pltpu.VMEM((rows, depth), BF16)] * (len(blocks) > 1),
            fetch,
            [pltpu.VMEM((rows, tile_of(width)), F32)],
            COST * 2 * rows * depth * width,
            COST * 2 * bytes_of(fetch),
            after,
        )
        got = [send(outs[1 + (k - 1) * n + j], "pair", k) for k in range(1, n_pair) for j in range(n)]
        return (outs[0], *got), outs[-1], fetched

    def pair_sum(parts, chunks, pieces, after=()):
        outs = call(
            order, functools.partial(pair_sum_kernel, chunks, pieces), parts,
            [pltpu.VMEM((half, width), kind) for kind in (F32, BF16) for _, width in pieces],
            [], [], 0, COST * 8 * parts[0].size, after,
        )[0]
        sums = []
        for own, away in zip(outs[: len(pieces)], outs[len(pieces) :]):
            sums.append([own] + [send(away, "seq", k) for k in range(1, n_seq)])
        return sums

    def activate(ups, gates, start, width):
        split = SPLIT if start == 0 else 1
        hidden, _ = call(
            order, functools.partial(activate_kernel, start), [*ups, *gates],
            [pltpu.VMEM((half // split, width), BF16)] * split, [], [], 0, COST * 8 * half * width,
        )
        got = [send(piece, "pair", k) for k in range(1, n_pair) for piece in hidden]
        return [*hidden, *got]

    def load(array, fetch, traffic, after=()):
        (array,), fetched = call(
            order, load_kernel, [array], [pltpu.VMEM(array.shape, BF16)], fetch, [], 0, traffic, after
        )
        return array, fetched

    def multiply_down(j, parts, total):
        first, last = j == 0, j == n - 1
        start, width = chunks[j]
        weights = [down[at] for at in sorted(down) if start <= at < start + width]
        if last:
            outs = [pltpu.VMEM((share, features), F32)]
            outs += [pltpu.VMEM((share, features), BF16)] * (n_wide - 1)
        else:
            outs = [pltpu.VMEM((rows, features), F32)]
        name = ("first", "second", "")[min(j, 2)]
        fetch = down_of(name) if n > 1 and name else []
        total, more = call(
            order,
            functools.partial(down_kernel, n_pair, n_wide, len(weights), first, last),
            [*parts, *weights, *total],
            outs,
            fetch,
            [pltpu.VMEM((rows, width), BF16)],
            COST * 2 * rows * width * features,
            COST * 2 * bytes_of(fetch),
        )
        if fetch:
            keep(name, more)
        return total

    _, (staged, *early) = call(
        order, load_kernel, [], [], [(tokens, 0, 0, share), (down_weight, 0, 0, share)], [],
        0, 2 * up_weight.size * size,
    )
    blocks = [staged] + [send(tokens if k > 1 else staged, "wide", k) for k in range(1, n_wide)]
    up = pltpu.with_memory_space_constraint(up_weight, pltpu.VMEM)
    columns = gate_weight.shape[1]
    down, whole = {}, [(0, columns)]
    if n == 1:
        ups, x, gate = project(blocks, [up], whole, gate_of(0), early)
        (ups,) = pair_sum(ups, whole, whole)
        parts, _, (down[0],) = project([x], gate, chunks, [(down_weight, 0, 0, columns)])
        sums = pair_sum(parts, chunks, chunks)
    else:
        ups, x, first = project(blocks, [up], whole, gate_of(0), early)
        x, more = load(x, down_of("wait"), COST * 2 * bytes_of(down_of("wait")))
        keep("wait", more)
        (ups,) = pair_sum(ups, whole, whole)
        edge = loads[1][0]
        inner = [chunk for chunk in chunks if chunk[0] < edge]
        parts, _, (second,) = project([x], first, inner, gate_of(1))
        outer = [(start - edge, width) for start, width in chunks if start >= edge]
        others, _, more = project([x], [second], outer, down_of("rest"))
        keep("rest", more)
        sums = pair_sum(parts, inner, inner) + pair_sum(others, outer, outer)
        _, more = load(x, down_of("late"), 0)
        keep("late", more)
    load(x, [], 0, ups[1:])
    hiddens = [activate(ups, sums[j], *chunks[j]) for j in range(min(n, 2))]
    total = []
    for j in range(n):
        if j and j + 1 < n:
            hiddens.append(activate(ups, sums[j + 1], *chunks[j + 1]))
        total = multiply_down(j, hiddens[j], total)

    result = total[0]
    for k in reversed(range(1, n_wide)):
        result = result + send(total[k], "wide", k).astype(F32)
    return result.astype(BF16)


def solution(mesh):
    return jax.shard_map(
        functools.partial(shards, dict(mesh.shape)),
        mesh=mesh,
        in_specs=(
            P(("parts", "wide"), ("seq", "pair")),
            P(("seq", "pair"), "wide"),
            P(("seq", "pair"), "wide"),
            P("wide", ("seq", "pair")),
        ),
        out_specs=P(("parts", "wide"), ("seq", "pair")),
        check_vma=False,
    )
```

```python
import functools

import jax
import jax.numpy as jnp
from jax import lax
from jax.experimental import pallas as pl
from jax.experimental.pallas import tpu as pltpu
from jax.sharding import PartitionSpec as P

BF16, F32 = jnp.bfloat16, jnp.float32
TILE = 512
GATE = (8, 5)
DOWN = (4, 4, 5)
DOWN_LOADS = dict(wait=((0, 1),), rest=((1, 2),), late=((3, 1), (4, 4), (8, 1)), first=((9, 2),), second=((11, 2),))
PAIR_TYPE = BF16
COST = 1
SPLIT = 2


def on_chip():
    return pl.BlockSpec(memory_space=pltpu.VMEM)


def in_place():
    return pl.BlockSpec(memory_space=pl.ANY)


def cuts(columns, shares):
    if columns % (TILE * sum(shares)):
        return [(0, columns)]
    unit = columns // sum(shares)
    chunks, start = [], 0
    for share in shares:
        chunks.append((start, share * unit))
        start += share * unit
    return chunks


def tile_of(width):
    return TILE if width % TILE == 0 else width


def copies(fetch, sources, targets, sems):
    made = []
    for at, ((axis, start, size), source, target) in enumerate(zip(fetch, sources, targets)):
        view = source.at[:, pl.ds(start, size)] if axis else source.at[pl.ds(start, size), :]
        made.append(pltpu.make_async_copy(view, target, sems.at[at]))
    return made


def call(order, body, operands, outs, fetch, scratch, flops, traffic, after=()):
    fetched = []
    for array, axis, start, size in fetch:
        shape = (array.shape[0], size) if axis else (size, array.shape[1])
        fetched.append(pltpu.VMEM(shape, array.dtype))
    n_in = len(operands)
    after = [*after, *order[-1:]]

    def kernel(*refs):
        ins, rest = refs[:n_in], refs[n_in + len(after) :]
        sources, rest = rest[: len(fetch)], rest[len(fetch) :]
        results, rest = rest[: len(outs)], rest[len(outs) :]
        targets, (*room, sems) = rest[: len(fetch)], rest[len(fetch) :]
        made = copies([f[1:] for f in fetch], sources, targets, sems)
        for copy in made:
            copy.start()
        body(ins, results, room)
        for copy in made:
            copy.wait()

    out = pl.pallas_call(
        kernel,
        out_shape=tuple(outs) + tuple(fetched),
        in_specs=[on_chip()] * n_in + [in_place()] * (len(after) + len(fetch)),
        out_specs=tuple([on_chip()] * (len(outs) + len(fetch))),
        scratch_shapes=list(scratch) + [pltpu.SemaphoreType.DMA((max(len(fetch), 1),))],
        compiler_params=pltpu.CompilerParams(vmem_limit_bytes=4 * 2**20),
        cost_estimate=pl.CostEstimate(flops=int(flops), bytes_accessed=int(traffic), transcendentals=0),
    )(*operands, *after, *[pltpu.with_memory_space_constraint(f[0], pltpu.HBM) for f in fetch])
    order.append(min(out, key=lambda array: array.size))
    return out[: len(outs)], out[len(outs) :]


def load_kernel(ins, outs, room):
    for source, target in zip(ins, outs):
        target[...] = source[...]


def pair_part_kernel(n_pair, chunks, n_weights, ins, outs, room):
    blocks, weights = ins[:-n_weights], ins[-n_weights:]
    n = len(chunks)
    keep, sends = outs[0], outs[1 : 1 + n * (n_pair - 1)]
    x = blocks[0]
    if len(outs) > 1 + len(sends):
        x = outs[-1]
        share = blocks[0].shape[0]
        for k, block in enumerate(blocks):
            x[k * share : (k + 1) * share, :] = block[...]
    (res,) = room
    me = lax.axis_index("pair")
    rows = keep.shape[0]
    start = 0
    for weight in weights:
        for j, (first, width) in enumerate(chunks):
            low, high = max(start, first), min(start + weight.shape[1], first + width)
            if low >= high:
                continue
            tile = tile_of(high - low)

            @pl.loop(0, (high - low) // tile)
            def _(step, weight=weight, tile=tile, j=j, low=low, first=first, start=start):
                def at(offset):
                    return pl.ds(pl.multiple_of(offset + step * tile, tile), tile)

                res[...] = jnp.dot(x[...], weight[:, at(low - start)], preferred_element_type=F32)
                for k in range(n_pair):
                    block = pl.ds(pl.multiple_of(lax.rem(me + k, n_pair) * rows, 16), rows)
                    target, offset = (sends[(k - 1) * n + j], low - first) if k else (keep, low)
                    target[:, at(offset)] = res[block, :].astype(target.dtype)

        start += weight.shape[1]


def pair_sum_kernel(chunks, pieces, ins, outs, room):
    keep, got = ins[0], ins[1:]
    n, half = len(chunks), len(pieces)
    for j, (first, wide) in enumerate(chunks):
        for k, (start, width) in enumerate(pieces):
            low, high = max(first, start), min(first + wide, start + width)
            if low >= high:
                continue
            total = keep[:, low:high]
            for part in got[j::n]:
                total += part[:, low - first : high - first].astype(F32)
            for out in (outs[k], outs[half + k]):
                out[:, low - start : high - start] = total.astype(out.dtype)


def activate_kernel(start, ins, outs, room):
    at = slice(start, start + outs[0].shape[1])
    half = len(ins) // 2
    up = sum(part[:, at].astype(F32) for part in ins[:half])
    gate = sum(part[...].astype(F32) for part in ins[half:])
    hidden = (gate / (1.0 + jnp.exp(-gate)) * up).astype(BF16)
    rows = outs[0].shape[0]
    for k, out in enumerate(outs):
        out[...] = hidden[k * rows : (k + 1) * rows]


def down_kernel(n_pair, n_wide, n_weights, first, last, ins, outs, room):
    before = ins[-1:] if not first else []
    ins = ins[: len(ins) - len(before)]
    parts, weights = ins[:-n_weights], ins[-n_weights:]
    hidden, res = room
    c, w = lax.axis_index("pair"), lax.axis_index("wide")
    rows = parts[0].shape[0]
    pieces = len(parts) // n_pair
    for at, part in enumerate(parts):
        k, piece = divmod(at, pieces)
        block = lax.rem(c + n_pair - k, n_pair) * pieces + piece
        hidden[pl.ds(pl.multiple_of(block * rows, 16), rows), :] = part[...]
    width = weights[0].shape[1]
    tile = tile_of(width)

    @pl.loop(0, width // tile)
    def _(step):
        at = pl.ds(pl.multiple_of(step * tile, tile), tile)
        total, start = 0, 0
        for weight in weights:
            deep = slice(start, start + weight.shape[0])
            total += jnp.dot(hidden[:, deep], weight[:, at], preferred_element_type=F32)
            start += weight.shape[0]
        if before:
            total += before[0][:, at]
        if last:
            share = total.shape[0] // n_wide
            res[...] = total
            for k in range(n_wide):
                other = lax.rem(w + k, n_wide)
                place = jnp.bitwise_xor(w, other) if n_wide & (n_wide - 1) == 0 else (n_wide - k) % n_wide
                rows_of = pl.ds(pl.multiple_of(place * share, 16), share)
                outs[k][:, at] = res[rows_of, :].astype(outs[k].dtype)
        else:
            outs[0][:, at] = total


def shards(sizes, tokens, gate_weight, up_weight, down_weight):
    n_seq, n_wide, n_pair = sizes["seq"], sizes["wide"], sizes["pair"]

    def send(value, axis, k, paired=False):
        n = sizes[axis]
        paired = paired and n & (n - 1) == 0
        return lax.ppermute(value, axis, [(i, i ^ k if paired else (i + k) % n) for i in range(n)])

    share, depth = tokens.shape
    rows = share * n_wide
    features = down_weight.shape[1]
    half = rows // n_pair
    loads = cuts(gate_weight.shape[1], GATE)
    chunks = cuts(down_weight.shape[0], DOWN)
    n = len(chunks)
    size = tokens.dtype.itemsize

    def bytes_of(fetch):
        return sum(size * f[3] * f[0].shape[1 - f[1]] for f in fetch)

    unit = gate_weight.shape[1] // sum(GATE)

    def gate_of(j):
        return [(gate_weight, 1, *loads[j])]

    def down_of(name):
        return [(down_weight, 0, start * unit, count * unit) for start, count in DOWN_LOADS[name]]

    def keep(name, fetched):
        for (start, _), array in zip(DOWN_LOADS[name], fetched):
            down[start * unit] = array

    order = []

    def project(blocks, weights, chunks, fetch, after=()):
        width, n = sum(width for _, width in chunks), len(chunks)
        outs, fetched = call(
            order,
            functools.partial(pair_part_kernel, n_pair, chunks, len(weights)),
            [*blocks, *weights],
            [pltpu.VMEM((half, width), F32)]
            + [pltpu.VMEM((half, wide), PAIR_TYPE) for _, wide in chunks] * (n_pair - 1)
            + [pltpu.VMEM((rows, depth), BF16)] * (len(blocks) > 1),
            fetch,
            [pltpu.VMEM((rows, tile_of(width)), F32)],
            COST * 2 * rows * depth * width,
            COST * 2 * bytes_of(fetch),
            after,
        )
        got = [send(outs[1 + (k - 1) * n + j], "pair", k) for k in range(1, n_pair) for j in range(n)]
        return (outs[0], *got), outs[-1], fetched

    def pair_sum(parts, chunks, pieces, after=()):
        outs = call(
            order, functools.partial(pair_sum_kernel, chunks, pieces), parts,
            [pltpu.VMEM((half, width), kind) for kind in (F32, BF16) for _, width in pieces],
            [], [], 0, COST * 8 * parts[0].size, after,
        )[0]
        sums = []
        for own, away in zip(outs[: len(pieces)], outs[len(pieces) :]):
            sums.append([own] + [send(away, "seq", k) for k in range(1, n_seq)])
        return sums

    def activate(ups, gates, start, width):
        split = SPLIT if start == 0 else 1
        hidden, _ = call(
            order, functools.partial(activate_kernel, start), [*ups, *gates],
            [pltpu.VMEM((half // split, width), BF16)] * split, [], [], 0, COST * 8 * half * width,
        )
        got = [send(piece, "pair", k) for k in range(1, n_pair) for piece in hidden]
        return [*hidden, *got]

    def load(array, fetch, traffic, after=()):
        (array,), fetched = call(
            order, load_kernel, [array], [pltpu.VMEM(array.shape, BF16)], fetch, [], 0, traffic, after
        )
        return array, fetched

    def multiply_down(j, parts, total):
        first, last = j == 0, j == n - 1
        start, width = chunks[j]
        weights = [down[at] for at in sorted(down) if start <= at < start + width]
        if last:
            outs = [pltpu.VMEM((share, features), F32)]
            outs += [pltpu.VMEM((share, features), BF16)] * (n_wide - 1)
        else:
            outs = [pltpu.VMEM((rows, features), F32)]
        name = ("first", "second", "")[min(j, 2)]
        fetch = down_of(name) if n > 1 and name else []
        total, more = call(
            order,
            functools.partial(down_kernel, n_pair, n_wide, len(weights), first, last),
            [*parts, *weights, *total],
            outs,
            fetch,
            [pltpu.VMEM((rows, width), BF16), pltpu.VMEM((rows, tile_of(features)), F32)],
            COST * 2 * rows * width * features,
            COST * 2 * bytes_of(fetch),
        )
        if fetch:
            keep(name, more)
        return total

    _, (staged, *early) = call(
        order, load_kernel, [], [], [(tokens, 0, 0, share), (down_weight, 0, 0, share)], [],
        0, 2 * up_weight.size * size,
    )
    blocks = [staged] + [send(tokens if k > 1 else staged, "wide", k, True) for k in range(1, n_wide)]
    up = pltpu.with_memory_space_constraint(up_weight, pltpu.VMEM)
    columns = gate_weight.shape[1]
    down, whole = {}, [(0, columns)]
    if n == 1:
        ups, x, gate = project(blocks, [up], whole, gate_of(0), early)
        (ups,) = pair_sum(ups, whole, whole)
        parts, _, (down[0],) = project([x], gate, chunks, [(down_weight, 0, 0, columns)])
        sums = pair_sum(parts, chunks, chunks)
    else:
        ups, x, first = project(blocks, [up], whole, gate_of(0), early)
        x, more = load(x, down_of("wait"), COST * 2 * bytes_of(down_of("wait")))
        keep("wait", more)
        (ups,) = pair_sum(ups, whole, whole)
        edge = loads[1][0]
        inner = [chunk for chunk in chunks if chunk[0] < edge]
        parts, _, (second,) = project([x], first, inner, gate_of(1))
        outer = [(start - edge, width) for start, width in chunks if start >= edge]
        others, _, more = project([x], [second], outer, down_of("rest"))
        keep("rest", more)
        sums = pair_sum(parts, inner, inner) + pair_sum(others, outer, outer)
        _, more = load(x, down_of("late"), 0)
        keep("late", more)
    load(x, [], 0, ups[1:])
    hiddens = [activate(ups, sums[j], *chunks[j]) for j in range(min(n, 2))]
    total = []
    for j in range(n):
        if j and j + 1 < n:
            hiddens.append(activate(ups, sums[j + 1], *chunks[j + 1]))
        total = multiply_down(j, hiddens[j], total)

    result = total[0]
    for k in range(1, n_wide):
        result = result + send(total[k], "wide", k).astype(F32)
    return result.astype(BF16)


def solution(mesh):
    return jax.shard_map(
        functools.partial(shards, dict(mesh.shape)),
        mesh=mesh,
        in_specs=(
            P(("parts", "wide"), ("seq", "pair")),
            P(("seq", "pair"), "wide"),
            P(("seq", "pair"), "wide"),
            P("wide", ("seq", "pair")),
        ),
        out_specs=P(("parts", "wide"), ("seq", "pair")),
        check_vma=False,
    )
```

```python
import functools

import jax
import jax.numpy as jnp
from jax import lax
from jax.experimental import pallas as pl
from jax.experimental.pallas import tpu as pltpu
from jax.sharding import PartitionSpec as P

BF16, F32 = jnp.bfloat16, jnp.float32
TILE = 512
GATE = (8, 5)
DOWN = (4, 4, 5)
DOWN_LOADS = dict(wait=((0, 1),), rest=((1, 2),), late=((3, 1), (4, 4), (8, 1)), first=((9, 2),), second=((11, 2),))
PAIR_TYPE = BF16
COST = 1
SPLIT = 2


def on_chip():
    return pl.BlockSpec(memory_space=pltpu.VMEM)


def in_place():
    return pl.BlockSpec(memory_space=pl.ANY)


def cuts(columns, shares):
    if columns % (TILE * sum(shares)):
        return [(0, columns)]
    unit = columns // sum(shares)
    chunks, start = [], 0
    for share in shares:
        chunks.append((start, share * unit))
        start += share * unit
    return chunks


def tile_of(width):
    return TILE if width % TILE == 0 else width


def copies(fetch, sources, targets, sems):
    made = []
    for at, ((axis, start, size), source, target) in enumerate(zip(fetch, sources, targets)):
        view = source.at[:, pl.ds(start, size)] if axis else source.at[pl.ds(start, size), :]
        made.append(pltpu.make_async_copy(view, target, sems.at[at]))
    return made


def call(order, body, operands, outs, fetch, scratch, flops, traffic, after=()):
    fetched = []
    for array, axis, start, size in fetch:
        shape = (array.shape[0], size) if axis else (size, array.shape[1])
        fetched.append(pltpu.VMEM(shape, array.dtype))
    n_in = len(operands)
    after = [*after, *order[-1:]]

    def kernel(*refs):
        ins, rest = refs[:n_in], refs[n_in + len(after) :]
        sources, rest = rest[: len(fetch)], rest[len(fetch) :]
        results, rest = rest[: len(outs)], rest[len(outs) :]
        targets, (*room, sems) = rest[: len(fetch)], rest[len(fetch) :]
        made = copies([f[1:] for f in fetch], sources, targets, sems)
        for copy in made:
            copy.start()
        body(ins, results, room)
        for copy in made:
            copy.wait()

    out = pl.pallas_call(
        kernel,
        out_shape=tuple(outs) + tuple(fetched),
        in_specs=[on_chip()] * n_in + [in_place()] * (len(after) + len(fetch)),
        out_specs=tuple([on_chip()] * (len(outs) + len(fetch))),
        scratch_shapes=list(scratch) + [pltpu.SemaphoreType.DMA((max(len(fetch), 1),))],
        compiler_params=pltpu.CompilerParams(vmem_limit_bytes=4 * 2**20),
        cost_estimate=pl.CostEstimate(flops=int(flops), bytes_accessed=int(traffic), transcendentals=0),
    )(*operands, *after, *[pltpu.with_memory_space_constraint(f[0], pltpu.HBM) for f in fetch])
    order.append(min(out, key=lambda array: array.size))
    return out[: len(outs)], out[len(outs) :]


def load_kernel(ins, outs, room):
    for source, target in zip(ins, outs):
        target[...] = source[...]


def pair_part_kernel(n_pair, chunks, n_weights, ins, outs, room):
    blocks, weights = ins[:-n_weights], ins[-n_weights:]
    n = len(chunks)
    keep, sends = outs[0], outs[1 : 1 + n * (n_pair - 1)]
    x = blocks[0]
    if len(outs) > 1 + len(sends):
        x = outs[-1]
        share = blocks[0].shape[0]
        for k, block in enumerate(blocks):
            x[k * share : (k + 1) * share, :] = block[...]
    (res,) = room
    me = lax.axis_index("pair")
    rows = keep.shape[0]
    start = 0
    for weight in weights:
        for j, (first, width) in enumerate(chunks):
            low, high = max(start, first), min(start + weight.shape[1], first + width)
            if low >= high:
                continue
            tile = tile_of(high - low)

            @pl.loop(0, (high - low) // tile)
            def _(step, weight=weight, tile=tile, j=j, low=low, first=first, start=start):
                def at(offset):
                    return pl.ds(pl.multiple_of(offset + step * tile, tile), tile)

                res[...] = jnp.dot(x[...], weight[:, at(low - start)], preferred_element_type=F32)
                for k in range(n_pair):
                    block = pl.ds(pl.multiple_of(lax.rem(me + k, n_pair) * rows, 16), rows)
                    target, offset = (sends[(k - 1) * n + j], low - first) if k else (keep, low)
                    target[:, at(offset)] = res[block, :].astype(target.dtype)

        start += weight.shape[1]


def pair_sum_kernel(chunks, pieces, ins, outs, room):
    keep, got = ins[0], ins[1:]
    n, half = len(chunks), len(pieces)
    for j, (first, wide) in enumerate(chunks):
        for k, (start, width) in enumerate(pieces):
            low, high = max(first, start), min(first + wide, start + width)
            if low >= high:
                continue
            total = keep[:, low:high]
            for part in got[j::n]:
                total += part[:, low - first : high - first].astype(F32)
            for out in (outs[k], outs[half + k]):
                out[:, low - start : high - start] = total.astype(out.dtype)


def activate_kernel(start, ins, outs, room):
    at = slice(start, start + outs[0].shape[1])
    half = len(ins) // 2
    up = sum(part[:, at].astype(F32) for part in ins[:half])
    gate = sum(part[...].astype(F32) for part in ins[half:])
    hidden = (gate / (1.0 + jnp.exp(-gate)) * up).astype(BF16)
    rows = outs[0].shape[0]
    for k, out in enumerate(outs):
        out[...] = hidden[k * rows : (k + 1) * rows]


def down_kernel(n_pair, n_wide, n_weights, first, last, ins, outs, room):
    before = ins[-1:] if not first else []
    ins = ins[: len(ins) - len(before)]
    parts, weights = ins[:-n_weights], ins[-n_weights:]
    hidden, res = room
    c, w = lax.axis_index("pair"), lax.axis_index("wide")
    rows = parts[0].shape[0]
    pieces = len(parts) // n_pair
    for at, part in enumerate(parts):
        k, piece = divmod(at, pieces)
        block = lax.rem(c + n_pair - k, n_pair) * pieces + piece
        hidden[pl.ds(pl.multiple_of(block * rows, 16), rows), :] = part[...]
    width = weights[0].shape[1]
    tile = tile_of(width)

    @pl.loop(0, width // tile)
    def _(step):
        at = pl.ds(pl.multiple_of(step * tile, tile), tile)
        total, start = 0, 0
        for weight in weights:
            deep = slice(start, start + weight.shape[0])
            total += jnp.dot(hidden[:, deep], weight[:, at], preferred_element_type=F32)
            start += weight.shape[0]
        if before:
            total += before[0][:, at]
        if last:
            share = total.shape[0] // n_wide
            res[...] = total
            for k in range(n_wide):
                other = lax.rem(w + k, n_wide)
                place = jnp.bitwise_xor(w, other) if n_wide & (n_wide - 1) == 0 else (n_wide - k) % n_wide
                rows_of = pl.ds(pl.multiple_of(place * share, 16), share)
                outs[k][:, at] = res[rows_of, :].astype(outs[k].dtype)
        else:
            outs[0][:, at] = total


def shards(sizes, tokens, gate_weight, up_weight, down_weight):
    n_seq, n_wide, n_pair = sizes["seq"], sizes["wide"], sizes["pair"]

    def send(value, axis, k, paired=False):
        n = sizes[axis]
        paired = paired and n & (n - 1) == 0
        return lax.ppermute(value, axis, [(i, i ^ k if paired else (i + k) % n) for i in range(n)])

    share, depth = tokens.shape
    rows = share * n_wide
    features = down_weight.shape[1]
    half = rows // n_pair
    loads = cuts(gate_weight.shape[1], GATE)
    chunks = cuts(down_weight.shape[0], DOWN)
    n = len(chunks)
    size = tokens.dtype.itemsize

    def bytes_of(fetch):
        return sum(size * f[3] * f[0].shape[1 - f[1]] for f in fetch)

    unit = gate_weight.shape[1] // sum(GATE)

    def gate_of(j):
        return [(gate_weight, 1, *loads[j])]

    def down_of(name):
        return [(down_weight, 0, start * unit, count * unit) for start, count in DOWN_LOADS[name]]

    def keep(name, fetched):
        for (start, _), array in zip(DOWN_LOADS[name], fetched):
            down[start * unit] = array

    order = []

    def project(blocks, weights, chunks, fetch, after=()):
        width, n = sum(width for _, width in chunks), len(chunks)
        outs, fetched = call(
            order,
            functools.partial(pair_part_kernel, n_pair, chunks, len(weights)),
            [*blocks, *weights],
            [pltpu.VMEM((half, width), F32)]
            + [pltpu.VMEM((half, wide), PAIR_TYPE) for _, wide in chunks] * (n_pair - 1)
            + [pltpu.VMEM((rows, depth), BF16)] * (len(blocks) > 1),
            fetch,
            [pltpu.VMEM((rows, tile_of(width)), F32)],
            COST * 2 * rows * depth * width,
            COST * 2 * bytes_of(fetch),
            after,
        )
        got = [send(outs[1 + (k - 1) * n + j], "pair", k) for k in range(1, n_pair) for j in range(n)]
        return (outs[0], *got), outs[-1], fetched

    def pair_sum(parts, chunks, pieces, after=()):
        outs = call(
            order, functools.partial(pair_sum_kernel, chunks, pieces), parts,
            [pltpu.VMEM((half, width), kind) for kind in (F32, BF16) for _, width in pieces],
            [], [], 0, COST * 8 * parts[0].size, after,
        )[0]
        sums = []
        for own, away in zip(outs[: len(pieces)], outs[len(pieces) :]):
            sums.append([own] + [send(away, "seq", k) for k in range(1, n_seq)])
        return sums

    def activate(ups, gates, start, width):
        split = SPLIT if start == 0 else 1
        hidden, _ = call(
            order, functools.partial(activate_kernel, start), [*ups, *gates],
            [pltpu.VMEM((half // split, width), BF16)] * split, [], [], 0, COST * 8 * half * width,
        )
        got = [send(piece, "pair", k) for k in range(1, n_pair) for piece in hidden]
        return [*hidden, *got]

    def load(array, fetch, traffic, after=()):
        (array,), fetched = call(
            order, load_kernel, [array], [pltpu.VMEM(array.shape, BF16)], fetch, [], 0, traffic, after
        )
        return array, fetched

    def multiply_down(j, parts, total):
        first, last = j == 0, j == n - 1
        start, width = chunks[j]
        weights = [down[at] for at in sorted(down) if start <= at < start + width]
        if last:
            outs = [pltpu.VMEM((share, features), F32)]
            outs += [pltpu.VMEM((share, features), BF16)] * (n_wide - 1)
        else:
            outs = [pltpu.VMEM((rows, features), F32)]
        name = ("first", "second", "")[min(j, 2)]
        fetch = down_of(name) if n > 1 and name else []
        total, more = call(
            order,
            functools.partial(down_kernel, n_pair, n_wide, len(weights), first, last),
            [*parts, *weights, *total],
            outs,
            fetch,
            [pltpu.VMEM((rows, width), BF16), pltpu.VMEM((rows, tile_of(features)), F32)],
            COST * 2 * rows * width * features,
            COST * 2 * bytes_of(fetch),
        )
        if fetch:
            keep(name, more)
        return total

    _, (staged, *early) = call(
        order, load_kernel, [], [], [(tokens, 0, 0, share), (down_weight, 0, 0, share)], [],
        0, 2 * up_weight.size * size,
    )
    blocks = [staged] + [send(tokens, "wide", k, True) for k in range(1, n_wide)]
    up = pltpu.with_memory_space_constraint(up_weight, pltpu.VMEM)
    columns = gate_weight.shape[1]
    down, whole = {}, [(0, columns)]
    if n == 1:
        ups, x, gate = project(blocks, [up], whole, gate_of(0), early)
        (ups,) = pair_sum(ups, whole, whole)
        parts, _, (down[0],) = project([x], gate, chunks, [(down_weight, 0, 0, columns)])
        sums = pair_sum(parts, chunks, chunks)
    else:
        ups, x, first = project(blocks, [up], whole, gate_of(0), early)
        x, more = load(x, down_of("wait"), COST * 2 * bytes_of(down_of("wait")))
        keep("wait", more)
        (ups,) = pair_sum(ups, whole, whole)
        edge = loads[1][0]
        inner = [chunk for chunk in chunks if chunk[0] < edge]
        parts, _, (second,) = project([x], first, inner, gate_of(1))
        outer = [(start - edge, width) for start, width in chunks if start >= edge]
        others, _, more = project([x], [second], outer, down_of("rest"))
        keep("rest", more)
        sums = pair_sum(parts, inner, inner) + pair_sum(others, outer, outer)
        _, more = load(x, down_of("late"), 0)
        keep("late", more)
    load(x, [], 0, ups[1:])
    hiddens = [activate(ups, sums[j], *chunks[j]) for j in range(min(n, 2))]
    total = []
    for j in range(n):
        if j and j + 1 < n:
            hiddens.append(activate(ups, sums[j + 1], *chunks[j + 1]))
        total = multiply_down(j, hiddens[j], total)

    result = total[0]
    for k in range(1, n_wide):
        result = result + send(total[k], "wide", k).astype(F32)
    return result.astype(BF16)


def solution(mesh):
    return jax.shard_map(
        functools.partial(shards, dict(mesh.shape)),
        mesh=mesh,
        in_specs=(
            P(("parts", "wide"), ("seq", "pair")),
            P(("seq", "pair"), "wide"),
            P(("seq", "pair"), "wide"),
            P("wide", ("seq", "pair")),
        ),
        out_specs=P(("parts", "wide"), ("seq", "pair")),
        check_vma=False,
    )
```

```python
import functools

import jax
import jax.numpy as jnp
from jax import lax
from jax.experimental import pallas as pl
from jax.experimental.pallas import tpu as pltpu
from jax.sharding import PartitionSpec as P

BF16, F32 = jnp.bfloat16, jnp.float32
TILE = 512
GATE = (8, 5)
DOWN = (4, 4, 5)
DOWN_LOADS = dict(wait=((0, 1),), rest=((1, 2),), late=((3, 1), (4, 4), (8, 1)), first=((9, 2),), second=((11, 2),))
PAIR_TYPE = BF16
COST = 1
SPLIT = 2


def on_chip():
    return pl.BlockSpec(memory_space=pltpu.VMEM)


def in_place():
    return pl.BlockSpec(memory_space=pl.ANY)


def cuts(columns, shares):
    if columns % (TILE * sum(shares)):
        return [(0, columns)]
    unit = columns // sum(shares)
    chunks, start = [], 0
    for share in shares:
        chunks.append((start, share * unit))
        start += share * unit
    return chunks


def tile_of(width):
    return TILE if width % TILE == 0 else width


def copies(fetch, sources, targets, sems):
    made = []
    for at, ((axis, start, size), source, target) in enumerate(zip(fetch, sources, targets)):
        view = source.at[:, pl.ds(start, size)] if axis else source.at[pl.ds(start, size), :]
        made.append(pltpu.make_async_copy(view, target, sems.at[at]))
    return made


def call(order, body, operands, outs, fetch, scratch, flops, traffic, after=()):
    fetched = []
    for array, axis, start, size in fetch:
        shape = (array.shape[0], size) if axis else (size, array.shape[1])
        fetched.append(pltpu.VMEM(shape, array.dtype))
    n_in = len(operands)
    after = [*after, *order[-1:]]

    def kernel(*refs):
        ins, rest = refs[:n_in], refs[n_in + len(after) :]
        sources, rest = rest[: len(fetch)], rest[len(fetch) :]
        results, rest = rest[: len(outs)], rest[len(outs) :]
        targets, (*room, sems) = rest[: len(fetch)], rest[len(fetch) :]
        made = copies([f[1:] for f in fetch], sources, targets, sems)
        for copy in made:
            copy.start()
        body(ins, results, room)
        for copy in made:
            copy.wait()

    out = pl.pallas_call(
        kernel,
        out_shape=tuple(outs) + tuple(fetched),
        in_specs=[on_chip()] * n_in + [in_place()] * (len(after) + len(fetch)),
        out_specs=tuple([on_chip()] * (len(outs) + len(fetch))),
        scratch_shapes=list(scratch) + [pltpu.SemaphoreType.DMA((max(len(fetch), 1),))],
        compiler_params=pltpu.CompilerParams(vmem_limit_bytes=4 * 2**20),
        cost_estimate=pl.CostEstimate(flops=int(flops), bytes_accessed=int(traffic), transcendentals=0),
    )(*operands, *after, *[pltpu.with_memory_space_constraint(f[0], pltpu.HBM) for f in fetch])
    order.append(min(out, key=lambda array: array.size))
    return out[: len(outs)], out[len(outs) :]


def load_kernel(ins, outs, room):
    for source, target in zip(ins, outs):
        target[...] = source[...]


def pair_part_kernel(n_pair, chunks, n_weights, ins, outs, room):
    blocks, weights = ins[:-n_weights], ins[-n_weights:]
    n = len(chunks)
    keep, sends = outs[0], outs[1 : 1 + n * (n_pair - 1)]
    x = blocks[0]
    if len(outs) > 1 + len(sends):
        x = outs[-1]
        share = blocks[0].shape[0]
        for k, block in enumerate(blocks):
            x[k * share : (k + 1) * share, :] = block[...]
    (res,) = room
    me = lax.axis_index("pair")
    rows = keep.shape[0]
    start = 0
    for weight in weights:
        for j, (first, width) in enumerate(chunks):
            low, high = max(start, first), min(start + weight.shape[1], first + width)
            if low >= high:
                continue
            tile = tile_of(high - low)

            @pl.loop(0, (high - low) // tile)
            def _(step, weight=weight, tile=tile, j=j, low=low, first=first, start=start):
                def at(offset):
                    return pl.ds(pl.multiple_of(offset + step * tile, tile), tile)

                res[...] = jnp.dot(x[...], weight[:, at(low - start)], preferred_element_type=F32)
                for k in range(n_pair):
                    block = pl.ds(pl.multiple_of(lax.rem(me + k, n_pair) * rows, 16), rows)
                    target, offset = (sends[(k - 1) * n + j], low - first) if k else (keep, low)
                    target[:, at(offset)] = res[block, :].astype(target.dtype)

        start += weight.shape[1]


def pair_sum_kernel(chunks, pieces, ins, outs, room):
    keep, got = ins[0], ins[1:]
    n, half = len(chunks), len(pieces)
    for j, (first, wide) in enumerate(chunks):
        for k, (start, width) in enumerate(pieces):
            low, high = max(first, start), min(first + wide, start + width)
            if low >= high:
                continue
            total = keep[:, low:high]
            for part in got[j::n]:
                total += part[:, low - first : high - first].astype(F32)
            for out in (outs[k], outs[half + k]):
                out[:, low - start : high - start] = total.astype(out.dtype)


def activate_kernel(start, ins, outs, room):
    at = slice(start, start + outs[0].shape[1])
    half = len(ins) // 2
    up = sum(part[:, at].astype(F32) for part in ins[:half])
    gate = sum(part[...].astype(F32) for part in ins[half:])
    hidden = (gate / (1.0 + jnp.exp(-gate)) * up).astype(BF16)
    rows = outs[0].shape[0]
    for k, out in enumerate(outs):
        out[...] = hidden[k * rows : (k + 1) * rows]


def down_kernel(n_pair, n_wide, n_weights, first, last, ins, outs, room):
    before = ins[-1:] if not first else []
    ins = ins[: len(ins) - len(before)]
    parts, weights = ins[:-n_weights], ins[-n_weights:]
    hidden, res = room
    c, w = lax.axis_index("pair"), lax.axis_index("wide")
    rows = parts[0].shape[0]
    pieces = len(parts) // n_pair
    for at, part in enumerate(parts):
        k, piece = divmod(at, pieces)
        block = lax.rem(c + n_pair - k, n_pair) * pieces + piece
        hidden[pl.ds(pl.multiple_of(block * rows, 16), rows), :] = part[...]
    width = weights[0].shape[1]
    tile = tile_of(width)

    @pl.loop(0, width // tile)
    def _(step):
        at = pl.ds(pl.multiple_of(step * tile, tile), tile)
        total, start = 0, 0
        for weight in weights:
            deep = slice(start, start + weight.shape[0])
            total += jnp.dot(hidden[:, deep], weight[:, at], preferred_element_type=F32)
            start += weight.shape[0]
        if before:
            total += before[0][:, at]
        if last:
            share = total.shape[0] // n_wide
            res[...] = total
            for k in range(n_wide):
                other = lax.rem(w + k, n_wide)
                place = jnp.bitwise_xor(w, other) if n_wide & (n_wide - 1) == 0 else (n_wide - k) % n_wide
                rows_of = pl.ds(pl.multiple_of(place * share, 16), share)
                outs[k][:, at] = res[rows_of, :].astype(outs[k].dtype)
        else:
            outs[0][:, at] = total


def shards(sizes, tokens, gate_weight, up_weight, down_weight):
    n_seq, n_wide, n_pair = sizes["seq"], sizes["wide"], sizes["pair"]

    def send(value, axis, k, paired=False):
        n = sizes[axis]
        paired = paired and n & (n - 1) == 0
        return lax.ppermute(value, axis, [(i, i ^ k if paired else (i + k) % n) for i in range(n)])

    share, depth = tokens.shape
    rows = share * n_wide
    features = down_weight.shape[1]
    half = rows // n_pair
    loads = cuts(gate_weight.shape[1], GATE)
    chunks = cuts(down_weight.shape[0], DOWN)
    n = len(chunks)
    size = tokens.dtype.itemsize

    def bytes_of(fetch):
        return sum(size * f[3] * f[0].shape[1 - f[1]] for f in fetch)

    unit = gate_weight.shape[1] // sum(GATE)

    def gate_of(j):
        return [(gate_weight, 1, *loads[j])]

    def down_of(name):
        return [(down_weight, 0, start * unit, count * unit) for start, count in DOWN_LOADS[name]]

    def keep(name, fetched):
        for (start, _), array in zip(DOWN_LOADS[name], fetched):
            down[start * unit] = array

    order = []

    def project(blocks, weights, chunks, fetch, after=()):
        width, n = sum(width for _, width in chunks), len(chunks)
        outs, fetched = call(
            order,
            functools.partial(pair_part_kernel, n_pair, chunks, len(weights)),
            [*blocks, *weights],
            [pltpu.VMEM((half, width), F32)]
            + [pltpu.VMEM((half, wide), PAIR_TYPE) for _, wide in chunks] * (n_pair - 1)
            + [pltpu.VMEM((rows, depth), BF16)] * (len(blocks) > 1),
            fetch,
            [pltpu.VMEM((rows, tile_of(width)), F32)],
            COST * 2 * rows * depth * width,
            COST * 2 * bytes_of(fetch),
            after,
        )
        got = [send(outs[1 + (k - 1) * n + j], "pair", k) for k in range(1, n_pair) for j in range(n)]
        return (outs[0], *got), outs[-1], fetched

    def pair_sum(parts, chunks, pieces, after=()):
        outs = call(
            order, functools.partial(pair_sum_kernel, chunks, pieces), parts,
            [pltpu.VMEM((half, width), kind) for kind in (F32, BF16) for _, width in pieces],
            [], [], 0, COST * 8 * parts[0].size, after,
        )[0]
        sums = []
        for own, away in zip(outs[: len(pieces)], outs[len(pieces) :]):
            sums.append([own] + [send(away, "seq", k) for k in range(1, n_seq)])
        return sums

    def activate(ups, gates, start, width):
        split = SPLIT if start == 0 else 1
        hidden, _ = call(
            order, functools.partial(activate_kernel, start), [*ups, *gates],
            [pltpu.VMEM((half // split, width), BF16)] * split, [], [], 0, COST * 8 * half * width,
        )
        got = [send(piece, "pair", k) for k in range(1, n_pair) for piece in hidden]
        return [*hidden, *got]

    def load(array, fetch, traffic, after=()):
        (array,), fetched = call(
            order, load_kernel, [array], [pltpu.VMEM(array.shape, BF16)], fetch, [], 0, traffic, after
        )
        return array, fetched

    def multiply_down(j, parts, total):
        first, last = j == 0, j == n - 1
        start, width = chunks[j]
        weights = [down[at] for at in sorted(down) if start <= at < start + width]
        if last:
            outs = [pltpu.VMEM((share, features), F32)]
            outs += [pltpu.VMEM((share, features), BF16)] * (n_wide - 1)
        else:
            outs = [pltpu.VMEM((rows, features), F32)]
        name = ("first", "second", "")[min(j, 2)]
        fetch = down_of(name) if n > 1 and name else []
        total, more = call(
            order,
            functools.partial(down_kernel, n_pair, n_wide, len(weights), first, last),
            [*parts, *weights, *total],
            outs,
            fetch,
            [pltpu.VMEM((rows, width), BF16), pltpu.VMEM((rows, tile_of(features)), F32)],
            COST * 2 * rows * width * features,
            COST * 2 * bytes_of(fetch),
        )
        if fetch:
            keep(name, more)
        return total

    _, (staged, *early) = call(
        order, load_kernel, [], [], [(tokens, 0, 0, share), (down_weight, 0, 0, share)], [],
        0, 2 * up_weight.size * size,
    )
    blocks = [staged] + [send(tokens if k > 1 else staged, "wide", k, True) for k in range(1, n_wide)]
    up = pltpu.with_memory_space_constraint(up_weight, pltpu.VMEM)
    columns = gate_weight.shape[1]
    down, whole = {}, [(0, columns)]
    if n == 1:
        ups, x, gate = project(blocks, [up], whole, gate_of(0), early)
        (ups,) = pair_sum(ups, whole, whole)
        parts, _, (down[0],) = project([x], gate, chunks, [(down_weight, 0, 0, columns)])
        sums = pair_sum(parts, chunks, chunks)
    else:
        ups, x, first = project(blocks, [up], whole, gate_of(0), early)
        x, more = load(x, down_of("wait"), COST * 2 * bytes_of(down_of("wait")))
        keep("wait", more)
        (ups,) = pair_sum(ups, whole, whole)
        edge = loads[1][0]
        inner = [chunk for chunk in chunks if chunk[0] < edge]
        parts, _, (second,) = project([x], first, inner, gate_of(1))
        outer = [(start - edge, width) for start, width in chunks if start >= edge]
        others, _, more = project([x], [second], outer, down_of("rest"))
        keep("rest", more)
        sums = pair_sum(parts, inner, inner) + pair_sum(others, outer, outer)
        _, more = load(x, down_of("late"), 0)
        keep("late", more)
    load(x, [], 0, ups[1:])
    hiddens = [activate(ups, sums[j], *chunks[j]) for j in range(min(n, 2))]
    total = []
    for j in range(n):
        if j and j + 1 < n:
            hiddens.append(activate(ups, sums[j + 1], *chunks[j + 1]))
        total = multiply_down(j, hiddens[j], total)

    result = total[0]
    for k in sorted(range(1, n_wide), key=lambda k: -min(k, n_wide - k)):
        result = result + send(total[k], "wide", k).astype(F32)
    return result.astype(BF16)


def solution(mesh):
    return jax.shard_map(
        functools.partial(shards, dict(mesh.shape)),
        mesh=mesh,
        in_specs=(
            P(("parts", "wide"), ("seq", "pair")),
            P(("seq", "pair"), "wide"),
            P(("seq", "pair"), "wide"),
            P("wide", ("seq", "pair")),
        ),
        out_specs=P(("parts", "wide"), ("seq", "pair")),
        check_vma=False,
    )
```

```python
import functools

import jax
import jax.numpy as jnp
from jax import lax
from jax.experimental import pallas as pl
from jax.experimental.pallas import tpu as pltpu
from jax.sharding import PartitionSpec as P

BF16, F32 = jnp.bfloat16, jnp.float32
TILE = 512
GATE = (8, 5)
DOWN = (4, 4, 5)
DOWN_LOADS = dict(wait=((0, 1),), rest=((1, 2),), late=((3, 1), (4, 4), (8, 2)), first=((10, 3),), second=())
PAIR_TYPE = BF16
COST = 1
SPLIT = 2


def on_chip():
    return pl.BlockSpec(memory_space=pltpu.VMEM)


def in_place():
    return pl.BlockSpec(memory_space=pl.ANY)


def cuts(columns, shares):
    if columns % (TILE * sum(shares)):
        return [(0, columns)]
    unit = columns // sum(shares)
    chunks, start = [], 0
    for share in shares:
        chunks.append((start, share * unit))
        start += share * unit
    return chunks


def tile_of(width):
    return TILE if width % TILE == 0 else width


def copies(fetch, sources, targets, sems):
    made = []
    for at, ((axis, start, size), source, target) in enumerate(zip(fetch, sources, targets)):
        view = source.at[:, pl.ds(start, size)] if axis else source.at[pl.ds(start, size), :]
        made.append(pltpu.make_async_copy(view, target, sems.at[at]))
    return made


def call(order, body, operands, outs, fetch, scratch, flops, traffic, after=()):
    fetched = []
    for array, axis, start, size in fetch:
        shape = (array.shape[0], size) if axis else (size, array.shape[1])
        fetched.append(pltpu.VMEM(shape, array.dtype))
    n_in = len(operands)
    after = [*after, *order[-1:]]

    def kernel(*refs):
        ins, rest = refs[:n_in], refs[n_in + len(after) :]
        sources, rest = rest[: len(fetch)], rest[len(fetch) :]
        results, rest = rest[: len(outs)], rest[len(outs) :]
        targets, (*room, sems) = rest[: len(fetch)], rest[len(fetch) :]
        made = copies([f[1:] for f in fetch], sources, targets, sems)
        for copy in made:
            copy.start()
        body(ins, results, room)
        for copy in made:
            copy.wait()

    out = pl.pallas_call(
        kernel,
        out_shape=tuple(outs) + tuple(fetched),
        in_specs=[on_chip()] * n_in + [in_place()] * (len(after) + len(fetch)),
        out_specs=tuple([on_chip()] * (len(outs) + len(fetch))),
        scratch_shapes=list(scratch) + [pltpu.SemaphoreType.DMA((max(len(fetch), 1),))],
        compiler_params=pltpu.CompilerParams(vmem_limit_bytes=4 * 2**20),
        cost_estimate=pl.CostEstimate(flops=int(flops), bytes_accessed=int(traffic), transcendentals=0),
    )(*operands, *after, *[pltpu.with_memory_space_constraint(f[0], pltpu.HBM) for f in fetch])
    order.append(min(out, key=lambda array: array.size))
    return out[: len(outs)], out[len(outs) :]


def load_kernel(ins, outs, room):
    for source, target in zip(ins, outs):
        target[...] = source[...]


def pair_part_kernel(n_pair, chunks, n_weights, ins, outs, room):
    blocks, weights = ins[:-n_weights], ins[-n_weights:]
    n = len(chunks)
    keep, sends = outs[0], outs[1 : 1 + n * (n_pair - 1)]
    x = blocks[0]
    if len(outs) > 1 + len(sends):
        x = outs[-1]
        share = blocks[0].shape[0]
        for k, block in enumerate(blocks):
            x[k * share : (k + 1) * share, :] = block[...]
    (res,) = room
    me = lax.axis_index("pair")
    rows = keep.shape[0]
    start = 0
    for weight in weights:
        for j, (first, width) in enumerate(chunks):
            low, high = max(start, first), min(start + weight.shape[1], first + width)
            if low >= high:
                continue
            tile = tile_of(high - low)

            @pl.loop(0, (high - low) // tile)
            def _(step, weight=weight, tile=tile, j=j, low=low, first=first, start=start):
                def at(offset):
                    return pl.ds(pl.multiple_of(offset + step * tile, tile), tile)

                res[...] = jnp.dot(x[...], weight[:, at(low - start)], preferred_element_type=F32)
                for k in range(n_pair):
                    block = pl.ds(pl.multiple_of(lax.rem(me + k, n_pair) * rows, 16), rows)
                    target, offset = (sends[(k - 1) * n + j], low - first) if k else (keep, low)
                    target[:, at(offset)] = res[block, :].astype(target.dtype)

        start += weight.shape[1]


def pair_sum_kernel(chunks, pieces, ins, outs, room):
    keep, got = ins[0], ins[1:]
    n, half = len(chunks), len(pieces)
    for j, (first, wide) in enumerate(chunks):
        for k, (start, width) in enumerate(pieces):
            low, high = max(first, start), min(first + wide, start + width)
            if low >= high:
                continue
            total = keep[:, low:high]
            for part in got[j::n]:
                total += part[:, low - first : high - first].astype(F32)
            for out in (outs[k], outs[half + k]):
                out[:, low - start : high - start] = total.astype(out.dtype)


def activate_kernel(start, ins, outs, room):
    at = slice(start, start + outs[0].shape[1])
    half = len(ins) // 2
    up = sum(part[:, at].astype(F32) for part in ins[:half])
    gate = sum(part[...].astype(F32) for part in ins[half:])
    hidden = (gate / (1.0 + jnp.exp(-gate)) * up).astype(BF16)
    rows = outs[0].shape[0]
    for k, out in enumerate(outs):
        out[...] = hidden[k * rows : (k + 1) * rows]


def down_kernel(n_pair, n_wide, n_weights, first, last, ins, outs, room):
    before = ins[-1:] if not first else []
    ins = ins[: len(ins) - len(before)]
    parts, weights = ins[:-n_weights], ins[-n_weights:]
    hidden, res = room
    c, w = lax.axis_index("pair"), lax.axis_index("wide")
    rows = parts[0].shape[0]
    pieces = len(parts) // n_pair
    for at, part in enumerate(parts):
        k, piece = divmod(at, pieces)
        block = lax.rem(c + n_pair - k, n_pair) * pieces + piece
        hidden[pl.ds(pl.multiple_of(block * rows, 16), rows), :] = part[...]
    width = weights[0].shape[1]
    tile = tile_of(width)

    @pl.loop(0, width // tile)
    def _(step):
        at = pl.ds(pl.multiple_of(step * tile, tile), tile)
        total, start = 0, 0
        for weight in weights:
            deep = slice(start, start + weight.shape[0])
            total += jnp.dot(hidden[:, deep], weight[:, at], preferred_element_type=F32)
            start += weight.shape[0]
        if before:
            total += before[0][:, at]
        if last:
            share = total.shape[0] // n_wide
            res[...] = total
            for k in range(n_wide):
                other = lax.rem(w + k, n_wide)
                place = jnp.bitwise_xor(w, other) if n_wide & (n_wide - 1) == 0 else (n_wide - k) % n_wide
                rows_of = pl.ds(pl.multiple_of(place * share, 16), share)
                outs[k][:, at] = res[rows_of, :].astype(outs[k].dtype)
        else:
            outs[0][:, at] = total


def shards(sizes, tokens, gate_weight, up_weight, down_weight):
    n_seq, n_wide, n_pair = sizes["seq"], sizes["wide"], sizes["pair"]

    def send(value, axis, k, paired=False):
        n = sizes[axis]
        paired = paired and n & (n - 1) == 0
        return lax.ppermute(value, axis, [(i, i ^ k if paired else (i + k) % n) for i in range(n)])

    share, depth = tokens.shape
    rows = share * n_wide
    features = down_weight.shape[1]
    half = rows // n_pair
    loads = cuts(gate_weight.shape[1], GATE)
    chunks = cuts(down_weight.shape[0], DOWN)
    n = len(chunks)
    size = tokens.dtype.itemsize

    def bytes_of(fetch):
        return sum(size * f[3] * f[0].shape[1 - f[1]] for f in fetch)

    unit = gate_weight.shape[1] // sum(GATE)

    def gate_of(j):
        return [(gate_weight, 1, *loads[j])]

    def down_of(name):
        return [(down_weight, 0, start * unit, count * unit) for start, count in DOWN_LOADS[name]]

    def keep(name, fetched):
        for (start, _), array in zip(DOWN_LOADS[name], fetched):
            down[start * unit] = array

    order = []

    def project(blocks, weights, chunks, fetch, after=()):
        width, n = sum(width for _, width in chunks), len(chunks)
        outs, fetched = call(
            order,
            functools.partial(pair_part_kernel, n_pair, chunks, len(weights)),
            [*blocks, *weights],
            [pltpu.VMEM((half, width), F32)]
            + [pltpu.VMEM((half, wide), PAIR_TYPE) for _, wide in chunks] * (n_pair - 1)
            + [pltpu.VMEM((rows, depth), BF16)] * (len(blocks) > 1),
            fetch,
            [pltpu.VMEM((rows, tile_of(width)), F32)],
            COST * 2 * rows * depth * width,
            COST * 2 * bytes_of(fetch),
            after,
        )
        got = [send(outs[1 + (k - 1) * n + j], "pair", k) for k in range(1, n_pair) for j in range(n)]
        return (outs[0], *got), outs[-1], fetched

    def pair_sum(parts, chunks, pieces, after=()):
        outs = call(
            order, functools.partial(pair_sum_kernel, chunks, pieces), parts,
            [pltpu.VMEM((half, width), kind) for kind in (F32, BF16) for _, width in pieces],
            [], [], 0, COST * 8 * parts[0].size, after,
        )[0]
        sums = []
        for own, away in zip(outs[: len(pieces)], outs[len(pieces) :]):
            sums.append([own] + [send(away, "seq", k) for k in range(1, n_seq)])
        return sums

    def activate(ups, gates, start, width):
        split = SPLIT if start == 0 else 1
        hidden, _ = call(
            order, functools.partial(activate_kernel, start), [*ups, *gates],
            [pltpu.VMEM((half // split, width), BF16)] * split, [], [], 0, COST * 8 * half * width,
        )
        got = [send(piece, "pair", k) for k in range(1, n_pair) for piece in hidden]
        return [*hidden, *got]

    def load(array, fetch, traffic, after=()):
        (array,), fetched = call(
            order, load_kernel, [array], [pltpu.VMEM(array.shape, BF16)], fetch, [], 0, traffic, after
        )
        return array, fetched

    def multiply_down(j, parts, total):
        first, last = j == 0, j == n - 1
        start, width = chunks[j]
        weights = [down[at] for at in sorted(down) if start <= at < start + width]
        if last:
            outs = [pltpu.VMEM((share, features), F32)]
            outs += [pltpu.VMEM((share, features), BF16)] * (n_wide - 1)
        else:
            outs = [pltpu.VMEM((rows, features), F32)]
        name = ("first", "second", "")[min(j, 2)]
        fetch = down_of(name) if n > 1 and name else []
        total, more = call(
            order,
            functools.partial(down_kernel, n_pair, n_wide, len(weights), first, last),
            [*parts, *weights, *total],
            outs,
            fetch,
            [pltpu.VMEM((rows, width), BF16), pltpu.VMEM((rows, tile_of(features)), F32)],
            COST * 2 * rows * width * features,
            COST * 2 * bytes_of(fetch),
        )
        if fetch:
            keep(name, more)
        return total

    _, (staged, *early) = call(
        order, load_kernel, [], [], [(tokens, 0, 0, share), (down_weight, 0, 0, share)], [],
        0, 2 * up_weight.size * size,
    )
    blocks = [staged] + [send(tokens if k > 1 else staged, "wide", k, True) for k in range(1, n_wide)]
    up = pltpu.with_memory_space_constraint(up_weight, pltpu.VMEM)
    columns = gate_weight.shape[1]
    down, whole = {}, [(0, columns)]
    if n == 1:
        ups, x, gate = project(blocks, [up], whole, gate_of(0), early)
        (ups,) = pair_sum(ups, whole, whole)
        parts, _, (down[0],) = project([x], gate, chunks, [(down_weight, 0, 0, columns)])
        sums = pair_sum(parts, chunks, chunks)
    else:
        ups, x, first = project(blocks, [up], whole, gate_of(0), early)
        x, more = load(x, down_of("wait"), COST * 2 * bytes_of(down_of("wait")))
        keep("wait", more)
        (ups,) = pair_sum(ups, whole, whole)
        edge = loads[1][0]
        inner = [chunk for chunk in chunks if chunk[0] < edge]
        parts, _, (second,) = project([x], first, inner, gate_of(1))
        outer = [(start - edge, width) for start, width in chunks if start >= edge]
        others, _, more = project([x], [second], outer, down_of("rest"))
        keep("rest", more)
        sums = pair_sum(parts, inner, inner) + pair_sum(others, outer, outer)
        _, more = load(x, down_of("late"), 0)
        keep("late", more)
    load(x, [], 0, ups[1:])
    hiddens = [activate(ups, sums[j], *chunks[j]) for j in range(min(n, 2))]
    total = []
    for j in range(n):
        if j and j + 1 < n:
            hiddens.append(activate(ups, sums[j + 1], *chunks[j + 1]))
        total = multiply_down(j, hiddens[j], total)

    result = total[0]
    for k in range(1, n_wide):
        result = result + send(total[k], "wide", k).astype(F32)
    return result.astype(BF16)


def solution(mesh):
    return jax.shard_map(
        functools.partial(shards, dict(mesh.shape)),
        mesh=mesh,
        in_specs=(
            P(("parts", "wide"), ("seq", "pair")),
            P(("seq", "pair"), "wide"),
            P(("seq", "pair"), "wide"),
            P("wide", ("seq", "pair")),
        ),
        out_specs=P(("parts", "wide"), ("seq", "pair")),
        check_vma=False,
    )
```

```python
import functools

import jax
import jax.numpy as jnp
from jax import lax
from jax.experimental import pallas as pl
from jax.experimental.pallas import tpu as pltpu
from jax.sharding import PartitionSpec as P

BF16, F32 = jnp.bfloat16, jnp.float32
TILE = 512
GATE = (8, 5)
DOWN = (4, 4, 5)
DOWN_LOADS = dict(rest=((1, 2),), late=((0, 1), (3, 1), (4, 4), (8, 1)), first=((9, 2),), second=((11, 2),))
PAIR_TYPE = BF16
COST = 1
SPLIT = 2


def on_chip():
    return pl.BlockSpec(memory_space=pltpu.VMEM)


def in_place():
    return pl.BlockSpec(memory_space=pl.ANY)


def cuts(columns, shares):
    if columns % (TILE * sum(shares)):
        return [(0, columns)]
    unit = columns // sum(shares)
    chunks, start = [], 0
    for share in shares:
        chunks.append((start, share * unit))
        start += share * unit
    return chunks


def tile_of(width):
    return TILE if width % TILE == 0 else width


def copies(fetch, sources, targets, sems):
    made = []
    for at, ((axis, start, size), source, target) in enumerate(zip(fetch, sources, targets)):
        view = source.at[:, pl.ds(start, size)] if axis else source.at[pl.ds(start, size), :]
        made.append(pltpu.make_async_copy(view, target, sems.at[at]))
    return made


def call(order, body, operands, outs, fetch, scratch, flops, traffic, after=()):
    fetched = []
    for array, axis, start, size in fetch:
        shape = (array.shape[0], size) if axis else (size, array.shape[1])
        fetched.append(pltpu.VMEM(shape, array.dtype))
    n_in = len(operands)
    after = [*after, *order[-1:]]

    def kernel(*refs):
        ins, rest = refs[:n_in], refs[n_in + len(after) :]
        sources, rest = rest[: len(fetch)], rest[len(fetch) :]
        results, rest = rest[: len(outs)], rest[len(outs) :]
        targets, (*room, sems) = rest[: len(fetch)], rest[len(fetch) :]
        made = copies([f[1:] for f in fetch], sources, targets, sems)
        for copy in made:
            copy.start()
        body(ins, results, room)
        for copy in made:
            copy.wait()

    out = pl.pallas_call(
        kernel,
        out_shape=tuple(outs) + tuple(fetched),
        in_specs=[on_chip()] * n_in + [in_place()] * (len(after) + len(fetch)),
        out_specs=tuple([on_chip()] * (len(outs) + len(fetch))),
        scratch_shapes=list(scratch) + [pltpu.SemaphoreType.DMA((max(len(fetch), 1),))],
        compiler_params=pltpu.CompilerParams(vmem_limit_bytes=4 * 2**20),
        cost_estimate=pl.CostEstimate(flops=int(flops), bytes_accessed=int(traffic), transcendentals=0),
    )(*operands, *after, *[pltpu.with_memory_space_constraint(f[0], pltpu.HBM) for f in fetch])
    order.append(min(out, key=lambda array: array.size))
    return out[: len(outs)], out[len(outs) :]


def load_kernel(ins, outs, room):
    for source, target in zip(ins, outs):
        target[...] = source[...]


def pair_part_kernel(n_pair, chunks, n_weights, ins, outs, room):
    blocks, weights = ins[:-n_weights], ins[-n_weights:]
    n = len(chunks)
    keep, sends = outs[0], outs[1 : 1 + n * (n_pair - 1)]
    x = blocks[0]
    if len(outs) > 1 + len(sends):
        x = outs[-1]
        share = blocks[0].shape[0]
        for k, block in enumerate(blocks):
            x[k * share : (k + 1) * share, :] = block[...]
    (res,) = room
    me = lax.axis_index("pair")
    rows = keep.shape[0]
    start = 0
    for weight in weights:
        for j, (first, width) in enumerate(chunks):
            low, high = max(start, first), min(start + weight.shape[1], first + width)
            if low >= high:
                continue
            tile = tile_of(high - low)

            @pl.loop(0, (high - low) // tile)
            def _(step, weight=weight, tile=tile, j=j, low=low, first=first, start=start):
                def at(offset):
                    return pl.ds(pl.multiple_of(offset + step * tile, tile), tile)

                res[...] = jnp.dot(x[...], weight[:, at(low - start)], preferred_element_type=F32)
                for k in range(n_pair):
                    block = pl.ds(pl.multiple_of(lax.rem(me + k, n_pair) * rows, 16), rows)
                    target, offset = (sends[(k - 1) * n + j], low - first) if k else (keep, low)
                    target[:, at(offset)] = res[block, :].astype(target.dtype)

        start += weight.shape[1]


def pair_sum_kernel(chunks, pieces, ins, outs, room):
    keep, got = ins[0], ins[1:]
    n, half = len(chunks), len(pieces)
    for j, (first, wide) in enumerate(chunks):
        for k, (start, width) in enumerate(pieces):
            low, high = max(first, start), min(first + wide, start + width)
            if low >= high:
                continue
            total = keep[:, low:high]
            for part in got[j::n]:
                total += part[:, low - first : high - first].astype(F32)
            for out in (outs[k], outs[half + k]):
                out[:, low - start : high - start] = total.astype(out.dtype)


def activate_kernel(start, ins, outs, room):
    at = slice(start, start + outs[0].shape[1])
    half = len(ins) // 2
    up = sum(part[:, at].astype(F32) for part in ins[:half])
    gate = sum(part[...].astype(F32) for part in ins[half:])
    hidden = (gate / (1.0 + jnp.exp(-gate)) * up).astype(BF16)
    rows = outs[0].shape[0]
    for k, out in enumerate(outs):
        out[...] = hidden[k * rows : (k + 1) * rows]


def down_kernel(n_pair, n_wide, n_weights, first, last, ins, outs, room):
    before = ins[-1:] if not first else []
    ins = ins[: len(ins) - len(before)]
    parts, weights = ins[:-n_weights], ins[-n_weights:]
    hidden, res = room
    c, w = lax.axis_index("pair"), lax.axis_index("wide")
    rows = parts[0].shape[0]
    pieces = len(parts) // n_pair
    for at, part in enumerate(parts):
        k, piece = divmod(at, pieces)
        block = lax.rem(c + n_pair - k, n_pair) * pieces + piece
        hidden[pl.ds(pl.multiple_of(block * rows, 16), rows), :] = part[...]
    width = weights[0].shape[1]
    tile = tile_of(width)

    @pl.loop(0, width // tile)
    def _(step):
        at = pl.ds(pl.multiple_of(step * tile, tile), tile)
        total, start = 0, 0
        for weight in weights:
            deep = slice(start, start + weight.shape[0])
            total += jnp.dot(hidden[:, deep], weight[:, at], preferred_element_type=F32)
            start += weight.shape[0]
        if before:
            total += before[0][:, at]
        if last:
            share = total.shape[0] // n_wide
            res[...] = total
            for k in range(n_wide):
                other = lax.rem(w + k, n_wide)
                place = jnp.bitwise_xor(w, other) if n_wide & (n_wide - 1) == 0 else (n_wide - k) % n_wide
                rows_of = pl.ds(pl.multiple_of(place * share, 16), share)
                outs[k][:, at] = res[rows_of, :].astype(outs[k].dtype)
        else:
            outs[0][:, at] = total


def shards(sizes, tokens, gate_weight, up_weight, down_weight):
    n_seq, n_wide, n_pair = sizes["seq"], sizes["wide"], sizes["pair"]

    def send(value, axis, k, paired=False):
        n = sizes[axis]
        paired = paired and n & (n - 1) == 0
        return lax.ppermute(value, axis, [(i, i ^ k if paired else (i + k) % n) for i in range(n)])

    share, depth = tokens.shape
    rows = share * n_wide
    features = down_weight.shape[1]
    half = rows // n_pair
    loads = cuts(gate_weight.shape[1], GATE)
    chunks = cuts(down_weight.shape[0], DOWN)
    n = len(chunks)
    size = tokens.dtype.itemsize

    def bytes_of(fetch):
        return sum(size * f[3] * f[0].shape[1 - f[1]] for f in fetch)

    unit = gate_weight.shape[1] // sum(GATE)

    def gate_of(j):
        return [(gate_weight, 1, *loads[j])]

    def down_of(name):
        return [(down_weight, 0, start * unit, count * unit) for start, count in DOWN_LOADS[name]]

    def keep(name, fetched):
        for (start, _), array in zip(DOWN_LOADS[name], fetched):
            down[start * unit] = array

    order = []

    def project(blocks, weights, chunks, fetch, after=()):
        width, n = sum(width for _, width in chunks), len(chunks)
        outs, fetched = call(
            order,
            functools.partial(pair_part_kernel, n_pair, chunks, len(weights)),
            [*blocks, *weights],
            [pltpu.VMEM((half, width), F32)]
            + [pltpu.VMEM((half, wide), PAIR_TYPE) for _, wide in chunks] * (n_pair - 1)
            + [pltpu.VMEM((rows, depth), BF16)] * (len(blocks) > 1),
            fetch,
            [pltpu.VMEM((rows, tile_of(width)), F32)],
            COST * 2 * rows * depth * width,
            COST * 2 * bytes_of(fetch),
            after,
        )
        got = [send(outs[1 + (k - 1) * n + j], "pair", k) for k in range(1, n_pair) for j in range(n)]
        return (outs[0], *got), outs[-1], fetched

    def pair_sum(parts, chunks, pieces, after=()):
        outs = call(
            order, functools.partial(pair_sum_kernel, chunks, pieces), parts,
            [pltpu.VMEM((half, width), kind) for kind in (F32, BF16) for _, width in pieces],
            [], [], 0, COST * 8 * parts[0].size, after,
        )[0]
        sums = []
        for own, away in zip(outs[: len(pieces)], outs[len(pieces) :]):
            sums.append([own] + [send(away, "seq", k) for k in range(1, n_seq)])
        return sums

    def activate(ups, gates, start, width):
        split = SPLIT if start == 0 else 1
        hidden, _ = call(
            order, functools.partial(activate_kernel, start), [*ups, *gates],
            [pltpu.VMEM((half // split, width), BF16)] * split, [], [], 0, COST * 8 * half * width,
        )
        got = [send(piece, "pair", k) for k in range(1, n_pair) for piece in hidden]
        return [*hidden, *got]

    def load(array, fetch, traffic, after=()):
        (array,), fetched = call(
            order, load_kernel, [array], [pltpu.VMEM(array.shape, BF16)], fetch, [], 0, traffic, after
        )
        return array, fetched

    def multiply_down(j, parts, total):
        first, last = j == 0, j == n - 1
        start, width = chunks[j]
        weights = [down[at] for at in sorted(down) if start <= at < start + width]
        if last:
            outs = [pltpu.VMEM((share, features), F32)]
            outs += [pltpu.VMEM((share, features), BF16)] * (n_wide - 1)
        else:
            outs = [pltpu.VMEM((rows, features), F32)]
        name = ("first", "second", "")[min(j, 2)]
        fetch = down_of(name) if n > 1 and name else []
        total, more = call(
            order,
            functools.partial(down_kernel, n_pair, n_wide, len(weights), first, last),
            [*parts, *weights, *total],
            outs,
            fetch,
            [pltpu.VMEM((rows, width), BF16), pltpu.VMEM((rows, tile_of(features)), F32)],
            COST * 2 * rows * width * features,
            COST * 2 * bytes_of(fetch),
        )
        if fetch:
            keep(name, more)
        return total

    _, (staged, *early) = call(
        order, load_kernel, [], [], [(tokens, 0, 0, share), (down_weight, 0, 0, share)], [],
        0, 2 * up_weight.size * size,
    )
    away = {k: send(tokens, "wide", k, True) for k in reversed(range(1, n_wide))}
    blocks = [staged] + [away[k] for k in range(1, n_wide)]
    up = pltpu.with_memory_space_constraint(up_weight, pltpu.VMEM)
    columns = gate_weight.shape[1]
    down, whole = {}, [(0, columns)]
    if n == 1:
        ups, x, gate = project(blocks, [up], whole, gate_of(0), early)
        (ups,) = pair_sum(ups, whole, whole)
        parts, _, (down[0],) = project([x], gate, chunks, [(down_weight, 0, 0, columns)])
        sums = pair_sum(parts, chunks, chunks)
    else:
        ups, x, first = project(blocks, [up], loads, gate_of(0), early)
        x, _ = load(x, [], 0)
        (ups,) = pair_sum(ups, loads, whole)
        edge = loads[1][0]
        inner = [chunk for chunk in chunks if chunk[0] < edge]
        parts, _, (second,) = project([x], first, inner, gate_of(1))
        outer = [(start - edge, width) for start, width in chunks if start >= edge]
        others, _, more = project([x], [second], outer, down_of("rest"))
        keep("rest", more)
        sums = pair_sum(parts, inner, inner) + pair_sum(others, outer, outer)
        _, more = load(x, down_of("late"), 0)
        keep("late", more)
    load(x, [], 0, ups[1:])
    hiddens = [activate(ups, sums[j], *chunks[j]) for j in range(min(n, 2))]
    total = []
    for j in range(n):
        if j and j + 1 < n:
            hiddens.append(activate(ups, sums[j + 1], *chunks[j + 1]))
        total = multiply_down(j, hiddens[j], total)

    result = total[0]
    for k in reversed(range(1, n_wide)):
        result = result + send(total[k], "wide", k).astype(F32)
    return result.astype(BF16)


def solution(mesh):
    return jax.shard_map(
        functools.partial(shards, dict(mesh.shape)),
        mesh=mesh,
        in_specs=(
            P(("parts", "wide"), ("seq", "pair")),
            P(("seq", "pair"), "wide"),
            P(("seq", "pair"), "wide"),
            P("wide", ("seq", "pair")),
        ),
        out_specs=P(("parts", "wide"), ("seq", "pair")),
        check_vma=False,
    )
```
